32 devices in a mesh: gx: 4 (over z), gy: 8 (over y, x, core).
Axes of the slice: x: 2, y: 2, z: 4, core: 2. Of those that a mesh axis runs over, the one named last changes fastest.
Arguments:
- initial_guess: float32 [128, 128, 128], P('gx', 'gy'), may hold values from -6 to 6
- source: float32 [128, 128, 128], P('gx', 'gy'), may hold values from -12 to 12
- leaf_density: float32 [128, 128, 16], P('gx', 'gy'), may hold values from 0 to 4
- absorption: float32 [128, 128, 16], P('gx', 'gy'), may hold values from 0.5 to 2.5
Outputs:
- solution: float32 [128, 128, 128], P('gx', 'gy')
- residual: float32 [128, 128, 128], P('gx', 'gy')
The draws below stay inside these ranges and needn't reach their ends.
All inputs are finite; a program needn't handle non-finite values.
Results may differ from the reference program's by a relative error of at most 0.0003.
Values sent between devices are 32-bit elements; how exact they have to be, the bound alone decides.
No kernel may reach another device: no remote copies, remote signals or barrier semaphores. Data moves between devices by JAX's collectives and lax.ppermute only.
A program may use at most 128 MiB of HBM per device.

```python
import jax
import jax.numpy as jnp
import numpy as np
from jax import lax

NZ = 16
NRHS = 8
S = 8
NX = 128
NY = 128


def shard_levels(own_key, dims, cuts, low, top_value):
    loudness = 1.0
    for axis_at, blocks in cuts:
        heights = jax.random.uniform(jax.random.fold_in(jax.random.fold_in(own_key, 6), axis_at), (blocks,), jnp.float32, low / len(cuts), top_value / len(cuts))
        loudness = loudness * jnp.repeat(jnp.exp(heights), dims[axis_at] // blocks).reshape((-1,) + (1,) * (len(dims) - 1 - axis_at))
    return loudness


def bell_draw(rng, dims, deviation, bound, shards=(), kind=jnp.bfloat16):
    drawn = deviation * jax.random.normal(rng, dims, jnp.float32)
    if shards:
        drawn = drawn * shard_levels(rng, dims, shards, -0.22, 0.18)
    return jnp.clip(drawn, -bound, bound).astype(kind)


def setup_inputs(seed: int = 0) -> dict:
    key_of = jax.random.split(jax.random.key(seed), 5)
    return {
        "initial_guess": bell_draw(key_of[0], (NX, NY, NZ * NRHS), 1.0, 6.0, ((0, 4), (1, 8)), jnp.float32),
        "source": bell_draw(key_of[1], (NX, NY, NZ * NRHS), 2.0, 12.0, ((0, 4), (1, 8)), jnp.float32),
        "leaf_density": jnp.clip(4.0 * jax.random.uniform(key_of[2], (NX, NY, NZ), jnp.float32) ** shard_levels(key_of[2], (NX, NY, NZ), ((0, 4), (1, 8)), -0.2, 0.2), 0.0, 4.0),
        "absorption": jnp.clip(0.5 + 2.0 * jax.random.uniform(key_of[3], (NX, NY, NZ), jnp.float32) ** shard_levels(key_of[3], (NX, NY, NZ), ((0, 4), (1, 8)), -0.2, 0.2), 0.5, 2.5),
    }


PEAK_COND = 0.6
CENTRE = 10.3
HALF_WIDTH = 9.8
RIDGE = 0.05

def offset_list():
    result = []
    for shift_x in (-1, 0, 1):
        for shift_y in (-1, 0, 1):
            for shift_z in (-1, 0, 1):
                distance = shift_x * shift_x + shift_y * shift_y + shift_z * shift_z
                if distance > 0:
                    result.append((shift_x, shift_y, shift_z, 1.0 / distance))
    return result

def coefficients(root_pad, absorb):
    span_x = root_pad.shape[0] - 2
    span_y = root_pad.shape[1] - 2
    depth = root_pad.shape[2]
    padded = jnp.pad(root_pad, ((0, 0), (0, 0), (1, 1)))
    centre_root = root_pad[1:-1, 1:-1]
    total = jnp.zeros((span_x, span_y, depth), root_pad.dtype)
    couplings = []
    for shift_x, shift_y, shift_z, weight in offset_list():
        near = padded[1 + shift_x:1 + shift_x + span_x, 1 + shift_y:1 + shift_y + span_y, 1 + shift_z:1 + shift_z + depth]
        term = weight * near
        total = total + term
        couplings.append(centre_root * term)
    return (absorb + centre_root * total, couplings)

def stencil(field, diagonal, couplings):
    span_x = field.shape[0] - 2
    span_y = field.shape[1] - 2
    span_c = field.shape[2]
    depth = span_c // NRHS
    grid = jnp.pad(field.reshape(span_x + 2, span_y + 2, depth, NRHS), ((0, 0), (0, 0), (1, 1), (0, 0)))
    off_sum = jnp.zeros((span_x, span_y, depth, NRHS), field.dtype)
    for (shift_x, shift_y, shift_z, weight), coupling in zip(offset_list(), couplings):
        near = grid[1 + shift_x:1 + shift_x + span_x, 1 + shift_y:1 + shift_y + span_y, 1 + shift_z:1 + shift_z + depth]
        off_sum = off_sum + coupling[..., None] * near
    centre = grid[1:-1, 1:-1, 1:-1]
    return (diagonal[..., None] * centre - off_sum).reshape(span_x, span_y, span_c)

def krylov_map():
    table = np.zeros((S + 1, S))
    table[0, 0] = CENTRE
    table[1, 0] = HALF_WIDTH
    for column in range(1, S):
        table[column, column] = CENTRE
        table[column - 1, column] = HALF_WIDTH / 2
        table[column + 1, column] = HALF_WIDTH / 2
    return np.kron(table, np.eye(NRHS))

def least_squares(gram):
    highest = lax.Precision.HIGHEST
    lift = jnp.asarray(krylov_map(), dtype=gram.dtype)
    normal = jnp.dot(lift.T, jnp.dot(gram, lift, precision=highest), precision=highest)
    project = jnp.dot(lift.T, gram[:, :NRHS], precision=highest)
    scale = 1.0 / jnp.sqrt(jnp.diagonal(normal))
    balanced = scale[:, None] * normal * scale[None, :] + RIDGE * jnp.eye(S * NRHS, dtype=gram.dtype)
    factor = jnp.linalg.cholesky(balanced)
    coeffs = scale[:, None] * jax.scipy.linalg.cho_solve((factor, True), scale[:, None] * project)
    select = jnp.eye((S + 1) * NRHS, dtype=gram.dtype)[:, :NRHS]
    remain = select - jnp.dot(lift, coeffs, precision=highest)
    return (coeffs, remain)

def reference(initial_guess, source, leaf_density, absorption):
    highest = lax.Precision.HIGHEST
    root = jnp.sqrt(PEAK_COND / (1.0 + leaf_density))
    root_pad = jnp.pad(root, ((1, 1), (1, 1), (0, 0)))
    diagonal, couplings = coefficients(root_pad, absorption)

    def apply_op(field):
        return stencil(jnp.pad(field, ((1, 1), (1, 1), (0, 0))), diagonal, couplings)
    blocks = [source - apply_op(initial_guess)]
    for power in range(S):
        current = blocks[-1]
        scaled = (apply_op(current) - CENTRE * current) / HALF_WIDTH
        if power == 0:
            blocks.append(scaled)
        else:
            blocks.append(2.0 * scaled - blocks[-2])
    cells = NX * NY * NZ
    flat = [block.reshape(cells, NRHS) for block in blocks]
    pieces = {}
    for first in range(S + 1):
        for second in range(first, S + 1):
            pieces[first, second] = jnp.dot(flat[first].T, flat[second], precision=highest)
    rows_list = []
    for first in range(S + 1):
        row = [pieces[first, second] if second >= first else pieces[second, first].T for second in range(S + 1)]
        rows_list.append(jnp.concatenate(row, axis=1))
    gram = jnp.concatenate(rows_list, axis=0)
    coeffs, remain = least_squares(gram)
    update = jnp.zeros((cells, NRHS), gram.dtype)
    rest = jnp.zeros((cells, NRHS), gram.dtype)
    for power in range(S + 1):
        if power < S:
            update = update + jnp.dot(flat[power], coeffs[power * NRHS:(power + 1) * NRHS], precision=highest)
        rest = rest + jnp.dot(flat[power], remain[power * NRHS:(power + 1) * NRHS], precision=highest)
    shape = initial_guess.shape
    return (initial_guess + update.reshape(shape), rest.reshape(shape))
```

```python
import functools

import jax
import jax.numpy as jnp
import numpy as np
from jax import lax
from jax.experimental import pallas as pl
from jax.experimental.pallas import tpu as pltpu
from jax.sharding import PartitionSpec as P

NRHS = 8
S = 8
DEEP = S
LANES = 128

PEAK_COND = 0.6
CENTRE = 10.3
HALF_WIDTH = 9.8
RIDGE = 0.05
HIGHEST = lax.Precision.HIGHEST
VMEM_BYTES = 48 * 1024 * 1024


def lanes_of(shape):
    return lax.broadcasted_iota(jnp.int32, shape, len(shape) - 1)


def rows_at(shape):
    return lax.broadcasted_iota(jnp.int32, shape, len(shape) - 2)


def z_sum(f):
    lane = lanes_of(f.shape)
    ax = f.ndim - 1
    up = jnp.where(lane >= NRHS, pltpu.roll(f, NRHS, ax), 0.0)
    down = jnp.where(lane < LANES - NRHS, pltpu.roll(f, LANES - NRHS, ax), 0.0)
    return up + down


def row_sum(f):
    n = f.shape[-2]
    ax = f.ndim - 2
    return pltpu.roll(f, 1, ax) + pltpu.roll(f, n - 1, ax)


def row_sum_zero(f):
    n = f.shape[-2]
    ax = f.ndim - 2
    row = rows_at(f.shape)
    up = jnp.where(row >= 1, pltpu.roll(f, 1, ax), 0.0)
    down = jnp.where(row < n - 1, pltpu.roll(f, n - 1, ax), 0.0)
    return up + down


def slab_sum(before, here, after, rows):
    ux = before[0] + after[0]
    px = before[1] + after[1]
    s = here[1] + ux
    q = here[0] + 0.5 * s + (1.0 / 3.0) * px
    return s + 0.5 * px + rows(q)


def cross_sum(f, rows):
    p = z_sum(f)
    return f + 0.5 * p + rows(0.5 * f + (1.0 / 3.0) * p)


def select(shape, rule):
    row = lax.broadcasted_iota(jnp.int32, shape, 0)
    col = lax.broadcasted_iota(jnp.int32, shape, 1)
    return jnp.where(rule(row, col), 1.0, 0.0).astype(jnp.float32)


def exact(a, b):
    return jnp.dot(a, b, precision=HIGHEST, preferred_element_type=jnp.float32)


def unpack_matrix(quarter, part, depth):
    base = quarter * 2 * depth + part * depth
    return select((LANES, LANES), lambda r, c: r == base + c // NRHS)


def pack_matrix(quarter, part, depth):
    base = quarter * 2 * depth + part * depth
    return select((LANES, LANES), lambda r, c: (r % NRHS == 0) & (c == base + r // NRHS))


def begin_kernel(px, guess, source, ra, root_o, abs_o, b0_o, send_a, send_b):
    nx, ny, _ = guess.shape
    depth = ra.shape[2] // 2
    flat = ra[...].reshape(nx * ny, 2 * depth)
    for part, out in ((0, root_o), (1, abs_o)):
        spread = select((2 * depth, LANES), lambda r, c: r == part * depth + c // NRHS)
        out[...] = exact(flat, spread).reshape(nx, ny, LANES)
    zero = jnp.zeros((ny, LANES), jnp.float32)

    def pair(x, field):
        if x < 0 or x >= nx:
            return (zero, zero)
        u = root_o[x] if field is None else root_o[x] * field[x]
        return (u, z_sum(u))

    moving = [pair(-1, guess), pair(0, guess)]
    still = [pair(-1, None), pair(0, None)]
    for x in range(nx):
        moving.append(pair(x + 1, guess))
        still.append(pair(x + 1, None))
        wu = slab_sum(*moving, row_sum_zero)
        wr = slab_sum(*still, row_sum_zero)
        moving, still = moving[1:], still[1:]
        v = guess[x]
        b0_o[x] = source[x] - abs_o[x] * v + root_o[x] * (wu - v * wr)

    def write(out, x0, face, beyond):
        n = DEEP * ny
        out[0:n] = b0_o[x0 : x0 + DEEP].reshape(n, LANES)
        out[n : n + ny] = guess[face]
        n += ny
        for col in (0, ny - 1):
            out[n : n + DEEP] = guess[x0 : x0 + DEEP, col, :]
            n += DEEP
        out[n : n + 8] = jnp.zeros((8, LANES), jnp.float32)
        for at, col in ((0, 0), (1, ny - 1)):
            out[n + at : n + at + 1] = guess[beyond, col : col + 1, :]
            out[n + 2 + at : n + 3 + at] = root_o[beyond, col : col + 1, :]
        n += 8
        group = DEEP // 4
        packed = jnp.zeros((group * ny, LANES), jnp.float32)
        for q in range(4):
            place = select((2 * depth, LANES), lambda r, c: c == q * 2 * depth + r)
            part = ra[x0 + q * group : x0 + (q + 1) * group].reshape(group * ny, 2 * depth)
            packed = packed + exact(part, place)
        out[n : n + group * ny] = packed

    @pl.when(px[0] == 0)
    def _():
        write(send_a, nx - DEEP, nx - 1, nx - DEEP - 1)
        write(send_b, 0, 0, DEEP)

    @pl.when(px[0] == 1)
    def _():
        write(send_b, nx - DEEP, nx - 1, nx - DEEP - 1)
        write(send_a, 0, 0, DEEP)


def widen_kernel(
    px, py, recv_a, recv_b, guess, root, absb, b0, rootx, absx, b0x, edge, send_a, send_b, face
):
    nx, ny, _ = guess.shape
    wide = nx + 2 * DEEP
    depth = LANES // NRHS
    rootx[DEEP : DEEP + nx] = root[...]
    absx[DEEP : DEEP + nx] = absb[...]
    b0x[DEEP : DEEP + nx] = b0[...]
    for at, col in ((0, 0), (1, ny - 1)):
        edge[at, DEEP : DEEP + nx] = guess[:, col, :]
        edge[at, wide : wide + 8] = jnp.zeros((8, LANES), jnp.float32)

    def read(msg, x0, side):
        n = DEEP * ny
        b0x[x0 : x0 + DEEP] = msg[0:n].reshape(DEEP, ny, LANES)
        face[side] = msg[n : n + ny]
        n += ny
        for at in (0, 1):
            edge[at, x0 : x0 + DEEP] = msg[n : n + DEEP]
            n += DEEP
        for at in (0, 1):
            edge[at, wide + side : wide + side + 1] = msg[n + at : n + at + 1]
            edge[at, wide + 2 + side : wide + 3 + side] = msg[n + 2 + at : n + 3 + at]
        n += 8
        group = DEEP // 4
        packed = msg[n : n + group * ny]
        for q in range(4):
            for part, out in ((0, rootx), (1, absx)):
                got = exact(packed, unpack_matrix(q, part, depth))
                out[x0 + q * group : x0 + (q + 1) * group] = got.reshape(group, ny, LANES)

    @pl.when(px[0] == 0)
    def _():
        read(recv_b, 0, 0)
        read(recv_a, DEEP + nx, 1)

    @pl.when(px[0] == 1)
    def _():
        read(recv_a, 0, 0)
        read(recv_b, DEEP + nx, 1)

    for side, out_x, in_x, own in ((0, DEEP - 1, DEEP, 0), (1, DEEP + nx, DEEP + nx - 1, nx - 1)):
        va, ra = face[side], rootx[out_x]
        vb, rb = guess[own], rootx[in_x]
        fix_a = ra * (cross_sum(rb * vb, row_sum_zero) - va * cross_sum(rb, row_sum_zero))
        fix_b = rb * (cross_sum(ra * va, row_sum_zero) - vb * cross_sum(ra, row_sum_zero))
        b0x[out_x] = b0x[out_x] + fix_a
        b0x[in_x] = b0x[in_x] + fix_b

    def write(out, y0, at):
        n = wide * DEEP
        out[0:n] = b0x[:, y0 : y0 + DEEP, :].reshape(n, LANES)
        out[n : n + wide + 8] = edge[at]
        n += wide + 8
        group = wide // 4
        packed = jnp.zeros((group * DEEP, LANES), jnp.float32)
        for q in range(4):
            for part, field in ((0, rootx), (1, absx)):
                some = field[q * group : (q + 1) * group, y0 : y0 + DEEP, :]
                packed = packed + exact(
                    some.reshape(group * DEEP, LANES), pack_matrix(q, part, depth)
                )
        out[n : n + group * DEEP] = packed

    @pl.when(py[0] == 0)
    def _():
        write(send_a, ny - DEEP, 1)
        write(send_b, 0, 0)

    @pl.when(py[0] == 1)
    def _():
        write(send_b, ny - DEEP, 1)
        write(send_a, 0, 0)


def halves(a):
    high = a.astype(jnp.bfloat16)
    return high, (a - high.astype(jnp.float32)).astype(jnp.bfloat16)


def dot_t(a, b):
    return lax.dot_general(a, b, (((0,), (0,)), ((), ())), preferred_element_type=jnp.float32)


def basis_kernel(
    py, recv_a, recv_b, rootx, absx, b0x, edge, basis, moments, root, diag, far, f0, f1, f2
):
    wide, ny, _ = b0x.shape
    nx = wide - 2 * DEEP
    tall = ny + 2 * DEEP
    depth = LANES // NRHS
    root[:, DEEP : DEEP + ny, :] = rootx[...]
    diag[:, DEEP : DEEP + ny, :] = absx[...]
    f0[:, DEEP : DEEP + ny, :] = b0x[...]

    def read(msg, y0, side):
        n = wide * DEEP
        f0[:, y0 : y0 + DEEP, :] = msg[0:n].reshape(wide, DEEP, LANES)
        far[side] = msg[n : n + wide + 8]
        n += wide + 8
        group = wide // 4
        packed = msg[n : n + group * DEEP]
        for q in range(4):
            for part, out in ((0, root), (1, diag)):
                got = exact(packed, unpack_matrix(q, part, depth))
                out[q * group : (q + 1) * group, y0 : y0 + DEEP, :] = got.reshape(
                    group, DEEP, LANES
                )

    @pl.when(py[0] == 0)
    def _():
        read(recv_b, 0, 0)
        read(recv_a, DEEP + ny, 1)

    @pl.when(py[0] == 1)
    def _():
        read(recv_a, 0, 0)
        read(recv_b, DEEP + ny, 1)

    row = lax.broadcasted_iota(jnp.int32, (wide, LANES), 0)

    def across(f, before, after):
        p = z_sum(f)
        ends = jnp.concatenate([before, after], axis=0)
        ends = 0.5 * ends + (1.0 / 3.0) * z_sum(ends)
        g = 0.5 * f + (1.0 / 3.0) * p
        up = jnp.where(row == 0, ends[0:1], pltpu.roll(g, 1, 0))
        down = jnp.where(row == wide - 1, ends[1:2], pltpu.roll(g, wide - 1, 0))
        return f + 0.5 * p + up + down

    def column(ref, at, y):
        v = ref[at, 0:wide]
        ends = ref[at, wide : wide + 8]
        r = root[:, y, :]
        r0, r1 = ends[2:3], ends[3:4]
        return v, r, across(r * v, r0 * ends[0:1], r1 * ends[1:2]), across(r, r0, r1)

    for side, out_y, in_y in ((0, DEEP - 1, DEEP), (1, DEEP + ny, DEEP + ny - 1)):
        va, ra, ua, wa = column(far, side, out_y)
        vb, rb, ub, wb = column(edge, side, in_y)
        f0[:, out_y, :] = f0[:, out_y, :] + ra * (ub - va * wb)
        f0[:, in_y, :] = f0[:, in_y, :] + rb * (ua - vb * wa)

    def pair(src, x):
        u = root[x] if src is None else root[x] * src[x]
        return (u, z_sum(u))

    def sweep(src, lo, hi, put):
        def two(i, carry):
            x = lo + 2 * i
            first, second = carry
            third = pair(src, x + 1)
            put(x, slab_sum(first, second, third, row_sum))
            fourth = pair(src, x + 2)
            put(x + 1, slab_sum(second, third, fourth, row_sum))
            return (third, fourth)

        lax.fori_loop(0, (hi - lo) // 2, two, (pair(src, lo - 1), pair(src, lo)))

    def put_diag(x, total):
        diag[x] = (diag[x] + root[x] * total - CENTRE) * (2.0 / HALF_WIDTH)

    sweep(None, 1, wide - 1, put_diag)

    lane = lanes_of((NRHS, LANES))
    same = select((LANES, LANES), lambda r, c: r // NRHS == c // NRHS)

    def fold(block):
        f = jnp.sum((block * same).reshape(LANES // NRHS, NRHS, LANES), axis=0)
        shift = LANES // 2
        while shift >= NRHS:
            f = f + pltpu.roll(f, shift, 1)
            shift //= 2
        return f

    tile = [jnp.zeros((NRHS, LANES), jnp.float32) for _ in range(2)]

    def note(tile, n, block):
        f = fold(block)
        which, place = divmod(n, LANES // NRHS)
        tile[which] = tile[which] + jnp.where(lane // NRHS == place, f, 0.0)

    frames = [f0, f1, f2]
    old = None
    for j in range(S + 1):
        now = frames[j % 3]
        if j > 0:
            src, prev = frames[(j - 1) % 3], frames[(j - 2) % 3]

            def put(x, total):
                new = diag[x] * src[x] - (2.0 / HALF_WIDTH) * root[x] * total
                now[x] = 0.5 * new if j == 1 else new - prev[x]

            sweep(src, j, wide - j, put)
        own = now[DEEP : DEEP + nx, DEEP : DEEP + ny, :]
        basis[:, :, j * LANES : (j + 1) * LANES] = own
        high, low = halves(own.reshape(nx * ny, LANES))
        note(tile, 2 * j, dot_t(high, high) + dot_t(high, low) + dot_t(low, high))
        if j > 0:
            note(tile, 2 * j - 1, dot_t(high, old[0]) + dot_t(high, old[1]) + dot_t(low, old[0]))
        old = (high, low)
    moments[0:NRHS] = tile[0]
    moments[NRHS : 2 * NRHS] = tile[1]


def combine_kernel(guess, basis, weights, update, rest, wh, wl):
    nx, ny, _ = guess.shape
    spread = select((NRHS, LANES), lambda r, c: r == c % NRHS)
    same = select((LANES, LANES), lambda r, c: r // NRHS == c // NRHS)
    for part in range(2):
        rows = exact(weights[part], spread)
        for j in range(S + 1):
            tile = rows[j * NRHS : (j + 1) * NRHS]
            full = jnp.concatenate([tile] * (LANES // NRHS), axis=0) * same
            high, low = halves(full)
            wh[j * LANES : (j + 1) * LANES, part * LANES : (part + 1) * LANES] = high
            wl[j * LANES : (j + 1) * LANES, part * LANES : (part + 1) * LANES] = low
    chunk = nx // 4
    for i in range(4):
        at = slice(i * chunk, (i + 1) * chunk)
        high, low = halves(basis[at].reshape(chunk * ny, (S + 1) * LANES))
        dot = functools.partial(jnp.dot, preferred_element_type=jnp.float32)
        out = dot(high, wh[...]) + dot(high, wl[...]) + dot(low, wh[...])
        out = out.reshape(chunk, ny, 2 * LANES)
        update[at] = guess[at] + out[:, :, :LANES]
        rest[at] = out[:, :, LANES:]


def call(kernel, ins, outs, scratch=(), scalars=0):
    specs = [pl.BlockSpec(memory_space=pltpu.SMEM)] * scalars
    specs += [pl.BlockSpec(memory_space=pltpu.VMEM)] * (len(ins) - scalars)
    result = pl.pallas_call(
        kernel,
        out_shape=[jax.ShapeDtypeStruct(s, jnp.float32) for s in outs],
        in_specs=specs,
        out_specs=[pl.BlockSpec(memory_space=pltpu.VMEM)] * len(outs),
        scratch_shapes=list(scratch),
        compiler_params=pltpu.CompilerParams(vmem_limit_bytes=VMEM_BYTES),
    )(*ins)
    return result


def exchange(first, second, axis):
    count = lax.axis_size(axis)
    got = []
    for cells, start in ((first, 0), (second, 1)):
        links = []
        for i in range(start, count - 1, 2):
            links += [(i, i + 1), (i + 1, i)]
        got.append(lax.ppermute(cells, axis, links))
    return got


def total_of(x, axis):
    count = lax.axis_size(axis)
    if count & (count - 1):
        return lax.psum(x, axis)
    step = 1
    while step < count:
        x = x + lax.ppermute(x, axis, [(i, i ^ step) for i in range(count)])
        step *= 2
    return x


def krylov_map():
    table = np.zeros((S + 1, S))
    table[0, 0] = CENTRE
    table[1, 0] = HALF_WIDTH
    for column in range(1, S):
        table[column, column] = CENTRE
        table[column - 1, column] = HALF_WIDTH / 2
        table[column + 1, column] = HALF_WIDTH / 2
    return np.kron(table, np.eye(NRHS))


def gram_of(moments):
    raw = [
        moments[(n // 16) * 8 : (n // 16) * 8 + 8, (n % 16) * 8 : (n % 16) * 8 + 8]
        for n in range(2 * S + 1)
    ]
    m = [raw[0], raw[1]] + [2.0 * raw[n] - raw[n % 2] for n in range(2, 2 * S + 1)]
    return jnp.concatenate(
        [
            jnp.concatenate([0.5 * (m[i + j] + m[abs(i - j)]) for j in range(S + 1)], axis=1)
            for i in range(S + 1)
        ],
        axis=0,
    )


def least_squares(gram):
    lift = jnp.asarray(krylov_map(), dtype=gram.dtype)
    normal = jnp.dot(lift.T, jnp.dot(gram, lift, precision=HIGHEST), precision=HIGHEST)
    project = jnp.dot(lift.T, gram[:, :NRHS], precision=HIGHEST)
    scale = 1.0 / jnp.sqrt(jnp.diagonal(normal))
    balanced = scale[:, None] * normal * scale[None, :] + RIDGE * jnp.eye(
        S * NRHS, dtype=gram.dtype
    )
    factor = jnp.linalg.cholesky(balanced)
    coeffs = scale[:, None] * jax.scipy.linalg.cho_solve((factor, True), scale[:, None] * project)
    select_first = jnp.eye((S + 1) * NRHS, dtype=gram.dtype)[:, :NRHS]
    remain = select_first - jnp.dot(lift, coeffs, precision=HIGHEST)
    return (coeffs, remain)


def body(initial_guess, source, leaf_density, absorption):
    nx, ny, lanes = initial_guess.shape
    root = jnp.sqrt(PEAK_COND / (1.0 + leaf_density))
    ra = jnp.concatenate([root, absorption], axis=-1)
    px = lax.rem(lax.axis_index("gx"), 2).astype(jnp.int32).reshape(1)
    py = lax.rem(lax.axis_index("gy"), 2).astype(jnp.int32).reshape(1)
    wide = nx + 2 * DEEP
    tall = ny + 2 * DEEP
    block = (nx, ny, lanes)
    x_rows = DEEP * ny + ny + 2 * DEEP + 8 + DEEP // 4 * ny
    y_rows = wide * DEEP + wide + 8 + wide // 4 * DEEP
    root, absb, b0, xa, xb = call(
        begin_kernel,
        (px, initial_guess, source, ra),
        (block, block, block, (x_rows, lanes), (x_rows, lanes)),
        scalars=1,
    )
    xa, xb = exchange(xa, xb, "gx")
    broad = (wide, ny, lanes)
    rootx, absx, b0x, edge, ya, yb = call(
        widen_kernel,
        (px, py, xa, xb, initial_guess, root, absb, b0),
        (broad, broad, broad, (2, wide + 8, lanes), (y_rows, lanes), (y_rows, lanes)),
        scratch=[pltpu.VMEM((2, ny, lanes), jnp.float32)],
        scalars=2,
    )
    ya, yb = exchange(ya, yb, "gy")
    frame = pltpu.VMEM((wide, tall, lanes), jnp.float32)
    basis, moments = call(
        basis_kernel,
        (py, ya, yb, rootx, absx, b0x, edge),
        ((nx, ny, (S + 1) * lanes), (2 * NRHS, lanes)),
        scratch=[frame, frame, pltpu.VMEM((2, wide + 8, lanes), jnp.float32), frame, frame, frame],
        scalars=1,
    )
    moments = total_of(total_of(moments, "gy"), "gx")
    coeffs, remain = least_squares(gram_of(moments))
    weights = jnp.stack([jnp.pad(coeffs, ((0, NRHS), (0, 0))), remain])
    return call(
        combine_kernel,
        (initial_guess, basis, weights),
        (block, block),
        scratch=[pltpu.VMEM(((S + 1) * lanes, 2 * lanes), jnp.bfloat16)] * 2,
    )


def solution(mesh):
    spec = P("gx", "gy", None)
    return jax.shard_map(
        lambda *arrays: tuple(body(*arrays)),
        mesh=mesh,
        in_specs=(spec,) * 4,
        out_specs=(spec, spec),
        check_vma=False,
    )
```

```python
import functools

import jax
import jax.numpy as jnp
from jax import lax
from jax.experimental import pallas as pl
from jax.experimental.pallas import tpu as pltpu
from jax.sharding import PartitionSpec as P

NRHS = 8
S = 8
DEEP = S
LANES = 128

PEAK_COND = 0.6
CENTRE = 10.3
HALF_WIDTH = 9.8
RIDGE = 0.05
HIGHEST = lax.Precision.HIGHEST
VMEM_BYTES = 48 * 1024 * 1024


def lanes_of(shape):
    return lax.broadcasted_iota(jnp.int32, shape, len(shape) - 1)


def rows_at(shape):
    return lax.broadcasted_iota(jnp.int32, shape, len(shape) - 2)


def z_sum(f):
    lane = lanes_of(f.shape)
    ax = f.ndim - 1
    up = jnp.where(lane >= NRHS, pltpu.roll(f, NRHS, ax), 0.0)
    down = jnp.where(lane < LANES - NRHS, pltpu.roll(f, LANES - NRHS, ax), 0.0)
    return up + down


def row_sum(f):
    n = f.shape[-2]
    ax = f.ndim - 2
    return pltpu.roll(f, 1, ax) + pltpu.roll(f, n - 1, ax)


def row_sum_zero(f):
    n = f.shape[-2]
    ax = f.ndim - 2
    row = rows_at(f.shape)
    up = jnp.where(row >= 1, pltpu.roll(f, 1, ax), 0.0)
    down = jnp.where(row < n - 1, pltpu.roll(f, n - 1, ax), 0.0)
    return up + down


def slab_sum(before, here, after, rows):
    ux = before[0] + after[0]
    px = before[1] + after[1]
    s = here[1] + ux
    q = here[0] + 0.5 * s + (1.0 / 3.0) * px
    return s + 0.5 * px + rows(q)


def cross_sum(f, rows):
    p = z_sum(f)
    return f + 0.5 * p + rows(0.5 * f + (1.0 / 3.0) * p)


def select(shape, rule):
    row = lax.broadcasted_iota(jnp.int32, shape, 0)
    col = lax.broadcasted_iota(jnp.int32, shape, 1)
    return jnp.where(rule(row, col), 1.0, 0.0).astype(jnp.float32)


def exact(a, b):
    return jnp.dot(a, b, precision=HIGHEST, preferred_element_type=jnp.float32)


def unpack_matrix(quarter, part, depth):
    base = quarter * 2 * depth + part * depth
    return select((LANES, LANES), lambda r, c: r == base + c // NRHS)


def pack_matrix(quarter, part, depth):
    base = quarter * 2 * depth + part * depth
    return select((LANES, LANES), lambda r, c: (r % NRHS == 0) & (c == base + r // NRHS))


def begin_kernel(px, guess, source, ra, root_o, abs_o, b0_o, send_a, send_b):
    nx, ny, _ = guess.shape
    depth = ra.shape[2] // 2
    flat = ra[...].reshape(nx * ny, 2 * depth)
    for part, out in ((0, root_o), (1, abs_o)):
        spread = select((2 * depth, LANES), lambda r, c: r == part * depth + c // NRHS)
        out[...] = exact(flat, spread).reshape(nx, ny, LANES)
    zero = jnp.zeros((ny, LANES), jnp.float32)

    def pair(x, field):
        if x < 0 or x >= nx:
            return (zero, zero)
        u = root_o[x] if field is None else root_o[x] * field[x]
        return (u, z_sum(u))

    moving = [pair(-1, guess), pair(0, guess)]
    still = [pair(-1, None), pair(0, None)]
    for x in range(nx):
        moving.append(pair(x + 1, guess))
        still.append(pair(x + 1, None))
        wu = slab_sum(*moving, row_sum_zero)
        wr = slab_sum(*still, row_sum_zero)
        moving, still = moving[1:], still[1:]
        v = guess[x]
        b0_o[x] = source[x] - abs_o[x] * v + root_o[x] * (wu - v * wr)

    def write(out, x0, face, beyond):
        n = DEEP * ny
        out[0:n] = b0_o[x0 : x0 + DEEP].reshape(n, LANES)
        out[n : n + ny] = guess[face]
        n += ny
        for col in (0, ny - 1):
            out[n : n + DEEP] = guess[x0 : x0 + DEEP, col, :]
            n += DEEP
        out[n : n + 8] = jnp.zeros((8, LANES), jnp.float32)
        for at, col in ((0, 0), (1, ny - 1)):
            out[n + at : n + at + 1] = guess[beyond, col : col + 1, :]
            out[n + 2 + at : n + 3 + at] = root_o[beyond, col : col + 1, :]
        n += 8
        group = DEEP // 4
        packed = jnp.zeros((group * ny, LANES), jnp.float32)
        for q in range(4):
            place = select((2 * depth, LANES), lambda r, c: c == q * 2 * depth + r)
            part = ra[x0 + q * group : x0 + (q + 1) * group].reshape(group * ny, 2 * depth)
            packed = packed + exact(part, place)
        out[n : n + group * ny] = packed

    @pl.when(px[0] == 0)
    def _():
        write(send_a, nx - DEEP, nx - 1, nx - DEEP - 1)
        write(send_b, 0, 0, DEEP)

    @pl.when(px[0] == 1)
    def _():
        write(send_b, nx - DEEP, nx - 1, nx - DEEP - 1)
        write(send_a, 0, 0, DEEP)


def widen_kernel(
    px, py, recv_a, recv_b, guess, root, absb, b0, rootx, absx, b0x, edge, send_a, send_b, face
):
    nx, ny, _ = guess.shape
    wide = nx + 2 * DEEP
    depth = LANES // NRHS
    rootx[DEEP : DEEP + nx] = root[...]
    absx[DEEP : DEEP + nx] = absb[...]
    b0x[DEEP : DEEP + nx] = b0[...]
    for at, col in ((0, 0), (1, ny - 1)):
        edge[at, DEEP : DEEP + nx] = guess[:, col, :]
        edge[at, wide : wide + 8] = jnp.zeros((8, LANES), jnp.float32)

    def read(msg, x0, side):
        n = DEEP * ny
        b0x[x0 : x0 + DEEP] = msg[0:n].reshape(DEEP, ny, LANES)
        face[side] = msg[n : n + ny]
        n += ny
        for at in (0, 1):
            edge[at, x0 : x0 + DEEP] = msg[n : n + DEEP]
            n += DEEP
        for at in (0, 1):
            edge[at, wide + side : wide + side + 1] = msg[n + at : n + at + 1]
            edge[at, wide + 2 + side : wide + 3 + side] = msg[n + 2 + at : n + 3 + at]
        n += 8
        group = DEEP // 4
        packed = msg[n : n + group * ny]
        for q in range(4):
            for part, out in ((0, rootx), (1, absx)):
                got = exact(packed, unpack_matrix(q, part, depth))
                out[x0 + q * group : x0 + (q + 1) * group] = got.reshape(group, ny, LANES)

    @pl.when(px[0] == 0)
    def _():
        read(recv_b, 0, 0)
        read(recv_a, DEEP + nx, 1)

    @pl.when(px[0] == 1)
    def _():
        read(recv_a, 0, 0)
        read(recv_b, DEEP + nx, 1)

    for side, out_x, in_x, own in ((0, DEEP - 1, DEEP, 0), (1, DEEP + nx, DEEP + nx - 1, nx - 1)):
        va, ra = face[side], rootx[out_x]
        vb, rb = guess[own], rootx[in_x]
        fix_a = ra * (cross_sum(rb * vb, row_sum_zero) - va * cross_sum(rb, row_sum_zero))
        fix_b = rb * (cross_sum(ra * va, row_sum_zero) - vb * cross_sum(ra, row_sum_zero))
        b0x[out_x] = b0x[out_x] + fix_a
        b0x[in_x] = b0x[in_x] + fix_b

    def write(out, y0, at):
        n = wide * DEEP
        out[0:n] = b0x[:, y0 : y0 + DEEP, :].reshape(n, LANES)
        out[n : n + wide + 8] = edge[at]
        n += wide + 8
        group = wide // 4
        packed = jnp.zeros((group * DEEP, LANES), jnp.float32)
        for q in range(4):
            for part, field in ((0, rootx), (1, absx)):
                some = field[q * group : (q + 1) * group, y0 : y0 + DEEP, :]
                packed = packed + exact(
                    some.reshape(group * DEEP, LANES), pack_matrix(q, part, depth)
                )
        out[n : n + group * DEEP] = packed

    @pl.when(py[0] == 0)
    def _():
        write(send_a, ny - DEEP, 1)
        write(send_b, 0, 0)

    @pl.when(py[0] == 1)
    def _():
        write(send_b, ny - DEEP, 1)
        write(send_a, 0, 0)


def halves(a):
    high = a.astype(jnp.bfloat16)
    return high, (a - high.astype(jnp.float32)).astype(jnp.bfloat16)


def basis_kernel(
    py, recv_a, recv_b, rootx, absx, b0x, edge, rough, fine, moments, root, diag, far, f0, f1, f2
):
    wide, ny, _ = b0x.shape
    nx = wide - 2 * DEEP
    tall = ny + 2 * DEEP
    depth = LANES // NRHS
    root[:, DEEP : DEEP + ny, :] = rootx[...]
    diag[:, DEEP : DEEP + ny, :] = absx[...]
    f0[:, DEEP : DEEP + ny, :] = b0x[...]

    def read(msg, y0, side):
        n = wide * DEEP
        f0[:, y0 : y0 + DEEP, :] = msg[0:n].reshape(wide, DEEP, LANES)
        far[side] = msg[n : n + wide + 8]
        n += wide + 8
        group = wide // 4
        packed = msg[n : n + group * DEEP]
        for q in range(4):
            for part, out in ((0, root), (1, diag)):
                got = exact(packed, unpack_matrix(q, part, depth))
                out[q * group : (q + 1) * group, y0 : y0 + DEEP, :] = got.reshape(
                    group, DEEP, LANES
                )

    @pl.when(py[0] == 0)
    def _():
        read(recv_b, 0, 0)
        read(recv_a, DEEP + ny, 1)

    @pl.when(py[0] == 1)
    def _():
        read(recv_a, 0, 0)
        read(recv_b, DEEP + ny, 1)

    row = lax.broadcasted_iota(jnp.int32, (wide, LANES), 0)

    def across(f, before, after):
        p = z_sum(f)
        ends = jnp.concatenate([before, after], axis=0)
        ends = 0.5 * ends + (1.0 / 3.0) * z_sum(ends)
        g = 0.5 * f + (1.0 / 3.0) * p
        up = jnp.where(row == 0, ends[0:1], pltpu.roll(g, 1, 0))
        down = jnp.where(row == wide - 1, ends[1:2], pltpu.roll(g, wide - 1, 0))
        return f + 0.5 * p + up + down

    def column(ref, at, y):
        v = ref[at, 0:wide]
        ends = ref[at, wide : wide + 8]
        r = root[:, y, :]
        r0, r1 = ends[2:3], ends[3:4]
        return v, r, across(r * v, r0 * ends[0:1], r1 * ends[1:2]), across(r, r0, r1)

    for side, out_y, in_y in ((0, DEEP - 1, DEEP), (1, DEEP + ny, DEEP + ny - 1)):
        va, ra, ua, wa = column(far, side, out_y)
        vb, rb, ub, wb = column(edge, side, in_y)
        f0[:, out_y, :] = f0[:, out_y, :] + ra * (ub - va * wb)
        f0[:, in_y, :] = f0[:, in_y, :] + rb * (ua - vb * wa)

    def pair(src, x):
        u = root[x] if src is None else root[x] * src[x]
        return (u, z_sum(u))

    def sweep(src, lo, hi, put):
        first, second = pair(src, lo - 1), pair(src, lo)
        for x in range(lo, hi):
            third = pair(src, x + 1)
            put(x, slab_sum(first, second, third, row_sum))
            first, second = second, third

    def put_diag(x, total):
        diag[x] = (diag[x] + root[x] * total - CENTRE) * (2.0 / HALF_WIDTH)

    sweep(None, 1, wide - 1, put_diag)

    level = lanes_of((NRHS, LANES)) // NRHS
    depth = LANES // NRHS
    folded = [None] * (2 * S + 1)

    def note(n, block):
        if n in (0, 1, 2 * S):
            block = 0.5 * (block + block.T)
        f = block[0:NRHS]
        for z in range(1, depth):
            f = jnp.where(level == z, block[z * NRHS : (z + 1) * NRHS], f)
        folded[n] = f

    frames = [f0, f1, f2]
    old = None
    for j in range(S + 1):
        now = frames[j % 3]
        if j > 0:
            src, prev = frames[(j - 1) % 3], frames[(j - 2) % 3]

            def put(x, total):
                new = diag[x] * src[x] - (2.0 / HALF_WIDTH) * root[x] * total
                now[x] = 0.5 * new if j == 1 else new - prev[x]

            sweep(src, j, wide - j, put)
        own = now[DEEP : DEEP + nx, DEEP : DEEP + ny, :]
        high, low = halves(own.reshape(nx * ny, LANES))
        rough[:, j * LANES : (j + 1) * LANES] = high
        fine[:, j * LANES : (j + 1) * LANES] = low
        turned = high.T
        both = jnp.concatenate([high, low], axis=1)
        left = turned if j == 0 else jnp.concatenate([turned, old[0]], axis=0)
        got = jnp.dot(left, both, preferred_element_type=jnp.float32)
        note(2 * j, got[:LANES, :LANES] + 2.0 * got[:LANES, LANES:])
        if j > 0:
            rest = jnp.dot(turned, old[1], preferred_element_type=jnp.float32)
            note(2 * j - 1, got[LANES:, :LANES] + got[LANES:, LANES:] + rest)
        old = (turned, low)
    every = jnp.concatenate(folded, axis=0)
    shift = LANES // 2
    while shift >= NRHS:
        every = every + pltpu.roll(every, shift, 1)
        shift //= 2
    blocks = [every[n * NRHS : (n + 1) * NRHS] for n in range(2 * S + 1)]
    tile = jnp.zeros((NRHS, LANES), jnp.float32)
    row, col = rows_at((NRHS, LANES)), lanes_of((NRHS, LANES)) % NRHS
    last = blocks[2 * S]
    below = jnp.where(row == col + 1, pltpu.roll(last, 1, 0), 0.0)
    below = jnp.where((row == NRHS - 1) & (col == 0), pltpu.roll(last, 1, 1), below)
    blocks[0] = jnp.where(row <= col, blocks[0], last)
    blocks[1] = jnp.where(row <= col, blocks[1], below)
    for n in range(2 * S):
        tile = jnp.where(level == n, blocks[n], tile)
    moments[...] = jnp.broadcast_to(tile[None], moments.shape)


def moment_blocks(tile):
    depth = LANES // NRHS
    row, lane = rows_at((NRHS, LANES)), lanes_of((NRHS, LANES))
    raw = [tile] + [pltpu.roll(tile, LANES - NRHS * n, 1) for n in range(1, depth)]
    square = jnp.concatenate([tile, jnp.zeros((LANES - NRHS, LANES), jnp.float32)], axis=0).T
    turned = [square[n * NRHS : (n + 1) * NRHS] for n in range(depth)]
    first, second = raw[0], raw[1]
    last = jnp.where(row > lane, first, turned[0])
    last = jnp.where(row == lane, pltpu.roll(second, NRHS - 1, 0), last)
    last = jnp.where((row == NRHS - 1) & (lane == NRHS - 1), pltpu.roll(second, NRHS - 1, 1), last)
    even = [0.5 * (r + t) for r, t in zip(raw, turned)] + [last]
    even[0] = jnp.where(row <= lane, first, turned[0])
    even[1] = jnp.where(row <= lane, second, turned[1])
    even = [jnp.where(lane < NRHS, e, 0.0) for e in even]
    return even[:2] + [2.0 * even[n] - even[n % 2] for n in range(2, 2 * S + 1)]


def solve_small(m):
    lane = lanes_of((NRHS, LANES))
    half = HALF_WIDTH / 2
    size = S * NRHS

    def a_on(seq, n):
        return CENTRE * seq[n] + half * (seq[n + 1] + seq[abs(n - 1)])

    nu = [a_on(m, n) for n in range(2 * S)]
    mu = [a_on(nu, n) for n in range(2 * S - 1)]
    up = functools.reduce(jnp.add, [mu[n] if n == 0 else pltpu.roll(mu[n], NRHS * n, 1) for n in range(2 * S - 1)])
    around = functools.reduce(
        jnp.add,
        [mu[abs(n - (S - 1))] if n == 0 else pltpu.roll(mu[abs(n - (S - 1))], NRHS * n, 1) for n in range(2 * S - 1)],
    )

    def left(f, places):
        return f if places == 0 else pltpu.roll(f, LANES - places, 1)

    rows = []
    for c in range(S):
        both = 0.5 * (left(up, NRHS * c) + left(around, NRHS * (S - 1 - c)))
        rows.append(jnp.where(lane < size, both, pltpu.roll(nu[c], size, 1)))
    m = jnp.concatenate(rows, axis=0)
    row, col = rows_at((size, LANES)), lanes_of((size, LANES))
    on = row == col
    kept = jnp.where(on, m, 0.0)
    scale = 1.0 / jnp.sqrt(jnp.sum(kept, axis=1, keepdims=True))
    across = jnp.sum(kept, axis=0, keepdims=True)
    across = jnp.where(lanes_of((1, LANES)) < size, 1.0 / jnp.sqrt(across), 1.0)
    m = scale * m * across + jnp.where(on, RIDGE, 0.0)
    for i in range(0, size, 2):
        c0 = jnp.broadcast_to(m[:, i : i + 1], m.shape)
        c1 = jnp.broadcast_to(m[:, i + 1 : i + 2], m.shape)
        r0, r1 = m[i : i + 1], m[i + 1 : i + 2]
        a, b, d = c0[i : i + 1], c1[i : i + 1], c1[i + 1 : i + 2]
        inverse = 1.0 / (a * d - b * b)
        q0 = inverse * (d * r0 - b * r1)
        q1 = inverse * (a * r1 - b * r0)
        c0 = jnp.where(row == i, c0 - 1.0, c0)
        c1 = jnp.where(row == i + 1, c1 - 1.0, c1)
        m = m - c0 * q0 - c1 * q1
    x = jnp.where((col >= size) & (col < size + NRHS), scale * m, 0.0)
    shift = NRHS
    while shift < LANES:
        x = x + pltpu.roll(x, shift, 1)
        shift *= 2
    c = [x[j * NRHS : (j + 1) * NRHS] for j in range(S)]
    unit = jnp.where(rows_at((NRHS, LANES)) == lane % NRHS, 1.0, 0.0)
    remain = []
    for j in range(S + 1):
        total = CENTRE * c[j] if j < S else 0.0
        if j > 0:
            total = total + (HALF_WIDTH if j == 1 else half) * c[j - 1]
        if j + 1 < S:
            total = total + half * c[j + 1]
        remain.append((unit if j == 0 else 0.0) - total)
    return c, remain


def combine_kernel(guess, rough, fine, parts, update, rest, wh, wl):
    nx, ny, _ = guess.shape
    level = lanes_of((NRHS, LANES)) // NRHS
    coeffs, remain = solve_small(moment_blocks(jnp.sum(parts[...], axis=0)))
    coeffs = coeffs + [jnp.zeros((NRHS, LANES), jnp.float32)]
    for part, tiles in ((0, coeffs), (1, remain)):
        for j in range(S + 1):
            full = jnp.concatenate(
                [jnp.where(level == z, tiles[j], 0.0) for z in range(LANES // NRHS)], axis=0
            )
            high, low = halves(full)
            wh[j * LANES : (j + 1) * LANES, part * LANES : (part + 1) * LANES] = high
            wl[j * LANES : (j + 1) * LANES, part * LANES : (part + 1) * LANES] = low
    chunk = nx // 4
    for i in range(4):
        at = slice(i * chunk, (i + 1) * chunk)
        cells = slice(i * chunk * ny, (i + 1) * chunk * ny)
        dot = functools.partial(jnp.dot, preferred_element_type=jnp.float32)
        out = dot(rough[cells], wh[...]) + dot(rough[cells], wl[...]) + dot(fine[cells], wh[...])
        out = out.reshape(chunk, ny, 2 * LANES)
        update[at] = guess[at] + out[:, :, :LANES]
        rest[at] = out[:, :, LANES:]


def call(kernel, ins, outs, scratch=(), scalars=0, kinds=None):
    specs = [pl.BlockSpec(memory_space=pltpu.SMEM)] * scalars
    specs += [pl.BlockSpec(memory_space=pltpu.VMEM)] * (len(ins) - scalars)
    result = pl.pallas_call(
        kernel,
        out_shape=[
            jax.ShapeDtypeStruct(s, k) for s, k in zip(outs, kinds or [jnp.float32] * len(outs))
        ],
        in_specs=specs,
        out_specs=[pl.BlockSpec(memory_space=pltpu.VMEM)] * len(outs),
        scratch_shapes=list(scratch),
        compiler_params=pltpu.CompilerParams(vmem_limit_bytes=VMEM_BYTES),
    )(*ins)
    return result


def exchange(first, second, axis):
    count = lax.axis_size(axis)
    got = []
    for cells, start in ((first, 0), (second, 1)):
        links = []
        for i in range(start, count - 1, 2):
            links += [(i, i + 1), (i + 1, i)]
        got.append(lax.ppermute(cells, axis, links))
    return got


def total_of(x, axis):
    count = lax.axis_size(axis)
    if count & (count - 1):
        return lax.psum(x, axis)
    step = 1
    while step < count:
        x = x + lax.ppermute(x, axis, [(i, i ^ step) for i in range(count)])
        step *= 2
    return x


def totals(parts):
    count = parts.shape[0]
    if count > 1:
        return lax.all_to_all(parts, ("gx", "gy"), 0, 0)
    return total_of(total_of(parts, "gy"), "gx")


def body(initial_guess, source, leaf_density, absorption):
    nx, ny, lanes = initial_guess.shape
    root = jnp.sqrt(PEAK_COND / (1.0 + leaf_density))
    ra = jnp.concatenate([root, absorption], axis=-1)
    px = lax.rem(lax.axis_index("gx"), 2).astype(jnp.int32).reshape(1)
    py = lax.rem(lax.axis_index("gy"), 2).astype(jnp.int32).reshape(1)
    wide = nx + 2 * DEEP
    tall = ny + 2 * DEEP
    block = (nx, ny, lanes)
    x_rows = DEEP * ny + ny + 2 * DEEP + 8 + DEEP // 4 * ny
    y_rows = wide * DEEP + wide + 8 + wide // 4 * DEEP
    root, absb, b0, xa, xb = call(
        begin_kernel,
        (px, initial_guess, source, ra),
        (block, block, block, (x_rows, lanes), (x_rows, lanes)),
        scalars=1,
    )
    xa, xb = exchange(xa, xb, "gx")
    broad = (wide, ny, lanes)
    rootx, absx, b0x, edge, ya, yb = call(
        widen_kernel,
        (px, py, xa, xb, initial_guess, root, absb, b0),
        (broad, broad, broad, (2, wide + 8, lanes), (y_rows, lanes), (y_rows, lanes)),
        scratch=[pltpu.VMEM((2, ny, lanes), jnp.float32)],
        scalars=2,
    )
    ya, yb = exchange(ya, yb, "gy")
    frame = pltpu.VMEM((wide, tall, lanes), jnp.float32)
    count = lax.axis_size("gx") * lax.axis_size("gy")
    count = count if count <= 64 else 1
    cells = nx * ny
    rough, fine, moments = call(
        basis_kernel,
        (py, ya, yb, rootx, absx, b0x, edge),
        ((cells, (S + 1) * lanes), (cells, (S + 1) * lanes), (count, NRHS, lanes)),
        scratch=[frame, frame, pltpu.VMEM((2, wide + 8, lanes), jnp.float32), frame, frame, frame],
        scalars=1,
        kinds=(jnp.bfloat16, jnp.bfloat16, jnp.float32),
    )
    return call(
        combine_kernel,
        (initial_guess, rough, fine, totals(moments)),
        (block, block),
        scratch=[pltpu.VMEM(((S + 1) * lanes, 2 * lanes), jnp.bfloat16)] * 2,
    )


def solution(mesh):
    spec = P("gx", "gy", None)
    return jax.shard_map(
        lambda *arrays: tuple(body(*arrays)),
        mesh=mesh,
        in_specs=(spec,) * 4,
        out_specs=(spec, spec),
        check_vma=False,
    )
```

```python
import functools

import jax
import jax.numpy as jnp
from jax import lax
from jax.experimental import pallas as pl
from jax.experimental.pallas import tpu as pltpu
from jax.sharding import PartitionSpec as P

NRHS = 8
S = 8
DEEP = S
LANES = 128

PEAK_COND = 0.6
CENTRE = 10.3
HALF_WIDTH = 9.8
RIDGE = 0.05
PANEL = 8
VMEM_BYTES = 48 * 1024 * 1024


def lanes_of(shape):
    return lax.broadcasted_iota(jnp.int32, shape, len(shape) - 1)


def rows_at(shape):
    return lax.broadcasted_iota(jnp.int32, shape, len(shape) - 2)


def z_sum(f):
    lane = lanes_of(f.shape)
    ax = f.ndim - 1
    up = jnp.where(lane >= NRHS, pltpu.roll(f, NRHS, ax), 0.0)
    down = jnp.where(lane < LANES - NRHS, pltpu.roll(f, LANES - NRHS, ax), 0.0)
    return up + down


def row_sum(f):
    n = f.shape[-2]
    ax = f.ndim - 2
    return pltpu.roll(f, 1, ax) + pltpu.roll(f, n - 1, ax)


def row_sum_zero(f):
    n = f.shape[-2]
    ax = f.ndim - 2
    row = rows_at(f.shape)
    up = jnp.where(row >= 1, pltpu.roll(f, 1, ax), 0.0)
    down = jnp.where(row < n - 1, pltpu.roll(f, n - 1, ax), 0.0)
    return up + down


def slab_sum(before, here, after, rows):
    ux = before[0] + after[0]
    px = before[1] + after[1]
    s = here[1] + ux
    q = here[0] + 0.5 * s + (1.0 / 3.0) * px
    return s + 0.5 * px + rows(q)


def cross_sum(f, rows):
    p = z_sum(f)
    return f + 0.5 * p + rows(0.5 * f + (1.0 / 3.0) * p)


def spread(rows):
    n = rows.shape[0]
    depth = LANES // NRHS
    at = rows_at((NRHS, LANES)) * depth + lanes_of((NRHS, LANES)) // NRHS
    out = []
    for x in range(n):
        line = jnp.broadcast_to(rows[x : x + 1], (NRHS, LANES))
        out.append(jnp.take_along_axis(line, at, axis=1))
    return jnp.stack(out)


def begin_kernel(px, guess, source, leaf, absorb, root_o, abs_o, b0_o, send_a, send_b, root, absb):
    nx, ny, _ = guess.shape
    depth = leaf.shape[1]
    turned = jnp.transpose(leaf[...].reshape(ny * depth, nx))
    root_o[...] = jnp.sqrt(PEAK_COND / (1.0 + turned))
    abs_o[...] = jnp.transpose(absorb[...].reshape(ny * depth, nx))
    for part, wide in ((root_o, root), (abs_o, absb)):
        for y in range(0, ny, NRHS):
            wide[:, y : y + NRHS, :] = spread(part[:, y * depth : (y + NRHS) * depth])
    zero = jnp.zeros((ny, LANES), jnp.float32)

    def pair(x, field):
        if x < 0 or x >= nx:
            return (zero, zero)
        u = root[x] if field is None else root[x] * field[x]
        return (u, z_sum(u))

    moving = [pair(-1, guess), pair(0, guess)]
    still = [pair(-1, None), pair(0, None)]
    for x in range(nx):
        moving.append(pair(x + 1, guess))
        still.append(pair(x + 1, None))
        wu = slab_sum(*moving, row_sum_zero)
        wr = slab_sum(*still, row_sum_zero)
        moving, still = moving[1:], still[1:]
        v = guess[x]
        b0_o[x] = source[x] - absb[x] * v + root[x] * (wu - v * wr)

    def write(out, x0, face, beyond):
        n = DEEP * ny
        out[0:n] = b0_o[x0 : x0 + DEEP].reshape(n, LANES)
        out[n : n + ny] = guess[face]
        n += ny
        for col in (0, ny - 1):
            out[n : n + DEEP] = guess[x0 : x0 + DEEP, col, :]
            n += DEEP
        out[n : n + 8] = jnp.zeros((8, LANES), jnp.float32)
        for at, col in ((0, 0), (1, ny - 1)):
            out[n + at : n + at + 1] = guess[beyond, col : col + 1, :]
            out[n + 2 + at : n + 3 + at] = root[beyond, col : col + 1, :]
        n += 8
        for part in (root_o, abs_o):
            for first in range(0, ny * depth, LANES):
                out[n : n + DEEP] = part[x0 : x0 + DEEP, first : first + LANES]
                n += DEEP

    @pl.when(px[0] == 0)
    def _():
        write(send_a, nx - DEEP, nx - 1, nx - DEEP - 1)
        write(send_b, 0, 0, DEEP)

    @pl.when(px[0] == 1)
    def _():
        write(send_b, nx - DEEP, nx - 1, nx - DEEP - 1)
        write(send_a, 0, 0, DEEP)


def widen_kernel(
    px, py, recv_a, recv_b, guess, root, absb, b0, rootx, absx, b0x, edge, send_a, send_b, face
):
    nx, ny, _ = guess.shape
    wide = nx + 2 * DEEP
    rootx[DEEP : DEEP + nx] = root[...]
    absx[DEEP : DEEP + nx] = absb[...]
    b0x[DEEP : DEEP + nx] = b0[...]
    for at, col in ((0, 0), (1, ny - 1)):
        edge[at, DEEP : DEEP + nx] = guess[:, col, :]
        edge[at, wide : wide + 8] = jnp.zeros((8, LANES), jnp.float32)

    def read(msg, x0, side):
        n = DEEP * ny
        b0x[x0 : x0 + DEEP] = msg[0:n].reshape(DEEP, ny, LANES)
        face[side] = msg[n : n + ny]
        n += ny
        for at in (0, 1):
            edge[at, x0 : x0 + DEEP] = msg[n : n + DEEP]
            n += DEEP
        for at in (0, 1):
            edge[at, wide + side : wide + side + 1] = msg[n + at : n + at + 1]
            edge[at, wide + 2 + side : wide + 3 + side] = msg[n + 2 + at : n + 3 + at]
        n += 8
        for out in (rootx, absx):
            for first in range(0, out.shape[1], LANES):
                out[x0 : x0 + DEEP, first : first + LANES] = msg[n : n + DEEP]
                n += DEEP

    @pl.when(px[0] == 0)
    def _():
        read(recv_b, 0, 0)
        read(recv_a, DEEP + nx, 1)

    @pl.when(px[0] == 1)
    def _():
        read(recv_a, 0, 0)
        read(recv_b, DEEP + nx, 1)

    def root_line(x):
        parts = [
            spread(rootx[x : x + 1, first : first + LANES])
            for first in range(0, rootx.shape[1], LANES)
        ]
        return jnp.concatenate(parts, axis=1)[0]

    for side, out_x, in_x, own in ((0, DEEP - 1, DEEP, 0), (1, DEEP + nx, DEEP + nx - 1, nx - 1)):
        va, ra = face[side], root_line(out_x)
        vb, rb = guess[own], root_line(in_x)
        fix_a = ra * (cross_sum(rb * vb, row_sum_zero) - va * cross_sum(rb, row_sum_zero))
        fix_b = rb * (cross_sum(ra * va, row_sum_zero) - vb * cross_sum(ra, row_sum_zero))
        b0x[out_x] = b0x[out_x] + fix_a
        b0x[in_x] = b0x[in_x] + fix_b

    def write(out, y0, at):
        n = wide * DEEP
        out[0:n] = b0x[:, y0 : y0 + DEEP, :].reshape(n, LANES)
        out[n : n + wide + 8] = edge[at]
        n += wide + 8
        first = y0 * (LANES // NRHS)
        for part in (rootx, absx):
            out[n : n + wide] = part[:, first : first + LANES]
            n += wide

    @pl.when(py[0] == 0)
    def _():
        write(send_a, ny - DEEP, 1)
        write(send_b, 0, 0)

    @pl.when(py[0] == 1)
    def _():
        write(send_b, ny - DEEP, 1)
        write(send_a, 0, 0)


def halves(a):
    high = a.astype(jnp.bfloat16)
    return high, (a - high.astype(jnp.float32)).astype(jnp.bfloat16)


def basis_kernel(
    py, recv_a, recv_b, rootx, absx, b0x, edge, rough, fine, moments, root, diag, far, f0, f1, f2
):
    wide, ny, _ = b0x.shape
    nx = wide - 2 * DEEP
    tall = ny + 2 * DEEP
    depth = LANES // NRHS
    for part, out in ((rootx, root), (absx, diag)):
        for y in range(0, ny, DEEP):
            first = y * depth
            out[:, DEEP + y : 2 * DEEP + y, :] = spread(part[:, first : first + LANES])
    f0[:, DEEP : DEEP + ny, :] = b0x[...]

    def read(msg, y0, side):
        n = wide * DEEP
        f0[:, y0 : y0 + DEEP, :] = msg[0:n].reshape(wide, DEEP, LANES)
        far[side] = msg[n : n + wide + 8]
        n += wide + 8
        for out in (root, diag):
            out[:, y0 : y0 + DEEP, :] = spread(msg[n : n + wide])
            n += wide

    @pl.when(py[0] == 0)
    def _():
        read(recv_b, 0, 0)
        read(recv_a, DEEP + ny, 1)

    @pl.when(py[0] == 1)
    def _():
        read(recv_a, 0, 0)
        read(recv_b, DEEP + ny, 1)

    row = lax.broadcasted_iota(jnp.int32, (wide, LANES), 0)

    def across(f, before, after):
        p = z_sum(f)
        ends = jnp.concatenate([before, after], axis=0)
        ends = 0.5 * ends + (1.0 / 3.0) * z_sum(ends)
        g = 0.5 * f + (1.0 / 3.0) * p
        up = jnp.where(row == 0, ends[0:1], pltpu.roll(g, 1, 0))
        down = jnp.where(row == wide - 1, ends[1:2], pltpu.roll(g, wide - 1, 0))
        return f + 0.5 * p + up + down

    def column(ref, at, y):
        v = ref[at, 0:wide]
        ends = ref[at, wide : wide + 8]
        r = root[:, y, :]
        r0, r1 = ends[2:3], ends[3:4]
        return v, r, across(r * v, r0 * ends[0:1], r1 * ends[1:2]), across(r, r0, r1)

    for side, out_y, in_y in ((0, DEEP - 1, DEEP), (1, DEEP + ny, DEEP + ny - 1)):
        va, ra, ua, wa = column(far, side, out_y)
        vb, rb, ub, wb = column(edge, side, in_y)
        f0[:, out_y, :] = f0[:, out_y, :] + ra * (ub - va * wb)
        f0[:, in_y, :] = f0[:, in_y, :] + rb * (ua - vb * wa)

    def pair(src, x):
        u = root[x] if src is None else root[x] * src[x]
        return (u, z_sum(u))

    def sweep(src, lo, hi, put):
        first, second = pair(src, lo - 1), pair(src, lo)
        for x in range(lo, hi):
            third = pair(src, x + 1)
            put(x, slab_sum(first, second, third, row_sum))
            first, second = second, third

    def put_diag(x, total):
        diag[x] = (diag[x] + root[x] * total - CENTRE) * (2.0 / HALF_WIDTH)

    sweep(None, 1, wide - 1, put_diag)

    level = lanes_of((NRHS, LANES)) // NRHS
    depth = LANES // NRHS
    folded = [None] * (2 * S + 1)

    def note(n, block):
        if n in (0, 1, 2 * S):
            block = 0.5 * (block + block.T)
        f = block[0:NRHS]
        for z in range(1, depth):
            f = jnp.where(level == z, block[z * NRHS : (z + 1) * NRHS], f)
        folded[n] = f

    frames = [f0, f1, f2]
    old = None
    for j in range(S + 1):
        now = frames[j % 3]
        if j > 0:
            src, prev = frames[(j - 1) % 3], frames[(j - 2) % 3]

            def put(x, total):
                new = diag[x] * src[x] - (2.0 / HALF_WIDTH) * root[x] * total
                now[x] = 0.5 * new if j == 1 else new - prev[x]

            sweep(src, j, wide - j, put)
        own = now[DEEP : DEEP + nx, DEEP : DEEP + ny, :]
        high, low = halves(own.reshape(nx * ny, LANES))
        rough[:, j * LANES : (j + 1) * LANES] = high
        fine[:, j * LANES : (j + 1) * LANES] = low
        turned = high.T
        both = jnp.concatenate([high, low], axis=1)
        left = turned if j == 0 else jnp.concatenate([turned, old[0]], axis=0)
        got = jnp.dot(left, both, preferred_element_type=jnp.float32)
        note(2 * j, got[:LANES, :LANES] + 2.0 * got[:LANES, LANES:])
        if j > 0:
            rest = jnp.dot(turned, old[1], preferred_element_type=jnp.float32)
            note(2 * j - 1, got[LANES:, :LANES] + got[LANES:, LANES:] + rest)
        old = (turned, low)
    every = jnp.concatenate(folded, axis=0)
    shift = LANES // 2
    while shift >= NRHS:
        every = every + pltpu.roll(every, shift, 1)
        shift //= 2
    blocks = [every[n * NRHS : (n + 1) * NRHS] for n in range(2 * S + 1)]
    tile = jnp.zeros((NRHS, LANES), jnp.float32)
    row, col = rows_at((NRHS, LANES)), lanes_of((NRHS, LANES)) % NRHS
    last = blocks[2 * S]
    below = jnp.where(row == col + 1, pltpu.roll(last, 1, 0), 0.0)
    below = jnp.where((row == NRHS - 1) & (col == 0), pltpu.roll(last, 1, 1), below)
    blocks[0] = jnp.where(row <= col, blocks[0], last)
    blocks[1] = jnp.where(row <= col, blocks[1], below)
    for n in range(2 * S):
        tile = jnp.where(level == n, blocks[n], tile)
    moments[...] = jnp.broadcast_to(tile[None], moments.shape)


def moment_blocks(tile):
    depth = LANES // NRHS
    row, lane = rows_at((NRHS, LANES)), lanes_of((NRHS, LANES))
    raw = [tile] + [pltpu.roll(tile, LANES - NRHS * n, 1) for n in range(1, depth)]
    square = jnp.concatenate([tile, jnp.zeros((LANES - NRHS, LANES), jnp.float32)], axis=0).T
    turned = [square[n * NRHS : (n + 1) * NRHS] for n in range(depth)]
    first, second = raw[0], raw[1]
    last = jnp.where(row > lane, first, turned[0])
    last = jnp.where(row == lane, pltpu.roll(second, NRHS - 1, 0), last)
    last = jnp.where((row == NRHS - 1) & (lane == NRHS - 1), pltpu.roll(second, NRHS - 1, 1), last)
    even = [0.5 * (r + t) for r, t in zip(raw, turned)] + [last]
    even[0] = jnp.where(row <= lane, first, turned[0])
    even[1] = jnp.where(row <= lane, second, turned[1])
    even = [jnp.where(lane < NRHS, e, 0.0) for e in even]
    return even[:2] + [2.0 * even[n] - even[n % 2] for n in range(2, 2 * S + 1)]


def solve_small(m):
    lane = lanes_of((NRHS, LANES))
    half = HALF_WIDTH / 2
    size = S * NRHS

    def a_on(seq, n):
        return CENTRE * seq[n] + half * (seq[n + 1] + seq[abs(n - 1)])

    nu = [a_on(m, n) for n in range(2 * S)]
    mu = [a_on(nu, n) for n in range(2 * S - 1)]
    up = functools.reduce(jnp.add, [mu[n] if n == 0 else pltpu.roll(mu[n], NRHS * n, 1) for n in range(2 * S - 1)])
    around = functools.reduce(
        jnp.add,
        [mu[abs(n - (S - 1))] if n == 0 else pltpu.roll(mu[abs(n - (S - 1))], NRHS * n, 1) for n in range(2 * S - 1)],
    )

    def left(f, places):
        return f if places == 0 else pltpu.roll(f, LANES - places, 1)

    rows = []
    for c in range(S):
        both = 0.5 * (left(up, NRHS * c) + left(around, NRHS * (S - 1 - c)))
        rows.append(jnp.where(lane < size, both, pltpu.roll(nu[c], size, 1)))
    m = jnp.concatenate(rows, axis=0)
    row, col = rows_at((size, LANES)), lanes_of((size, LANES))
    on = row == col
    kept = jnp.where(on, m, 0.0)
    scale = 1.0 / jnp.sqrt(jnp.sum(kept, axis=1, keepdims=True))
    across = jnp.sum(kept, axis=0, keepdims=True)
    across = jnp.where(lanes_of((1, LANES)) < size, 1.0 / jnp.sqrt(across), 1.0)
    m = scale * m * across + jnp.where(on, RIDGE, 0.0)
    for first in range(0, size, PANEL):
        columns = [
            jnp.broadcast_to(m[:, i : i + 1], m.shape) for i in range(first, first + PANEL)
        ]
        for p in range(0, PANEL, 2):
            i = first + p
            c0, c1 = columns[p], columns[p + 1]
            a, b, d = c0[i : i + 1], c1[i : i + 1], c1[i + 1 : i + 2]
            inverse = 1.0 / (a * d - b * b)
            a, b, d = inverse * a, inverse * b, inverse * d
            d0 = jnp.where(row == i, c0 - 1.0, c0)
            d1 = jnp.where(row == i + 1, c1 - 1.0, c1)
            for later in range(p + 2, PANEL):
                r0 = c0[first + later : first + later + 1]
                r1 = c1[first + later : first + later + 1]
                columns[later] = columns[later] - d0 * (d * r0 - b * r1) - d1 * (a * r1 - b * r0)
            r0, r1 = m[i : i + 1], m[i + 1 : i + 2]
            m = m - d0 * (d * r0 - b * r1) - d1 * (a * r1 - b * r0)
    x = jnp.where((col >= size) & (col < size + NRHS), scale * m, 0.0)
    shift = NRHS
    while shift < LANES:
        x = x + pltpu.roll(x, shift, 1)
        shift *= 2
    c = [x[j * NRHS : (j + 1) * NRHS] for j in range(S)]
    unit = jnp.where(rows_at((NRHS, LANES)) == lane % NRHS, 1.0, 0.0)
    remain = []
    for j in range(S + 1):
        total = CENTRE * c[j] if j < S else 0.0
        if j > 0:
            total = total + (HALF_WIDTH if j == 1 else half) * c[j - 1]
        if j + 1 < S:
            total = total + half * c[j + 1]
        remain.append((unit if j == 0 else 0.0) - total)
    return c, remain


def combine_kernel(guess, rough, fine, parts, update, rest, wh, wl):
    nx, ny, _ = guess.shape
    level = lanes_of((NRHS, LANES)) // NRHS
    coeffs, remain = solve_small(moment_blocks(jnp.sum(parts[...], axis=0)))
    coeffs = coeffs + [jnp.zeros((NRHS, LANES), jnp.float32)]
    for part, tiles in ((0, coeffs), (1, remain)):
        for j in range(S + 1):
            full = jnp.concatenate(
                [jnp.where(level == z, tiles[j], 0.0) for z in range(LANES // NRHS)], axis=0
            )
            high, low = halves(full)
            wh[j * LANES : (j + 1) * LANES, part * LANES : (part + 1) * LANES] = high
            wl[j * LANES : (j + 1) * LANES, part * LANES : (part + 1) * LANES] = low
    chunk = nx // 4
    for i in range(4):
        at = slice(i * chunk, (i + 1) * chunk)
        cells = slice(i * chunk * ny, (i + 1) * chunk * ny)
        dot = functools.partial(jnp.dot, preferred_element_type=jnp.float32)
        out = dot(rough[cells], wh[...]) + dot(rough[cells], wl[...]) + dot(fine[cells], wh[...])
        out = out.reshape(chunk, ny, 2 * LANES)
        update[at] = guess[at] + out[:, :, :LANES]
        rest[at] = out[:, :, LANES:]


def call(kernel, ins, outs, scratch=(), scalars=0, kinds=None):
    specs = [pl.BlockSpec(memory_space=pltpu.SMEM)] * scalars
    specs += [pl.BlockSpec(memory_space=pltpu.VMEM)] * (len(ins) - scalars)
    result = pl.pallas_call(
        kernel,
        out_shape=[
            jax.ShapeDtypeStruct(s, k) for s, k in zip(outs, kinds or [jnp.float32] * len(outs))
        ],
        in_specs=specs,
        out_specs=[pl.BlockSpec(memory_space=pltpu.VMEM)] * len(outs),
        scratch_shapes=list(scratch),
        compiler_params=pltpu.CompilerParams(vmem_limit_bytes=VMEM_BYTES),
    )(*ins)
    return result


def exchange(first, second, axis):
    count = lax.axis_size(axis)
    got = []
    for cells, start in ((first, 0), (second, 1)):
        links = []
        for i in range(start, count - 1, 2):
            links += [(i, i + 1), (i + 1, i)]
        got.append(lax.ppermute(cells, axis, links))
    return got


def total_of(x, axis):
    count = lax.axis_size(axis)
    if count & (count - 1):
        return lax.psum(x, axis)
    step = 1
    while step < count:
        x = x + lax.ppermute(x, axis, [(i, i ^ step) for i in range(count)])
        step *= 2
    return x


def totals(parts):
    count = parts.shape[0]
    if count > 1:
        return lax.all_to_all(parts, ("gx", "gy"), 0, 0)
    return total_of(total_of(parts, "gy"), "gx")


def body(initial_guess, source, leaf_density, absorption):
    nx, ny, lanes = initial_guess.shape
    leaf = jnp.transpose(leaf_density, (1, 2, 0))
    absorb = jnp.transpose(absorption, (1, 2, 0))
    depth = leaf.shape[1]
    px = lax.rem(lax.axis_index("gx"), 2).astype(jnp.int32).reshape(1)
    py = lax.rem(lax.axis_index("gy"), 2).astype(jnp.int32).reshape(1)
    wide = nx + 2 * DEEP
    tall = ny + 2 * DEEP
    block = (nx, ny, lanes)
    across = ny * depth
    x_rows = DEEP * ny + ny + 2 * DEEP + 8 + 2 * DEEP * (across // lanes)
    y_rows = wide * DEEP + wide + 8 + 2 * wide
    root, absb, b0, xa, xb = call(
        begin_kernel,
        (px, initial_guess, source, leaf, absorb),
        ((nx, across), (nx, across), block, (x_rows, lanes), (x_rows, lanes)),
        scratch=[pltpu.VMEM(block, jnp.float32)] * 2,
        scalars=1,
    )
    xa, xb = exchange(xa, xb, "gx")
    broad = (wide, ny, lanes)
    rootx, absx, b0x, edge, ya, yb = call(
        widen_kernel,
        (px, py, xa, xb, initial_guess, root, absb, b0),
        ((wide, across), (wide, across), broad, (2, wide + 8, lanes), (y_rows, lanes), (y_rows, lanes)),
        scratch=[pltpu.VMEM((2, ny, lanes), jnp.float32)],
        scalars=2,
    )
    ya, yb = exchange(ya, yb, "gy")
    frame = pltpu.VMEM((wide, tall, lanes), jnp.float32)
    count = lax.axis_size("gx") * lax.axis_size("gy")
    count = count if count <= 64 else 1
    cells = nx * ny
    rough, fine, moments = call(
        basis_kernel,
        (py, ya, yb, rootx, absx, b0x, edge),
        ((cells, (S + 1) * lanes), (cells, (S + 1) * lanes), (count, NRHS, lanes)),
        scratch=[frame, frame, pltpu.VMEM((2, wide + 8, lanes), jnp.float32), frame, frame, frame],
        scalars=1,
        kinds=(jnp.bfloat16, jnp.bfloat16, jnp.float32),
    )
    return call(
        combine_kernel,
        (initial_guess, rough, fine, totals(moments)),
        (block, block),
        scratch=[pltpu.VMEM(((S + 1) * lanes, 2 * lanes), jnp.bfloat16)] * 2,
    )


def solution(mesh):
    spec = P("gx", "gy", None)
    return jax.shard_map(
        lambda *arrays: tuple(body(*arrays)),
        mesh=mesh,
        in_specs=(spec,) * 4,
        out_specs=(spec, spec),
        check_vma=False,
    )
```

```python
import functools

import jax
import jax.numpy as jnp
from jax import lax
from jax.experimental import pallas as pl
from jax.experimental.pallas import tpu as pltpu
from jax.sharding import PartitionSpec as P

NRHS = 8
S = 8
DEEP = S
LANES = 128

PEAK_COND = 0.6
CENTRE = 10.3
HALF_WIDTH = 9.8
RIDGE = 0.05
PANEL = 16
VMEM_BYTES = 48 * 1024 * 1024


def lanes_of(shape):
    return lax.broadcasted_iota(jnp.int32, shape, len(shape) - 1)


def rows_at(shape):
    return lax.broadcasted_iota(jnp.int32, shape, len(shape) - 2)


def z_sum(f):
    lane = lanes_of(f.shape)
    ax = f.ndim - 1
    up = jnp.where(lane >= NRHS, pltpu.roll(f, NRHS, ax), 0.0)
    down = jnp.where(lane < LANES - NRHS, pltpu.roll(f, LANES - NRHS, ax), 0.0)
    return up + down


def row_sum(f):
    n = f.shape[-2]
    ax = f.ndim - 2
    return pltpu.roll(f, 1, ax) + pltpu.roll(f, n - 1, ax)


def row_sum_zero(f):
    n = f.shape[-2]
    ax = f.ndim - 2
    row = rows_at(f.shape)
    up = jnp.where(row >= 1, pltpu.roll(f, 1, ax), 0.0)
    down = jnp.where(row < n - 1, pltpu.roll(f, n - 1, ax), 0.0)
    return up + down


def slab_sum(before, here, after, rows):
    ux = before[0] + after[0]
    px = before[1] + after[1]
    s = here[1] + ux
    q = here[0] + 0.5 * s + (1.0 / 3.0) * px
    return s + 0.5 * px + rows(q)


def cross_sum(f, rows):
    p = z_sum(f)
    return f + 0.5 * p + rows(0.5 * f + (1.0 / 3.0) * p)


def spread(rows):
    n = rows.shape[0]
    depth = LANES // NRHS
    at = rows_at((NRHS, LANES)) * depth + lanes_of((NRHS, LANES)) // NRHS
    out = []
    for x in range(n):
        line = jnp.broadcast_to(rows[x : x + 1], (NRHS, LANES))
        out.append(jnp.take_along_axis(line, at, axis=1))
    return jnp.stack(out)


def begin_kernel(px, *refs):
    far, refs = refs[:4], refs[4:]
    (root_o, abs_o, b0_o, edge_o, face_o, send_a, send_b), refs = refs[:7], refs[7:]
    guess, source, leaf, absorb, root, absb, sems = refs
    copies = [
        pltpu.make_async_copy(there, here, sems.at[i])
        for i, (there, here) in enumerate(zip(far, (guess, source, leaf, absorb)))
    ]
    for i in (2, 3, 0, 1):
        copies[i].start()
    nx, ny, _ = guess.shape
    depth = leaf.shape[1]
    copies[2].wait()
    copies[3].wait()
    turned = jnp.transpose(leaf[...].reshape(ny * depth, nx))
    root_o[...] = jnp.sqrt(PEAK_COND / (1.0 + turned))
    abs_o[...] = jnp.transpose(absorb[...].reshape(ny * depth, nx))
    for part, wide in ((root_o, root), (abs_o, absb)):
        for y in range(0, ny, NRHS):
            wide[:, y : y + NRHS, :] = spread(part[:, y * depth : (y + NRHS) * depth])
    copies[0].wait()
    copies[1].wait()
    for at, col, face in ((0, 0, 0), (1, ny - 1, nx - 1)):
        edge_o[at] = guess[:, col, :]
        face_o[at] = guess[face]
    zero = jnp.zeros((ny, LANES), jnp.float32)

    def pair(x, field):
        if x < 0 or x >= nx:
            return (zero, zero)
        u = root[x] if field is None else root[x] * field[x]
        return (u, z_sum(u))

    moving = [pair(-1, guess), pair(0, guess)]
    still = [pair(-1, None), pair(0, None)]
    for x in range(nx):
        moving.append(pair(x + 1, guess))
        still.append(pair(x + 1, None))
        wu = slab_sum(*moving, row_sum_zero)
        wr = slab_sum(*still, row_sum_zero)
        moving, still = moving[1:], still[1:]
        v = guess[x]
        b0_o[x] = source[x] - absb[x] * v + root[x] * (wu - v * wr)

    def write(out, x0, face, beyond):
        n = DEEP * ny
        out[0:n] = b0_o[x0 : x0 + DEEP].reshape(n, LANES)
        out[n : n + ny] = guess[face]
        n += ny
        for col in (0, ny - 1):
            out[n : n + DEEP] = guess[x0 : x0 + DEEP, col, :]
            n += DEEP
        out[n : n + 8] = jnp.zeros((8, LANES), jnp.float32)
        for at, col in ((0, 0), (1, ny - 1)):
            out[n + at : n + at + 1] = guess[beyond, col : col + 1, :]
            out[n + 2 + at : n + 3 + at] = root[beyond, col : col + 1, :]
        n += 8
        for part in (root_o, abs_o):
            for first in range(0, ny * depth, LANES):
                out[n : n + DEEP] = part[x0 : x0 + DEEP, first : first + LANES]
                n += DEEP

    @pl.when(px[0] == 0)
    def _():
        write(send_a, nx - DEEP, nx - 1, nx - DEEP - 1)
        write(send_b, 0, 0, DEEP)

    @pl.when(px[0] == 1)
    def _():
        write(send_b, nx - DEEP, nx - 1, nx - DEEP - 1)
        write(send_a, 0, 0, DEEP)


def widen_kernel(
    px, py, recv_a, recv_b, edge_own, face_own, root, absb, b0,
    rootx, absx, b0x, edge, send_a, send_b, face
):
    nx, ny, _ = b0.shape
    wide = nx + 2 * DEEP
    rootx[DEEP : DEEP + nx] = root[...]
    absx[DEEP : DEEP + nx] = absb[...]
    b0x[DEEP : DEEP + nx] = b0[...]
    for at in (0, 1):
        edge[at, DEEP : DEEP + nx] = edge_own[at]
        edge[at, wide : wide + 8] = jnp.zeros((8, LANES), jnp.float32)

    def read(msg, x0, side):
        n = DEEP * ny
        b0x[x0 : x0 + DEEP] = msg[0:n].reshape(DEEP, ny, LANES)
        face[side] = msg[n : n + ny]
        n += ny
        for at in (0, 1):
            edge[at, x0 : x0 + DEEP] = msg[n : n + DEEP]
            n += DEEP
        for at in (0, 1):
            edge[at, wide + side : wide + side + 1] = msg[n + at : n + at + 1]
            edge[at, wide + 2 + side : wide + 3 + side] = msg[n + 2 + at : n + 3 + at]
        n += 8
        for out in (rootx, absx):
            for first in range(0, out.shape[1], LANES):
                out[x0 : x0 + DEEP, first : first + LANES] = msg[n : n + DEEP]
                n += DEEP

    @pl.when(px[0] == 0)
    def _():
        read(recv_b, 0, 0)
        read(recv_a, DEEP + nx, 1)

    @pl.when(px[0] == 1)
    def _():
        read(recv_a, 0, 0)
        read(recv_b, DEEP + nx, 1)

    def root_line(x):
        parts = [
            spread(rootx[x : x + 1, first : first + LANES])
            for first in range(0, rootx.shape[1], LANES)
        ]
        return jnp.concatenate(parts, axis=1)[0]

    for side, out_x, in_x in ((0, DEEP - 1, DEEP), (1, DEEP + nx, DEEP + nx - 1)):
        va, ra = face[side], root_line(out_x)
        vb, rb = face_own[side], root_line(in_x)
        fix_a = ra * (cross_sum(rb * vb, row_sum_zero) - va * cross_sum(rb, row_sum_zero))
        fix_b = rb * (cross_sum(ra * va, row_sum_zero) - vb * cross_sum(ra, row_sum_zero))
        b0x[out_x] = b0x[out_x] + fix_a
        b0x[in_x] = b0x[in_x] + fix_b

    def write(out, y0, at):
        n = wide * DEEP
        out[0:n] = b0x[:, y0 : y0 + DEEP, :].reshape(n, LANES)
        out[n : n + wide + 8] = edge[at]
        n += wide + 8
        first = y0 * (LANES // NRHS)
        for part in (rootx, absx):
            out[n : n + wide] = part[:, first : first + LANES]
            n += wide

    @pl.when(py[0] == 0)
    def _():
        write(send_a, ny - DEEP, 1)
        write(send_b, 0, 0)

    @pl.when(py[0] == 1)
    def _():
        write(send_b, ny - DEEP, 1)
        write(send_a, 0, 0)


def halves(a):
    high = a.astype(jnp.bfloat16)
    return high, (a - high.astype(jnp.float32)).astype(jnp.bfloat16)


def basis_kernel(
    py, recv_a, recv_b, rootx, absx, b0x, edge, rough, fine, moments, root, diag, far, f0, f1, f2
):
    wide, ny, _ = b0x.shape
    nx = wide - 2 * DEEP
    tall = ny + 2 * DEEP
    depth = LANES // NRHS
    for part, out in ((rootx, root), (absx, diag)):
        for y in range(0, ny, DEEP):
            first = y * depth
            out[:, DEEP + y : 2 * DEEP + y, :] = spread(part[:, first : first + LANES])
    f0[:, DEEP : DEEP + ny, :] = b0x[...]

    def read(msg, y0, side):
        n = wide * DEEP
        f0[:, y0 : y0 + DEEP, :] = msg[0:n].reshape(wide, DEEP, LANES)
        far[side] = msg[n : n + wide + 8]
        n += wide + 8
        for out in (root, diag):
            out[:, y0 : y0 + DEEP, :] = spread(msg[n : n + wide])
            n += wide

    @pl.when(py[0] == 0)
    def _():
        read(recv_b, 0, 0)
        read(recv_a, DEEP + ny, 1)

    @pl.when(py[0] == 1)
    def _():
        read(recv_a, 0, 0)
        read(recv_b, DEEP + ny, 1)

    row = lax.broadcasted_iota(jnp.int32, (wide, LANES), 0)

    def across(f, before, after):
        p = z_sum(f)
        ends = jnp.concatenate([before, after], axis=0)
        ends = 0.5 * ends + (1.0 / 3.0) * z_sum(ends)
        g = 0.5 * f + (1.0 / 3.0) * p
        up = jnp.where(row == 0, ends[0:1], pltpu.roll(g, 1, 0))
        down = jnp.where(row == wide - 1, ends[1:2], pltpu.roll(g, wide - 1, 0))
        return f + 0.5 * p + up + down

    def column(ref, at, y):
        v = ref[at, 0:wide]
        ends = ref[at, wide : wide + 8]
        r = root[:, y, :]
        r0, r1 = ends[2:3], ends[3:4]
        return v, r, across(r * v, r0 * ends[0:1], r1 * ends[1:2]), across(r, r0, r1)

    for side, out_y, in_y in ((0, DEEP - 1, DEEP), (1, DEEP + ny, DEEP + ny - 1)):
        va, ra, ua, wa = column(far, side, out_y)
        vb, rb, ub, wb = column(edge, side, in_y)
        f0[:, out_y, :] = f0[:, out_y, :] + ra * (ub - va * wb)
        f0[:, in_y, :] = f0[:, in_y, :] + rb * (ua - vb * wa)

    def pair(src, x):
        u = root[x] if src is None else root[x] * src[x]
        return (u, z_sum(u))

    def sweep(src, lo, hi, put):
        first, second = pair(src, lo - 1), pair(src, lo)
        for x in range(lo, hi):
            third = pair(src, x + 1)
            put(x, slab_sum(first, second, third, row_sum))
            first, second = second, third

    def put_diag(x, total):
        diag[x] = (diag[x] + root[x] * total - CENTRE) * (2.0 / HALF_WIDTH)

    sweep(None, 1, wide - 1, put_diag)

    level = lanes_of((NRHS, LANES)) // NRHS
    depth = LANES // NRHS
    folded = [None] * (2 * S + 1)

    def note(n, block):
        if n in (0, 1, 2 * S):
            block = 0.5 * (block + block.T)
        f = block[0:NRHS]
        for z in range(1, depth):
            f = jnp.where(level == z, block[z * NRHS : (z + 1) * NRHS], f)
        folded[n] = f

    frames = [f0, f1, f2]
    old = None
    for j in range(S + 1):
        now = frames[j % 3]
        if j > 0:
            src, prev = frames[(j - 1) % 3], frames[(j - 2) % 3]

            def put(x, total):
                new = diag[x] * src[x] - (2.0 / HALF_WIDTH) * root[x] * total
                now[x] = 0.5 * new if j == 1 else new - prev[x]

            sweep(src, j, wide - j, put)
        own = now[DEEP : DEEP + nx, DEEP : DEEP + ny, :]
        high, low = halves(own.reshape(nx * ny, LANES))
        rough[:, j * LANES : (j + 1) * LANES] = high
        fine[:, j * LANES : (j + 1) * LANES] = low
        turned = high.T
        both = jnp.concatenate([high, low], axis=1)
        left = turned if j == 0 else jnp.concatenate([turned, old[0]], axis=0)
        got = jnp.dot(left, both, preferred_element_type=jnp.float32)
        note(2 * j, got[:LANES, :LANES] + 2.0 * got[:LANES, LANES:])
        if j > 0:
            rest = jnp.dot(turned, old[1], preferred_element_type=jnp.float32)
            note(2 * j - 1, got[LANES:, :LANES] + got[LANES:, LANES:] + rest)
        old = (turned, low)
    every = jnp.concatenate(folded, axis=0)
    shift = LANES // 2
    while shift >= NRHS:
        every = every + pltpu.roll(every, shift, 1)
        shift //= 2
    blocks = [every[n * NRHS : (n + 1) * NRHS] for n in range(2 * S + 1)]
    tile = jnp.zeros((NRHS, LANES), jnp.float32)
    row, col = rows_at((NRHS, LANES)), lanes_of((NRHS, LANES)) % NRHS
    last = blocks[2 * S]
    below = jnp.where(row == col + 1, pltpu.roll(last, 1, 0), 0.0)
    below = jnp.where((row == NRHS - 1) & (col == 0), pltpu.roll(last, 1, 1), below)
    blocks[0] = jnp.where(row <= col, blocks[0], last)
    blocks[1] = jnp.where(row <= col, blocks[1], below)
    for n in range(2 * S):
        tile = jnp.where(level == n, blocks[n], tile)
    moments[...] = jnp.broadcast_to(tile[None], moments.shape)


def moment_blocks(tile):
    depth = LANES // NRHS
    row, lane = rows_at((NRHS, LANES)), lanes_of((NRHS, LANES))
    raw = [tile] + [pltpu.roll(tile, LANES - NRHS * n, 1) for n in range(1, depth)]
    square = jnp.concatenate([tile, jnp.zeros((LANES - NRHS, LANES), jnp.float32)], axis=0).T
    turned = [square[n * NRHS : (n + 1) * NRHS] for n in range(depth)]
    first, second = raw[0], raw[1]
    last = jnp.where(row > lane, first, turned[0])
    last = jnp.where(row == lane, pltpu.roll(second, NRHS - 1, 0), last)
    last = jnp.where((row == NRHS - 1) & (lane == NRHS - 1), pltpu.roll(second, NRHS - 1, 1), last)
    even = [0.5 * (r + t) for r, t in zip(raw, turned)] + [last]
    even[0] = jnp.where(row <= lane, first, turned[0])
    even[1] = jnp.where(row <= lane, second, turned[1])
    even = [jnp.where(lane < NRHS, e, 0.0) for e in even]
    return even[:2] + [2.0 * even[n] - even[n % 2] for n in range(2, 2 * S + 1)]


def solve_small(m):
    lane = lanes_of((NRHS, LANES))
    half = HALF_WIDTH / 2
    size = S * NRHS

    def a_on(seq, n):
        return CENTRE * seq[n] + half * (seq[n + 1] + seq[abs(n - 1)])

    nu = [a_on(m, n) for n in range(2 * S)]
    mu = [a_on(nu, n) for n in range(2 * S - 1)]
    up = functools.reduce(jnp.add, [mu[n] if n == 0 else pltpu.roll(mu[n], NRHS * n, 1) for n in range(2 * S - 1)])
    around = functools.reduce(
        jnp.add,
        [mu[abs(n - (S - 1))] if n == 0 else pltpu.roll(mu[abs(n - (S - 1))], NRHS * n, 1) for n in range(2 * S - 1)],
    )

    def left(f, places):
        return f if places == 0 else pltpu.roll(f, LANES - places, 1)

    rows = []
    for c in range(S):
        both = 0.5 * (left(up, NRHS * c) + left(around, NRHS * (S - 1 - c)))
        rows.append(jnp.where(lane < size, both, pltpu.roll(nu[c], size, 1)))
    m = jnp.concatenate(rows, axis=0)
    row, col = rows_at((size, LANES)), lanes_of((size, LANES))
    on = row == col
    kept = jnp.where(on, m, 0.0)
    scale = 1.0 / jnp.sqrt(jnp.sum(kept, axis=1, keepdims=True))
    across = jnp.sum(kept, axis=0, keepdims=True)
    across = jnp.where(lanes_of((1, LANES)) < size, 1.0 / jnp.sqrt(across), 1.0)
    m = scale * m * across + jnp.where(on, RIDGE, 0.0)
    for first in range(0, size, PANEL):
        columns = [
            jnp.broadcast_to(m[:, i : i + 1], m.shape) for i in range(first, first + PANEL)
        ]
        for p in range(0, PANEL, 2):
            i = first + p
            c0, c1 = columns[p], columns[p + 1]
            a, b, d = c0[i : i + 1], c1[i : i + 1], c1[i + 1 : i + 2]
            inverse = 1.0 / (a * d - b * b)
            a, b, d = inverse * a, inverse * b, inverse * d
            d0 = jnp.where(row == i, c0 - 1.0, c0)
            d1 = jnp.where(row == i + 1, c1 - 1.0, c1)
            for later in range(p + 2, PANEL):
                r0 = c0[first + later : first + later + 1]
                r1 = c1[first + later : first + later + 1]
                columns[later] = columns[later] - d0 * (d * r0 - b * r1) - d1 * (a * r1 - b * r0)
            r0, r1 = m[i : i + 1], m[i + 1 : i + 2]
            m = m - d0 * (d * r0 - b * r1) - d1 * (a * r1 - b * r0)
    x = jnp.where((col >= size) & (col < size + NRHS), scale * m, 0.0)
    shift = NRHS
    while shift < LANES:
        x = x + pltpu.roll(x, shift, 1)
        shift *= 2
    c = [x[j * NRHS : (j + 1) * NRHS] for j in range(S)]
    unit = jnp.where(rows_at((NRHS, LANES)) == lane % NRHS, 1.0, 0.0)
    remain = []
    for j in range(S + 1):
        total = CENTRE * c[j] if j < S else 0.0
        if j > 0:
            total = total + (HALF_WIDTH if j == 1 else half) * c[j - 1]
        if j + 1 < S:
            total = total + half * c[j + 1]
        remain.append((unit if j == 0 else 0.0) - total)
    return c, remain


def combine_kernel(guess, rough, fine, parts, update, rest, wh, wl):
    nx, ny, _ = guess.shape
    level = lanes_of((NRHS, LANES)) // NRHS
    coeffs, remain = solve_small(moment_blocks(jnp.sum(parts[...], axis=0)))
    coeffs = coeffs + [jnp.zeros((NRHS, LANES), jnp.float32)]
    for part, tiles in ((0, coeffs), (1, remain)):
        for j in range(S + 1):
            full = jnp.concatenate(
                [jnp.where(level == z, tiles[j], 0.0) for z in range(LANES // NRHS)], axis=0
            )
            high, low = halves(full)
            wh[j * LANES : (j + 1) * LANES, part * LANES : (part + 1) * LANES] = high
            wl[j * LANES : (j + 1) * LANES, part * LANES : (part + 1) * LANES] = low
    chunk = nx // 4
    for i in range(4):
        at = slice(i * chunk, (i + 1) * chunk)
        cells = slice(i * chunk * ny, (i + 1) * chunk * ny)
        dot = functools.partial(jnp.dot, preferred_element_type=jnp.float32)
        out = dot(rough[cells], wh[...]) + dot(rough[cells], wl[...]) + dot(fine[cells], wh[...])
        out = out.reshape(chunk, ny, 2 * LANES)
        update[at] = guess[at] + out[:, :, :LANES]
        rest[at] = out[:, :, LANES:]


def call(kernel, ins, outs, scratch=(), scalars=0, kinds=None, space=pltpu.VMEM):
    specs = [pl.BlockSpec(memory_space=pltpu.SMEM)] * scalars
    specs += [pl.BlockSpec(memory_space=space)] * (len(ins) - scalars)
    result = pl.pallas_call(
        kernel,
        out_shape=[
            jax.ShapeDtypeStruct(s, k) for s, k in zip(outs, kinds or [jnp.float32] * len(outs))
        ],
        in_specs=specs,
        out_specs=[pl.BlockSpec(memory_space=pltpu.VMEM)] * len(outs),
        scratch_shapes=list(scratch),
        compiler_params=pltpu.CompilerParams(vmem_limit_bytes=VMEM_BYTES),
    )(*ins)
    return result


def exchange(first, second, axis):
    count = lax.axis_size(axis)
    got = []
    for cells, start in ((first, 0), (second, 1)):
        links = []
        for i in range(start, count - 1, 2):
            links += [(i, i + 1), (i + 1, i)]
        got.append(lax.ppermute(cells, axis, links))
    return got


def total_of(x, axis):
    count = lax.axis_size(axis)
    if count & (count - 1):
        return lax.psum(x, axis)
    step = 1
    while step < count:
        x = x + lax.ppermute(x, axis, [(i, i ^ step) for i in range(count)])
        step *= 2
    return x


def totals(parts):
    count = parts.shape[0]
    if count > 1:
        return lax.all_to_all(parts, ("gx", "gy"), 0, 0)
    return total_of(total_of(parts, "gy"), "gx")


def body(initial_guess, source, leaf_density, absorption):
    nx, ny, lanes = initial_guess.shape
    leaf = jnp.transpose(leaf_density, (1, 2, 0))
    absorb = jnp.transpose(absorption, (1, 2, 0))
    depth = leaf.shape[1]
    px = lax.rem(lax.axis_index("gx"), 2).astype(jnp.int32).reshape(1)
    py = lax.rem(lax.axis_index("gy"), 2).astype(jnp.int32).reshape(1)
    wide = nx + 2 * DEEP
    tall = ny + 2 * DEEP
    block = (nx, ny, lanes)
    across = ny * depth
    x_rows = DEEP * ny + ny + 2 * DEEP + 8 + 2 * DEEP * (across // lanes)
    y_rows = wide * DEEP + wide + 8 + 2 * wide
    sides = ((2, nx, lanes), (2, ny, lanes))
    root, absb, b0, edge, face, xa, xb = call(
        begin_kernel,
        (px, initial_guess, source, leaf, absorb),
        ((nx, across), (nx, across), block, *sides, (x_rows, lanes), (x_rows, lanes)),
        scratch=[
            pltpu.VMEM(block, jnp.float32),
            pltpu.VMEM(block, jnp.float32),
            pltpu.VMEM(leaf.shape, jnp.float32),
            pltpu.VMEM(leaf.shape, jnp.float32),
            pltpu.VMEM(block, jnp.float32),
            pltpu.VMEM(block, jnp.float32),
            pltpu.SemaphoreType.DMA((4,)),
        ],
        scalars=1,
        space=pltpu.HBM,
    )
    xa, xb = exchange(xa, xb, "gx")
    broad = (wide, ny, lanes)
    rootx, absx, b0x, edge, ya, yb = call(
        widen_kernel,
        (px, py, xa, xb, edge, face, root, absb, b0),
        ((wide, across), (wide, across), broad, (2, wide + 8, lanes), (y_rows, lanes), (y_rows, lanes)),
        scratch=[pltpu.VMEM((2, ny, lanes), jnp.float32)],
        scalars=2,
    )
    ya, yb = exchange(ya, yb, "gy")
    frame = pltpu.VMEM((wide, tall, lanes), jnp.float32)
    count = lax.axis_size("gx") * lax.axis_size("gy")
    count = count if count <= 64 else 1
    cells = nx * ny
    rough, fine, moments = call(
        basis_kernel,
        (py, ya, yb, rootx, absx, b0x, edge),
        ((cells, (S + 1) * lanes), (cells, (S + 1) * lanes), (count, NRHS, lanes)),
        scratch=[frame, frame, pltpu.VMEM((2, wide + 8, lanes), jnp.float32), frame, frame, frame],
        scalars=1,
        kinds=(jnp.bfloat16, jnp.bfloat16, jnp.float32),
    )
    return call(
        combine_kernel,
        (initial_guess, rough, fine, totals(moments)),
        (block, block),
        scratch=[pltpu.VMEM(((S + 1) * lanes, 2 * lanes), jnp.bfloat16)] * 2,
    )


def solution(mesh):
    spec = P("gx", "gy", None)
    return jax.shard_map(
        lambda *arrays: tuple(body(*arrays)),
        mesh=mesh,
        in_specs=(spec,) * 4,
        out_specs=(spec, spec),
        check_vma=False,
    )
```

```python
import functools

import jax
import jax.numpy as jnp
from jax import lax
from jax.experimental import pallas as pl
from jax.experimental.pallas import tpu as pltpu
from jax.sharding import PartitionSpec as P

NRHS = 8
S = 8
DEEP = S
LANES = 128

PEAK_COND = 0.6
CENTRE = 10.3
HALF_WIDTH = 9.8
RIDGE = 0.05
PANEL = 16
VMEM_BYTES = 48 * 1024 * 1024
BEGIN_BYTES = 55000 * 1024


def lanes_of(shape):
    return lax.broadcasted_iota(jnp.int32, shape, len(shape) - 1)


def rows_at(shape):
    return lax.broadcasted_iota(jnp.int32, shape, len(shape) - 2)


def z_sum(f):
    lane = lanes_of(f.shape)
    ax = f.ndim - 1
    up = jnp.where(lane >= NRHS, pltpu.roll(f, NRHS, ax), 0.0)
    down = jnp.where(lane < LANES - NRHS, pltpu.roll(f, LANES - NRHS, ax), 0.0)
    return up + down


def row_sum(f):
    n = f.shape[-2]
    ax = f.ndim - 2
    return pltpu.roll(f, 1, ax) + pltpu.roll(f, n - 1, ax)


def row_sum_zero(f):
    n = f.shape[-2]
    ax = f.ndim - 2
    row = rows_at(f.shape)
    up = jnp.where(row >= 1, pltpu.roll(f, 1, ax), 0.0)
    down = jnp.where(row < n - 1, pltpu.roll(f, n - 1, ax), 0.0)
    return up + down


def slab_sum(before, here, after, rows):
    ux = before[0] + after[0]
    px = before[1] + after[1]
    s = here[1] + ux
    q = here[0] + 0.5 * s + (1.0 / 3.0) * px
    return s + 0.5 * px + rows(q)


def cross_sum(f, rows):
    p = z_sum(f)
    return f + 0.5 * p + rows(0.5 * f + (1.0 / 3.0) * p)


def spread(rows):
    n = rows.shape[0]
    depth = LANES // NRHS
    at = rows_at((NRHS, LANES)) * depth + lanes_of((NRHS, LANES)) // NRHS
    out = []
    for x in range(n):
        line = jnp.broadcast_to(rows[x : x + 1], (NRHS, LANES))
        out.append(jnp.take_along_axis(line, at, axis=1))
    return jnp.stack(out)


def begin_kernel(px, py, *refs):
    far, refs = refs[:4], refs[4:]
    (root_o, abs_o, b0_o, edge_o, face_o, send_a, send_b, side_a, side_b), refs = refs[:9], refs[9:]
    guess, source, leaf, absorb, root, absb, sems = refs
    copies = [
        pltpu.make_async_copy(there, here, sems.at[i])
        for i, (there, here) in enumerate(zip(far, (guess, source, leaf, absorb)))
    ]
    for i in (2, 3, 0, 1):
        copies[i].start()
    nx, ny, _ = guess.shape
    depth = leaf.shape[1]
    copies[2].wait()
    copies[3].wait()
    turned = jnp.transpose(leaf[...].reshape(ny * depth, nx))
    root_o[...] = jnp.sqrt(PEAK_COND / (1.0 + turned))
    abs_o[...] = jnp.transpose(absorb[...].reshape(ny * depth, nx))
    for part, wide in ((root_o, root), (abs_o, absb)):
        for y in range(0, ny, NRHS):
            wide[:, y : y + NRHS, :] = spread(part[:, y * depth : (y + NRHS) * depth])
    copies[0].wait()
    copies[1].wait()
    for at, col, face in ((0, 0, 0), (1, ny - 1, nx - 1)):
        edge_o[at] = guess[:, col, :]
        face_o[at] = guess[face]
    zero = jnp.zeros((ny, LANES), jnp.float32)

    def pair(x, field):
        if x < 0 or x >= nx:
            return (zero, zero)
        u = root[x] if field is None else root[x] * field[x]
        return (u, z_sum(u))

    moving = [pair(-1, guess), pair(0, guess)]
    still = [pair(-1, None), pair(0, None)]
    for x in range(nx):
        moving.append(pair(x + 1, guess))
        still.append(pair(x + 1, None))
        wu = slab_sum(*moving, row_sum_zero)
        wr = slab_sum(*still, row_sum_zero)
        moving, still = moving[1:], still[1:]
        v = guess[x]
        b0_o[x] = source[x] - absb[x] * v + root[x] * (wu - v * wr)

    def write(out, x0, face, beyond):
        n = DEEP * ny
        out[0:n] = b0_o[x0 : x0 + DEEP].reshape(n, LANES)
        out[n : n + ny] = guess[face]
        n += ny
        for col in (0, ny - 1):
            out[n : n + DEEP] = guess[x0 : x0 + DEEP, col, :]
            n += DEEP
        out[n : n + 8] = jnp.zeros((8, LANES), jnp.float32)
        for at, col in ((0, 0), (1, ny - 1)):
            out[n + at : n + at + 1] = guess[beyond, col : col + 1, :]
            out[n + 2 + at : n + 3 + at] = root[beyond, col : col + 1, :]
        n += 8
        for part in (root_o, abs_o):
            for first in range(0, ny * depth, LANES):
                out[n : n + DEEP] = part[x0 : x0 + DEEP, first : first + LANES]
                n += DEEP

    @pl.when(px[0] == 0)
    def _():
        write(send_a, nx - DEEP, nx - 1, nx - DEEP - 1)
        write(send_b, 0, 0, DEEP)

    @pl.when(px[0] == 1)
    def _():
        write(send_b, nx - DEEP, nx - 1, nx - DEEP - 1)
        write(send_a, 0, 0, DEEP)

    def write_side(out, y0, at):
        n = (nx - 2) * DEEP
        out[0:n] = b0_o[1 : nx - 1, y0 : y0 + DEEP, :].reshape(n, LANES)
        out[n : n + nx] = edge_o[at]
        n += nx
        for part in (root_o, abs_o):
            out[n : n + nx] = part[:, y0 * depth : (y0 + DEEP) * depth]
            n += nx

    @pl.when(py[0] == 0)
    def _():
        write_side(side_a, ny - DEEP, 1)
        write_side(side_b, 0, 0)

    @pl.when(py[0] == 1)
    def _():
        write_side(side_b, ny - DEEP, 1)
        write_side(side_a, 0, 0)


def widen_kernel(
    px, py, recv_a, recv_b, edge_own, face_own, root, absb, b0,
    rootx, absx, b0x, edge, send_a, send_b, face
):
    nx, ny, _ = b0.shape
    wide = nx + 2 * DEEP
    rootx[DEEP : DEEP + nx] = root[...]
    absx[DEEP : DEEP + nx] = absb[...]
    b0x[DEEP : DEEP + nx] = b0[...]
    for at in (0, 1):
        edge[at, DEEP : DEEP + nx] = edge_own[at]
        edge[at, wide : wide + 8] = jnp.zeros((8, LANES), jnp.float32)

    def read(msg, x0, side):
        n = DEEP * ny
        b0x[x0 : x0 + DEEP] = msg[0:n].reshape(DEEP, ny, LANES)
        face[side] = msg[n : n + ny]
        n += ny
        for at in (0, 1):
            edge[at, x0 : x0 + DEEP] = msg[n : n + DEEP]
            n += DEEP
        for at in (0, 1):
            edge[at, wide + side : wide + side + 1] = msg[n + at : n + at + 1]
            edge[at, wide + 2 + side : wide + 3 + side] = msg[n + 2 + at : n + 3 + at]
        n += 8
        for out in (rootx, absx):
            for first in range(0, out.shape[1], LANES):
                out[x0 : x0 + DEEP, first : first + LANES] = msg[n : n + DEEP]
                n += DEEP

    @pl.when(px[0] == 0)
    def _():
        read(recv_b, 0, 0)
        read(recv_a, DEEP + nx, 1)

    @pl.when(px[0] == 1)
    def _():
        read(recv_a, 0, 0)
        read(recv_b, DEEP + nx, 1)

    def root_line(x):
        parts = [
            spread(rootx[x : x + 1, first : first + LANES])
            for first in range(0, rootx.shape[1], LANES)
        ]
        return jnp.concatenate(parts, axis=1)[0]

    for side, out_x, in_x in ((0, DEEP - 1, DEEP), (1, DEEP + nx, DEEP + nx - 1)):
        va, ra = face[side], root_line(out_x)
        vb, rb = face_own[side], root_line(in_x)
        fix_a = ra * (cross_sum(rb * vb, row_sum_zero) - va * cross_sum(rb, row_sum_zero))
        fix_b = rb * (cross_sum(ra * va, row_sum_zero) - vb * cross_sum(ra, row_sum_zero))
        b0x[out_x] = b0x[out_x] + fix_a
        b0x[in_x] = b0x[in_x] + fix_b

    def write(out, y0, at):
        n = 0
        for x0 in (0, DEEP + nx - 1):
            m = (DEEP + 1) * DEEP
            out[n : n + m] = b0x[x0 : x0 + DEEP + 1, y0 : y0 + DEEP, :].reshape(m, LANES)
            n += m
        first = y0 * (LANES // NRHS)
        for x0 in (0, DEEP + nx):
            out[n : n + DEEP] = edge[at, x0 : x0 + DEEP]
            n += DEEP
            for part in (rootx, absx):
                out[n : n + DEEP] = part[x0 : x0 + DEEP, first : first + LANES]
                n += DEEP
        out[n : n + 8] = edge[at, wide : wide + 8]

    @pl.when(py[0] == 0)
    def _():
        write(send_a, ny - DEEP, 1)
        write(send_b, 0, 0)

    @pl.when(py[0] == 1)
    def _():
        write(send_b, ny - DEEP, 1)
        write(send_a, 0, 0)


def halves(a):
    high = a.astype(jnp.bfloat16)
    return high, (a - high.astype(jnp.float32)).astype(jnp.bfloat16)


def basis_kernel(
    py, side_a, side_b, recv_a, recv_b, rootx, absx, b0x, edge,
    rough, fine, moments, root, diag, far, f0, f1, f2
):
    wide, ny, _ = b0x.shape
    nx = wide - 2 * DEEP
    tall = ny + 2 * DEEP
    depth = LANES // NRHS
    for part, out in ((rootx, root), (absx, diag)):
        for y in range(0, ny, DEEP):
            first = y * depth
            out[:, DEEP + y : 2 * DEEP + y, :] = spread(part[:, first : first + LANES])
    f0[:, DEEP : DEEP + ny, :] = b0x[...]

    def read(inner, outer, y0, side):
        n = (nx - 2) * DEEP
        f0[DEEP + 1 : DEEP + nx - 1, y0 : y0 + DEEP, :] = inner[0:n].reshape(nx - 2, DEEP, LANES)
        far[side, DEEP : DEEP + nx] = inner[n : n + nx]
        n += nx
        for out in (root, diag):
            out[DEEP : DEEP + nx, y0 : y0 + DEEP, :] = spread(inner[n : n + nx])
            n += nx
        n = 0
        for x0 in (0, DEEP + nx - 1):
            m = (DEEP + 1) * DEEP
            f0[x0 : x0 + DEEP + 1, y0 : y0 + DEEP, :] = outer[n : n + m].reshape(
                DEEP + 1, DEEP, LANES
            )
            n += m
        for x0 in (0, DEEP + nx):
            far[side, x0 : x0 + DEEP] = outer[n : n + DEEP]
            n += DEEP
            for out in (root, diag):
                out[x0 : x0 + DEEP, y0 : y0 + DEEP, :] = spread(outer[n : n + DEEP])
                n += DEEP
        far[side, wide : wide + 8] = outer[n : n + 8]

    @pl.when(py[0] == 0)
    def _():
        read(side_b, recv_b, 0, 0)
        read(side_a, recv_a, DEEP + ny, 1)

    @pl.when(py[0] == 1)
    def _():
        read(side_a, recv_a, 0, 0)
        read(side_b, recv_b, DEEP + ny, 1)

    row = lax.broadcasted_iota(jnp.int32, (wide, LANES), 0)

    def across(f, before, after):
        p = z_sum(f)
        ends = jnp.concatenate([before, after], axis=0)
        ends = 0.5 * ends + (1.0 / 3.0) * z_sum(ends)
        g = 0.5 * f + (1.0 / 3.0) * p
        up = jnp.where(row == 0, ends[0:1], pltpu.roll(g, 1, 0))
        down = jnp.where(row == wide - 1, ends[1:2], pltpu.roll(g, wide - 1, 0))
        return f + 0.5 * p + up + down

    def column(ref, at, y):
        v = ref[at, 0:wide]
        ends = ref[at, wide : wide + 8]
        r = root[:, y, :]
        r0, r1 = ends[2:3], ends[3:4]
        return v, r, across(r * v, r0 * ends[0:1], r1 * ends[1:2]), across(r, r0, r1)

    for side, out_y, in_y in ((0, DEEP - 1, DEEP), (1, DEEP + ny, DEEP + ny - 1)):
        va, ra, ua, wa = column(far, side, out_y)
        vb, rb, ub, wb = column(edge, side, in_y)
        f0[:, out_y, :] = f0[:, out_y, :] + ra * (ub - va * wb)
        f0[:, in_y, :] = f0[:, in_y, :] + rb * (ua - vb * wa)

    def pair(src, x):
        u = root[x] if src is None else root[x] * src[x]
        return (u, z_sum(u))

    def sweep(src, lo, hi, put):
        first, second = pair(src, lo - 1), pair(src, lo)
        for x in range(lo, hi):
            third = pair(src, x + 1)
            put(x, slab_sum(first, second, third, row_sum))
            first, second = second, third

    def put_diag(x, total):
        diag[x] = (diag[x] + root[x] * total - CENTRE) * (2.0 / HALF_WIDTH)

    sweep(None, 1, wide - 1, put_diag)

    level = lanes_of((NRHS, LANES)) // NRHS
    depth = LANES // NRHS
    folded = [None] * (2 * S + 1)

    def note(n, block):
        if n in (0, 1, 2 * S):
            block = 0.5 * (block + block.T)
        f = block[0:NRHS]
        for z in range(1, depth):
            f = jnp.where(level == z, block[z * NRHS : (z + 1) * NRHS], f)
        folded[n] = f

    frames = [f0, f1, f2]
    old = None
    for j in range(S + 1):
        now = frames[j % 3]
        if j > 0:
            src, prev = frames[(j - 1) % 3], frames[(j - 2) % 3]

            def put(x, total):
                new = diag[x] * src[x] - (2.0 / HALF_WIDTH) * root[x] * total
                now[x] = 0.5 * new if j == 1 else new - prev[x]

            sweep(src, j, wide - j, put)
        own = now[DEEP : DEEP + nx, DEEP : DEEP + ny, :]
        high, low = halves(own.reshape(nx * ny, LANES))
        rough[:, j * LANES : (j + 1) * LANES] = high
        fine[:, j * LANES : (j + 1) * LANES] = low
        turned = high.T
        both = jnp.concatenate([high, low], axis=1)
        left = turned if j == 0 else jnp.concatenate([turned, old[0]], axis=0)
        got = jnp.dot(left, both, preferred_element_type=jnp.float32)
        note(2 * j, got[:LANES, :LANES] + 2.0 * got[:LANES, LANES:])
        if j > 0:
            rest = jnp.dot(turned, old[1], preferred_element_type=jnp.float32)
            note(2 * j - 1, got[LANES:, :LANES] + got[LANES:, LANES:] + rest)
        old = (turned, low)
    every = jnp.concatenate(folded, axis=0)
    shift = LANES // 2
    while shift >= NRHS:
        every = every + pltpu.roll(every, shift, 1)
        shift //= 2
    blocks = [every[n * NRHS : (n + 1) * NRHS] for n in range(2 * S + 1)]
    tile = jnp.zeros((NRHS, LANES), jnp.float32)
    row, col = rows_at((NRHS, LANES)), lanes_of((NRHS, LANES)) % NRHS
    last = blocks[2 * S]
    below = jnp.where(row == col + 1, pltpu.roll(last, 1, 0), 0.0)
    below = jnp.where((row == NRHS - 1) & (col == 0), pltpu.roll(last, 1, 1), below)
    blocks[0] = jnp.where(row <= col, blocks[0], last)
    blocks[1] = jnp.where(row <= col, blocks[1], below)
    for n in range(2 * S):
        tile = jnp.where(level == n, blocks[n], tile)
    moments[...] = jnp.broadcast_to(tile[None], moments.shape)


def moment_blocks(tile):
    depth = LANES // NRHS
    row, lane = rows_at((NRHS, LANES)), lanes_of((NRHS, LANES))
    raw = [tile] + [pltpu.roll(tile, LANES - NRHS * n, 1) for n in range(1, depth)]
    square = jnp.concatenate([tile, jnp.zeros((LANES - NRHS, LANES), jnp.float32)], axis=0).T
    turned = [square[n * NRHS : (n + 1) * NRHS] for n in range(depth)]
    first, second = raw[0], raw[1]
    last = jnp.where(row > lane, first, turned[0])
    last = jnp.where(row == lane, pltpu.roll(second, NRHS - 1, 0), last)
    last = jnp.where((row == NRHS - 1) & (lane == NRHS - 1), pltpu.roll(second, NRHS - 1, 1), last)
    even = [0.5 * (r + t) for r, t in zip(raw, turned)] + [last]
    even[0] = jnp.where(row <= lane, first, turned[0])
    even[1] = jnp.where(row <= lane, second, turned[1])
    even = [jnp.where(lane < NRHS, e, 0.0) for e in even]
    return even[:2] + [2.0 * even[n] - even[n % 2] for n in range(2, 2 * S + 1)]


def solve_small(m):
    lane = lanes_of((NRHS, LANES))
    half = HALF_WIDTH / 2
    size = S * NRHS

    def a_on(seq, n):
        return CENTRE * seq[n] + half * (seq[n + 1] + seq[abs(n - 1)])

    nu = [a_on(m, n) for n in range(2 * S)]
    mu = [a_on(nu, n) for n in range(2 * S - 1)]
    up = functools.reduce(jnp.add, [mu[n] if n == 0 else pltpu.roll(mu[n], NRHS * n, 1) for n in range(2 * S - 1)])
    around = functools.reduce(
        jnp.add,
        [mu[abs(n - (S - 1))] if n == 0 else pltpu.roll(mu[abs(n - (S - 1))], NRHS * n, 1) for n in range(2 * S - 1)],
    )

    def left(f, places):
        return f if places == 0 else pltpu.roll(f, LANES - places, 1)

    rows = []
    for c in range(S):
        both = 0.5 * (left(up, NRHS * c) + left(around, NRHS * (S - 1 - c)))
        rows.append(jnp.where(lane < size, both, pltpu.roll(nu[c], size, 1)))
    m = jnp.concatenate(rows, axis=0)
    row, col = rows_at((size, LANES)), lanes_of((size, LANES))
    on = row == col
    kept = jnp.where(on, m, 0.0)
    scale = 1.0 / jnp.sqrt(jnp.sum(kept, axis=1, keepdims=True))
    across = jnp.sum(kept, axis=0, keepdims=True)
    across = jnp.where(lanes_of((1, LANES)) < size, 1.0 / jnp.sqrt(across), 1.0)
    m = scale * m * across + jnp.where(on, RIDGE, 0.0)
    for first in range(0, size, PANEL):
        columns = [
            jnp.broadcast_to(m[:, i : i + 1], m.shape) for i in range(first, first + PANEL)
        ]
        for p in range(0, PANEL, 2):
            i = first + p
            c0, c1 = columns[p], columns[p + 1]
            a, b, d = c0[i : i + 1], c1[i : i + 1], c1[i + 1 : i + 2]
            inverse = 1.0 / (a * d - b * b)
            a, b, d = inverse * a, inverse * b, inverse * d
            d0 = jnp.where(row == i, c0 - 1.0, c0)
            d1 = jnp.where(row == i + 1, c1 - 1.0, c1)
            for later in range(p + 2, PANEL):
                r0 = c0[first + later : first + later + 1]
                r1 = c1[first + later : first + later + 1]
                columns[later] = columns[later] - d0 * (d * r0 - b * r1) - d1 * (a * r1 - b * r0)
            r0, r1 = m[i : i + 1], m[i + 1 : i + 2]
            m = m - d0 * (d * r0 - b * r1) - d1 * (a * r1 - b * r0)
    x = jnp.where((col >= size) & (col < size + NRHS), scale * m, 0.0)
    shift = NRHS
    while shift < LANES:
        x = x + pltpu.roll(x, shift, 1)
        shift *= 2
    c = [x[j * NRHS : (j + 1) * NRHS] for j in range(S)]
    unit = jnp.where(rows_at((NRHS, LANES)) == lane % NRHS, 1.0, 0.0)
    remain = []
    for j in range(S + 1):
        total = CENTRE * c[j] if j < S else 0.0
        if j > 0:
            total = total + (HALF_WIDTH if j == 1 else half) * c[j - 1]
        if j + 1 < S:
            total = total + half * c[j + 1]
        remain.append((unit if j == 0 else 0.0) - total)
    return c, remain


def combine_kernel(guess, rough, fine, parts, update, rest, wh, wl):
    nx, ny, _ = guess.shape
    level = lanes_of((NRHS, LANES)) // NRHS
    coeffs, remain = solve_small(moment_blocks(jnp.sum(parts[...], axis=0)))
    coeffs = coeffs + [jnp.zeros((NRHS, LANES), jnp.float32)]
    for part, tiles in ((0, coeffs), (1, remain)):
        for j in range(S + 1):
            full = jnp.concatenate(
                [jnp.where(level == z, tiles[j], 0.0) for z in range(LANES // NRHS)], axis=0
            )
            high, low = halves(full)
            wh[j * LANES : (j + 1) * LANES, part * LANES : (part + 1) * LANES] = high
            wl[j * LANES : (j + 1) * LANES, part * LANES : (part + 1) * LANES] = low
    chunk = nx // 4
    for i in range(4):
        at = slice(i * chunk, (i + 1) * chunk)
        cells = slice(i * chunk * ny, (i + 1) * chunk * ny)
        dot = functools.partial(jnp.dot, preferred_element_type=jnp.float32)
        out = dot(rough[cells], wh[...]) + dot(rough[cells], wl[...]) + dot(fine[cells], wh[...])
        out = out.reshape(chunk, ny, 2 * LANES)
        update[at] = guess[at] + out[:, :, :LANES]
        rest[at] = out[:, :, LANES:]


def call(kernel, ins, outs, scratch=(), scalars=0, kinds=None, space=pltpu.VMEM, limit=VMEM_BYTES):
    specs = [pl.BlockSpec(memory_space=pltpu.SMEM)] * scalars
    specs += [pl.BlockSpec(memory_space=space)] * (len(ins) - scalars)
    result = pl.pallas_call(
        kernel,
        out_shape=[
            jax.ShapeDtypeStruct(s, k) for s, k in zip(outs, kinds or [jnp.float32] * len(outs))
        ],
        in_specs=specs,
        out_specs=[pl.BlockSpec(memory_space=pltpu.VMEM)] * len(outs),
        scratch_shapes=list(scratch),
        compiler_params=pltpu.CompilerParams(vmem_limit_bytes=limit),
    )(*ins)
    return result


def exchange(first, second, axis):
    count = lax.axis_size(axis)
    got = []
    for cells, start in ((first, 0), (second, 1)):
        links = []
        for i in range(start, count - 1, 2):
            links += [(i, i + 1), (i + 1, i)]
        got.append(lax.ppermute(cells, axis, links))
    return got


def total_of(x, axis):
    count = lax.axis_size(axis)
    if count & (count - 1):
        return lax.psum(x, axis)
    step = 1
    while step < count:
        x = x + lax.ppermute(x, axis, [(i, i ^ step) for i in range(count)])
        step *= 2
    return x


def totals(parts):
    count = parts.shape[0]
    if count > 1:
        return lax.all_to_all(parts, ("gx", "gy"), 0, 0)
    return total_of(total_of(parts, "gy"), "gx")


def body(initial_guess, source, leaf_density, absorption):
    nx, ny, lanes = initial_guess.shape
    leaf = jnp.transpose(leaf_density, (1, 2, 0))
    absorb = jnp.transpose(absorption, (1, 2, 0))
    depth = leaf.shape[1]
    px = lax.rem(lax.axis_index("gx"), 2).astype(jnp.int32).reshape(1)
    py = lax.rem(lax.axis_index("gy"), 2).astype(jnp.int32).reshape(1)
    wide = nx + 2 * DEEP
    tall = ny + 2 * DEEP
    block = (nx, ny, lanes)
    across = ny * depth
    x_rows = DEEP * ny + ny + 2 * DEEP + 8 + 2 * DEEP * (across // lanes)
    side_rows = (nx - 2) * DEEP + 3 * nx
    y_rows = 2 * (DEEP + 1) * DEEP + 6 * DEEP + 8
    sides = ((2, nx, lanes), (2, ny, lanes))
    root, absb, b0, edge, face, xa, xb, sa, sb = call(
        begin_kernel,
        (px, py, initial_guess, source, leaf, absorb),
        ((nx, across), (nx, across), block, *sides)
        + ((x_rows, lanes),) * 2
        + ((side_rows, lanes),) * 2,
        scratch=[
            pltpu.VMEM(block, jnp.float32),
            pltpu.VMEM(block, jnp.float32),
            pltpu.VMEM(leaf.shape, jnp.float32),
            pltpu.VMEM(leaf.shape, jnp.float32),
            pltpu.VMEM(block, jnp.float32),
            pltpu.VMEM(block, jnp.float32),
            pltpu.SemaphoreType.DMA((4,)),
        ],
        scalars=2,
        space=pltpu.HBM,
        limit=BEGIN_BYTES,
    )
    xa, xb = exchange(xa, xb, "gx")
    sa, sb = exchange(sa, sb, "gy")
    broad = (wide, ny, lanes)
    rootx, absx, b0x, edge, ya, yb = call(
        widen_kernel,
        (px, py, xa, xb, edge, face, root, absb, b0),
        ((wide, across), (wide, across), broad, (2, wide + 8, lanes), (y_rows, lanes), (y_rows, lanes)),
        scratch=[pltpu.VMEM((2, ny, lanes), jnp.float32)],
        scalars=2,
    )
    ya, yb = exchange(ya, yb, "gy")
    frame = pltpu.VMEM((wide, tall, lanes), jnp.float32)
    count = lax.axis_size("gx") * lax.axis_size("gy")
    count = count if count <= 64 else 1
    cells = nx * ny
    rough, fine, moments = call(
        basis_kernel,
        (py, sa, sb, ya, yb, rootx, absx, b0x, edge),
        ((cells, (S + 1) * lanes), (cells, (S + 1) * lanes), (count, NRHS, lanes)),
        scratch=[frame, frame, pltpu.VMEM((2, wide + 8, lanes), jnp.float32), frame, frame, frame],
        scalars=1,
        kinds=(jnp.bfloat16, jnp.bfloat16, jnp.float32),
    )
    return call(
        combine_kernel,
        (initial_guess, rough, fine, totals(moments)),
        (block, block),
        scratch=[pltpu.VMEM(((S + 1) * lanes, 2 * lanes), jnp.bfloat16)] * 2,
    )


def solution(mesh):
    spec = P("gx", "gy", None)
    return jax.shard_map(
        lambda *arrays: tuple(body(*arrays)),
        mesh=mesh,
        in_specs=(spec,) * 4,
        out_specs=(spec, spec),
        check_vma=False,
    )
```

```python
import functools

import jax
import jax.numpy as jnp
from jax import lax
from jax.experimental import pallas as pl
from jax.experimental.pallas import tpu as pltpu
from jax.sharding import PartitionSpec as P

NRHS = 8
S = 8
DEEP = S
LANES = 128

PEAK_COND = 0.6
CENTRE = 10.3
HALF_WIDTH = 9.8
RIDGE = 0.05
PANEL = 16
VMEM_BYTES = 24 * 1024 * 1024
BEGIN_BYTES = 54300 * 1024


def lanes_of(shape):
    return lax.broadcasted_iota(jnp.int32, shape, len(shape) - 1)


def rows_at(shape):
    return lax.broadcasted_iota(jnp.int32, shape, len(shape) - 2)


def z_sum(f):
    lane = lanes_of(f.shape)
    ax = f.ndim - 1
    up = jnp.where(lane >= NRHS, pltpu.roll(f, NRHS, ax), 0.0)
    down = jnp.where(lane < LANES - NRHS, pltpu.roll(f, LANES - NRHS, ax), 0.0)
    return up + down


def row_sum(f):
    n = f.shape[-2]
    ax = f.ndim - 2
    return pltpu.roll(f, 1, ax) + pltpu.roll(f, n - 1, ax)


def row_sum_zero(f):
    n = f.shape[-2]
    ax = f.ndim - 2
    row = rows_at(f.shape)
    up = jnp.where(row >= 1, pltpu.roll(f, 1, ax), 0.0)
    down = jnp.where(row < n - 1, pltpu.roll(f, n - 1, ax), 0.0)
    return up + down


def slab_sum(before, here, after, rows):
    ux = before[0] + after[0]
    px = before[1] + after[1]
    s = here[1] + ux
    q = here[0] + 0.5 * s + (1.0 / 3.0) * px
    return s + 0.5 * px + rows(q)


def cross_sum(f, rows):
    p = z_sum(f)
    return f + 0.5 * p + rows(0.5 * f + (1.0 / 3.0) * p)


def spread(rows):
    n = rows.shape[0]
    depth = LANES // NRHS
    at = rows_at((NRHS, LANES)) * depth + lanes_of((NRHS, LANES)) // NRHS
    out = []
    for x in range(n):
        line = jnp.broadcast_to(rows[x : x + 1], (NRHS, LANES))
        out.append(jnp.take_along_axis(line, at, axis=1))
    return jnp.stack(out)


def begin_kernel(px, py, *refs):
    far, refs = refs[:3], refs[3:]
    (root_o, abs_o, b0_o, rim_o, edge_o, face_o), refs = refs[:6], refs[6:]
    (send_a, send_b, side_a, side_b), refs = refs[:4], refs[4:]
    guess, source, pair_in, root, absb, sems = refs
    copies = [
        pltpu.make_async_copy(there, here, sems.at[i])
        for i, (there, here) in enumerate(zip(far, (guess, source, pair_in)))
    ]
    for i in (2, 0, 1):
        copies[i].start()
    nx, ny, _ = guess.shape
    depth = pair_in.shape[2]
    copies[2].wait()
    turned = jnp.transpose(pair_in[0].reshape(ny * depth, nx))
    root_o[...] = jnp.sqrt(PEAK_COND / (1.0 + turned))
    abs_o[...] = jnp.transpose(pair_in[1].reshape(ny * depth, nx))
    for part, wide in ((root_o, root), (abs_o, absb)):
        for y in range(0, ny, NRHS):
            wide[:, y : y + NRHS, :] = spread(part[:, y * depth : (y + NRHS) * depth])
    copies[0].wait()
    copies[1].wait()
    for at, col, face in ((0, 0, 0), (1, ny - 1, nx - 1)):
        edge_o[at] = guess[:, col, :]
        face_o[at] = guess[face]
    zero = jnp.zeros((ny, LANES), jnp.float32)

    def pair(x, field):
        if x < 0 or x >= nx:
            return (zero, zero)
        u = root[x] if field is None else root[x] * field[x]
        return (u, z_sum(u))

    moving = [pair(-1, guess), pair(0, guess)]
    still = [pair(-1, None), pair(0, None)]
    for x in range(nx):
        moving.append(pair(x + 1, guess))
        still.append(pair(x + 1, None))
        wu = slab_sum(*moving, row_sum_zero)
        wr = slab_sum(*still, row_sum_zero)
        moving, still = moving[1:], still[1:]
        v = guess[x]
        b0_o[x] = source[x] - absb[x] * v + root[x] * (wu - v * wr)

    rim_o[0] = b0_o[0]
    rim_o[1] = b0_o[nx - 1]

    def write(out, x0, face, beyond):
        n = DEEP * ny
        out[0:n] = b0_o[x0 : x0 + DEEP].reshape(n, LANES)
        out[n : n + ny] = guess[face]
        n += ny
        for col in (0, ny - 1):
            out[n : n + DEEP] = guess[x0 : x0 + DEEP, col, :]
            n += DEEP
        out[n : n + 8] = jnp.zeros((8, LANES), jnp.float32)
        for at, col in ((0, 0), (1, ny - 1)):
            out[n + at : n + at + 1] = guess[beyond, col : col + 1, :]
            out[n + 2 + at : n + 3 + at] = root[beyond, col : col + 1, :]
        n += 8
        for part in (root_o, abs_o):
            for first in range(0, ny * depth, LANES):
                out[n : n + DEEP] = part[x0 : x0 + DEEP, first : first + LANES]
                n += DEEP

    @pl.when(px[0] == 0)
    def _():
        write(send_a, nx - DEEP, nx - 1, nx - DEEP - 1)
        write(send_b, 0, 0, DEEP)

    @pl.when(px[0] == 1)
    def _():
        write(send_b, nx - DEEP, nx - 1, nx - DEEP - 1)
        write(send_a, 0, 0, DEEP)

    def write_side(out, y0, at):
        n = (nx - 2) * DEEP
        out[0:n] = b0_o[1 : nx - 1, y0 : y0 + DEEP, :].reshape(n, LANES)
        out[n : n + nx] = edge_o[at]
        n += nx
        for part in (root_o, abs_o):
            out[n : n + nx] = part[:, y0 * depth : (y0 + DEEP) * depth]
            n += nx

    @pl.when(py[0] == 0)
    def _():
        write_side(side_a, ny - DEEP, 1)
        write_side(side_b, 0, 0)

    @pl.when(py[0] == 1)
    def _():
        write_side(side_b, ny - DEEP, 1)
        write_side(side_a, 0, 0)


def widen_kernel(
    px, py, recv_a, recv_b, edge_own, face_own, root, absb, rim,
    root_h, abs_h, band, edge, send_a, send_b, face
):
    nx, ny = edge_own.shape[1], face_own.shape[1]
    wide = nx + 2 * DEEP
    for at in (0, 1):
        edge[at, DEEP : DEEP + nx] = edge_own[at]
        edge[at, wide : wide + 8] = jnp.zeros((8, LANES), jnp.float32)

    def read(msg, x0, side):
        n = DEEP * ny
        band[side, side : side + DEEP] = msg[0:n].reshape(DEEP, ny, LANES)
        face[side] = msg[n : n + ny]
        n += ny
        for at in (0, 1):
            edge[at, x0 : x0 + DEEP] = msg[n : n + DEEP]
            n += DEEP
        for at in (0, 1):
            edge[at, wide + side : wide + side + 1] = msg[n + at : n + at + 1]
            edge[at, wide + 2 + side : wide + 3 + side] = msg[n + 2 + at : n + 3 + at]
        n += 8
        for out in (root_h, abs_h):
            for first in range(0, out.shape[2], LANES):
                out[side, :, first : first + LANES] = msg[n : n + DEEP]
                n += DEEP

    @pl.when(px[0] == 0)
    def _():
        read(recv_b, 0, 0)
        read(recv_a, DEEP + nx, 1)

    @pl.when(px[0] == 1)
    def _():
        read(recv_a, 0, 0)
        read(recv_b, DEEP + nx, 1)

    def line(rows):
        parts = [spread(rows[:, at : at + LANES]) for at in range(0, rows.shape[1], LANES)]
        return jnp.concatenate(parts, axis=1)[0]

    for side, out_x, in_x, far_x, near_x in (
        (0, DEEP - 1, DEEP, DEEP - 1, 0),
        (1, 1, 0, 0, nx - 1),
    ):
        va, ra = face[side], line(root_h[side, far_x : far_x + 1])
        vb, rb = face_own[side], line(root[near_x : near_x + 1])
        fix_a = ra * (cross_sum(rb * vb, row_sum_zero) - va * cross_sum(rb, row_sum_zero))
        fix_b = rb * (cross_sum(ra * va, row_sum_zero) - vb * cross_sum(ra, row_sum_zero))
        band[side, out_x] = band[side, out_x] + fix_a
        band[side, in_x] = rim[side] + fix_b

    def write(out, y0, at):
        n = 0
        for side in (0, 1):
            m = (DEEP + 1) * DEEP
            out[n : n + m] = band[side, :, y0 : y0 + DEEP, :].reshape(m, LANES)
            n += m
        first = y0 * (LANES // NRHS)
        for side, x0 in ((0, 0), (1, DEEP + nx)):
            out[n : n + DEEP] = edge[at, x0 : x0 + DEEP]
            n += DEEP
            for part in (root_h, abs_h):
                out[n : n + DEEP] = part[side, :, first : first + LANES]
                n += DEEP
        out[n : n + 8] = edge[at, wide : wide + 8]

    @pl.when(py[0] == 0)
    def _():
        write(send_a, ny - DEEP, 1)
        write(send_b, 0, 0)

    @pl.when(py[0] == 1)
    def _():
        write(send_b, ny - DEEP, 1)
        write(send_a, 0, 0)


def halves(a):
    high = a.astype(jnp.bfloat16)
    return high, (a - high.astype(jnp.float32)).astype(jnp.bfloat16)


def sweep(root, field, lo, hi, put):
    def pair(x):
        u = root(x) if field is None else root(x) * field(x)
        return (u, z_sum(u))

    first, second = pair(lo - 1), pair(lo)
    for x in range(lo, hi):
        third = pair(x + 1)
        put(x, slab_sum(first, second, third, row_sum))
        first, second = second, third


def final_diag(raw, root, total):
    return (raw + root * total - CENTRE) * (2.0 / HALF_WIDTH)


def next_basis(j, diag, root, here, total, before):
    new = diag * here - (2.0 / HALF_WIDTH) * root * total
    return 0.5 * new if j == 1 else new - before


def inner_kernel(py, side_a, side_b, root_own, abs_own, b0, edge, root, diag, frames, far):
    nx, ny, _ = b0.shape
    for part, out in ((root_own, root), (abs_own, diag)):
        for y in range(0, ny, DEEP):
            first = y * (LANES // NRHS)
            out[:, DEEP + y : 2 * DEEP + y, :] = spread(part[:, first : first + LANES])
    inner = slice(1, nx - 1)
    frames[0, inner, DEEP : DEEP + ny, :] = b0[inner]

    def read(msg, y0, side):
        n = (nx - 2) * DEEP
        frames[0, inner, y0 : y0 + DEEP, :] = msg[0:n].reshape(nx - 2, DEEP, LANES)
        far[side] = msg[n : n + nx]
        n += nx
        for out in (root, diag):
            out[:, y0 : y0 + DEEP, :] = spread(msg[n : n + nx])
            n += nx

    @pl.when(py[0] == 0)
    def _():
        read(side_b, 0, 0)
        read(side_a, DEEP + ny, 1)

    @pl.when(py[0] == 1)
    def _():
        read(side_a, 0, 0)
        read(side_b, DEEP + ny, 1)

    def column(v, y):
        r = root[:, y, :]
        return v, r, cross_sum(r * v, row_sum), cross_sum(r, row_sum)

    for side, out_y, in_y in ((0, DEEP - 1, DEEP), (1, DEEP + ny, DEEP + ny - 1)):
        va, ra, ua, wa = column(far[side], out_y)
        vb, rb, ub, wb = column(edge[side], in_y)
        for y, fix in ((out_y, ra * (ub - va * wb)), (in_y, rb * (ua - vb * wa))):
            frames[0, inner, y, :] = frames[0, inner, y, :] + fix[inner]

    def put_diag(x, total):
        diag[x] = final_diag(diag[x], root[x], total)

    sweep(lambda x: root[x], None, 1, nx - 1, put_diag)
    for j in range(1, S + 1):

        def put(x, total):
            before = frames[j - 2, x] if j > 1 else None
            frames[j, x] = next_basis(j, diag[x], root[x], frames[j - 1, x], total, before)

        sweep(lambda x: root[x], lambda x: frames[j - 1, x], 1 + j, nx - 1 - j, put)


def basis_kernel(
    py, recv_a, recv_b, root_h, abs_h, band, edge, root_i, diag_i, frames, far_own,
    rough, fine, moments, root_o, diag_o, far, f0, f1, f2
):
    _, nx, tall, _ = frames.shape
    ny = tall - 2 * DEEP
    wide = nx + 2 * DEEP
    low, high_x = DEEP + 1, DEEP + nx - 1
    for side in (0, 1):
        rows = slice(side * DEEP, (side + 1) * DEEP)
        for y in range(0, ny, DEEP):
            first = y * (LANES // NRHS)
            for part, out in ((root_h, root_o), (abs_h, diag_o)):
                out[rows, DEEP + y : 2 * DEEP + y, :] = spread(
                    part[side, :, first : first + LANES]
                )
        far[side, DEEP : DEEP + nx] = far_own[side]
    f0[0:low, DEEP : DEEP + ny, :] = band[0]
    f0[high_x:wide, DEEP : DEEP + ny, :] = band[1]

    def read(msg, y0, side):
        n = 0
        for x0 in (0, high_x):
            m = (DEEP + 1) * DEEP
            f0[x0 : x0 + DEEP + 1, y0 : y0 + DEEP, :] = msg[n : n + m].reshape(
                DEEP + 1, DEEP, LANES
            )
            n += m
        for at, x0 in ((0, 0), (DEEP, DEEP + nx)):
            far[side, x0 : x0 + DEEP] = msg[n : n + DEEP]
            n += DEEP
            for out in (root_o, diag_o):
                out[at : at + DEEP, y0 : y0 + DEEP, :] = spread(msg[n : n + DEEP])
                n += DEEP
        far[side, wide : wide + 8] = msg[n : n + 8]

    @pl.when(py[0] == 0)
    def _():
        read(recv_b, 0, 0)
        read(recv_a, DEEP + ny, 1)

    @pl.when(py[0] == 1)
    def _():
        read(recv_a, 0, 0)
        read(recv_b, DEEP + ny, 1)

    row = lax.broadcasted_iota(jnp.int32, (wide, LANES), 0)

    def across(f, before, after):
        p = z_sum(f)
        ends = jnp.concatenate([before, after], axis=0)
        ends = 0.5 * ends + (1.0 / 3.0) * z_sum(ends)
        g = 0.5 * f + (1.0 / 3.0) * p
        up = jnp.where(row == 0, ends[0:1], pltpu.roll(g, 1, 0))
        down = jnp.where(row == wide - 1, ends[1:2], pltpu.roll(g, wide - 1, 0))
        return f + 0.5 * p + up + down

    def column(ref, at, y):
        v = ref[at, 0:wide]
        ends = ref[at, wide : wide + 8]
        r = jnp.concatenate([root_o[0:DEEP, y, :], root_i[:, y, :], root_o[DEEP:, y, :]], axis=0)
        r0, r1 = ends[2:3], ends[3:4]
        return v, r, across(r * v, r0 * ends[0:1], r1 * ends[1:2]), across(r, r0, r1)

    for side, out_y, in_y in ((0, DEEP - 1, DEEP), (1, DEEP + ny, DEEP + ny - 1)):
        va, ra, ua, wa = column(far, side, out_y)
        vb, rb, ub, wb = column(edge, side, in_y)
        for y, fix in ((out_y, ra * (ub - va * wb)), (in_y, rb * (ua - vb * wa))):
            f0[0:low, y, :] = f0[0:low, y, :] + fix[0:low]
            f0[high_x:wide, y, :] = f0[high_x:wide, y, :] + fix[high_x:wide]

    outer = [f0, f1, f2]

    def root(x):
        if DEEP <= x < DEEP + nx:
            return root_i[x - DEEP]
        return root_o[x if x < DEEP else x - nx]

    def field(j):
        def at(x):
            if low + j <= x < high_x - j:
                return frames[j, x - DEEP]
            return outer[j % 3][x]

        return at

    edges = {}

    def diag(x):
        if low <= x < high_x:
            return diag_i[x - DEEP]
        if x in (DEEP, DEEP + nx - 1):
            return diag_e[0 if x == DEEP else 1]
        return diag_o[x if x < DEEP else x - nx]

    def put_diag(x, total):
        if DEEP <= x < DEEP + nx:
            edges[x] = final_diag(diag_i[x - DEEP], root(x), total)
        else:
            at = x if x < DEEP else x - nx
            diag_o[at] = final_diag(diag_o[at], root(x), total)

    for lo, hi in ((1, low), (high_x, wide - 1)):
        sweep(root, None, lo, hi, put_diag)
    diag_e = (edges[DEEP], edges[DEEP + nx - 1])

    level = lanes_of((NRHS, LANES)) // NRHS
    depth = LANES // NRHS
    folded = [None] * (2 * S + 1)

    def note(n, block):
        if n in (0, 1, 2 * S):
            block = 0.5 * (block + block.T)
        f = block[0:NRHS]
        for z in range(1, depth):
            f = jnp.where(level == z, block[z * NRHS : (z + 1) * NRHS], f)
        folded[n] = f

    old = None
    for j in range(S + 1):
        now = outer[j % 3]
        if j > 0:
            here, before = field(j - 1), field(j - 2)

            def put(x, total):
                past = before(x) if j > 1 else None
                now[x] = next_basis(j, diag(x), root(x), here(x), total, past)

            for lo, hi in ((j, low + j), (high_x - j, wide - j)):
                sweep(root, here, lo, hi, put)
        columns = slice(DEEP, DEEP + ny)
        own = jnp.concatenate(
            [
                now[DEEP : low + j, columns, :],
                frames[j, 1 + j : nx - 1 - j, columns, :],
                now[high_x - j : DEEP + nx, columns, :],
            ],
            axis=0,
        )
        high, rest = halves(own.reshape(nx * ny, LANES))
        rough[:, j * LANES : (j + 1) * LANES] = high
        fine[:, j * LANES : (j + 1) * LANES] = rest
        turned = high.T
        both = jnp.concatenate([high, rest], axis=1)
        left = turned if j == 0 else jnp.concatenate([turned, old[0]], axis=0)
        got = jnp.dot(left, both, preferred_element_type=jnp.float32)
        note(2 * j, got[:LANES, :LANES] + 2.0 * got[:LANES, LANES:])
        if j > 0:
            more = jnp.dot(turned, old[1], preferred_element_type=jnp.float32)
            note(2 * j - 1, got[LANES:, :LANES] + got[LANES:, LANES:] + more)
        old = (turned, rest)
    every = jnp.concatenate(folded, axis=0)
    shift = LANES // 2
    while shift >= NRHS:
        every = every + pltpu.roll(every, shift, 1)
        shift //= 2
    blocks = [every[n * NRHS : (n + 1) * NRHS] for n in range(2 * S + 1)]
    tile = jnp.zeros((NRHS, LANES), jnp.float32)
    row, col = rows_at((NRHS, LANES)), lanes_of((NRHS, LANES)) % NRHS
    last = blocks[2 * S]
    below = jnp.where(row == col + 1, pltpu.roll(last, 1, 0), 0.0)
    below = jnp.where((row == NRHS - 1) & (col == 0), pltpu.roll(last, 1, 1), below)
    blocks[0] = jnp.where(row <= col, blocks[0], last)
    blocks[1] = jnp.where(row <= col, blocks[1], below)
    for n in range(2 * S):
        tile = jnp.where(level == n, blocks[n], tile)
    moments[...] = jnp.broadcast_to(tile[None], moments.shape)


def moment_blocks(tile):
    depth = LANES // NRHS
    row, lane = rows_at((NRHS, LANES)), lanes_of((NRHS, LANES))
    raw = [tile] + [pltpu.roll(tile, LANES - NRHS * n, 1) for n in range(1, depth)]
    square = jnp.concatenate([tile, jnp.zeros((LANES - NRHS, LANES), jnp.float32)], axis=0).T
    turned = [square[n * NRHS : (n + 1) * NRHS] for n in range(depth)]
    first, second = raw[0], raw[1]
    last = jnp.where(row > lane, first, turned[0])
    last = jnp.where(row == lane, pltpu.roll(second, NRHS - 1, 0), last)
    last = jnp.where((row == NRHS - 1) & (lane == NRHS - 1), pltpu.roll(second, NRHS - 1, 1), last)
    even = [0.5 * (r + t) for r, t in zip(raw, turned)] + [last]
    even[0] = jnp.where(row <= lane, first, turned[0])
    even[1] = jnp.where(row <= lane, second, turned[1])
    even = [jnp.where(lane < NRHS, e, 0.0) for e in even]
    return even[:2] + [2.0 * even[n] - even[n % 2] for n in range(2, 2 * S + 1)]


def solve_small(m):
    lane = lanes_of((NRHS, LANES))
    half = HALF_WIDTH / 2
    size = S * NRHS

    def a_on(seq, n):
        return CENTRE * seq[n] + half * (seq[n + 1] + seq[abs(n - 1)])

    nu = [a_on(m, n) for n in range(2 * S)]
    mu = [a_on(nu, n) for n in range(2 * S - 1)]
    up = functools.reduce(jnp.add, [mu[n] if n == 0 else pltpu.roll(mu[n], NRHS * n, 1) for n in range(2 * S - 1)])
    around = functools.reduce(
        jnp.add,
        [mu[abs(n - (S - 1))] if n == 0 else pltpu.roll(mu[abs(n - (S - 1))], NRHS * n, 1) for n in range(2 * S - 1)],
    )

    def left(f, places):
        return f if places == 0 else pltpu.roll(f, LANES - places, 1)

    rows = []
    for c in range(S):
        both = 0.5 * (left(up, NRHS * c) + left(around, NRHS * (S - 1 - c)))
        rows.append(jnp.where(lane < size, both, pltpu.roll(nu[c], size, 1)))
    m = jnp.concatenate(rows, axis=0)
    row, col = rows_at((size, LANES)), lanes_of((size, LANES))
    on = row == col
    kept = jnp.where(on, m, 0.0)
    scale = 1.0 / jnp.sqrt(jnp.sum(kept, axis=1, keepdims=True))
    across = jnp.sum(kept, axis=0, keepdims=True)
    across = jnp.where(lanes_of((1, LANES)) < size, 1.0 / jnp.sqrt(across), 1.0)
    m = scale * m * across + jnp.where(on, RIDGE, 0.0)
    for first in range(0, size, PANEL):
        columns = [
            jnp.broadcast_to(m[:, i : i + 1], m.shape) for i in range(first, first + PANEL)
        ]
        for p in range(0, PANEL, 2):
            i = first + p
            c0, c1 = columns[p], columns[p + 1]
            a, b, d = c0[i : i + 1], c1[i : i + 1], c1[i + 1 : i + 2]
            inverse = 1.0 / (a * d - b * b)
            a, b, d = inverse * a, inverse * b, inverse * d
            d0 = jnp.where(row == i, c0 - 1.0, c0)
            d1 = jnp.where(row == i + 1, c1 - 1.0, c1)
            for later in range(p + 2, PANEL):
                r0 = c0[first + later : first + later + 1]
                r1 = c1[first + later : first + later + 1]
                columns[later] = columns[later] - d0 * (d * r0 - b * r1) - d1 * (a * r1 - b * r0)
            r0, r1 = m[i : i + 1], m[i + 1 : i + 2]
            m = m - d0 * (d * r0 - b * r1) - d1 * (a * r1 - b * r0)
    x = jnp.where((col >= size) & (col < size + NRHS), scale * m, 0.0)
    shift = NRHS
    while shift < LANES:
        x = x + pltpu.roll(x, shift, 1)
        shift *= 2
    c = [x[j * NRHS : (j + 1) * NRHS] for j in range(S)]
    unit = jnp.where(rows_at((NRHS, LANES)) == lane % NRHS, 1.0, 0.0)
    remain = []
    for j in range(S + 1):
        total = CENTRE * c[j] if j < S else 0.0
        if j > 0:
            total = total + (HALF_WIDTH if j == 1 else half) * c[j - 1]
        if j + 1 < S:
            total = total + half * c[j + 1]
        remain.append((unit if j == 0 else 0.0) - total)
    return c, remain


def combine_kernel(guess, rough, fine, parts, update, rest, wh, wl):
    nx, ny, _ = guess.shape
    level = lanes_of((NRHS, LANES)) // NRHS
    coeffs, remain = solve_small(moment_blocks(jnp.sum(parts[...], axis=0)))
    coeffs = coeffs + [jnp.zeros((NRHS, LANES), jnp.float32)]
    for part, tiles in ((0, coeffs), (1, remain)):
        for j in range(S + 1):
            full = jnp.concatenate(
                [jnp.where(level == z, tiles[j], 0.0) for z in range(LANES // NRHS)], axis=0
            )
            high, low = halves(full)
            wh[j * LANES : (j + 1) * LANES, part * LANES : (part + 1) * LANES] = high
            wl[j * LANES : (j + 1) * LANES, part * LANES : (part + 1) * LANES] = low
    chunk = nx // 4
    for i in range(4):
        at = slice(i * chunk, (i + 1) * chunk)
        cells = slice(i * chunk * ny, (i + 1) * chunk * ny)
        dot = functools.partial(jnp.dot, preferred_element_type=jnp.float32)
        out = dot(rough[cells], wh[...]) + dot(rough[cells], wl[...]) + dot(fine[cells], wh[...])
        out = out.reshape(chunk, ny, 2 * LANES)
        update[at] = guess[at] + out[:, :, :LANES]
        rest[at] = out[:, :, LANES:]


def call(kernel, ins, outs, scratch=(), scalars=0, kinds=None, space=pltpu.VMEM, limit=VMEM_BYTES):
    specs = [pl.BlockSpec(memory_space=pltpu.SMEM)] * scalars
    specs += [pl.BlockSpec(memory_space=space)] * (len(ins) - scalars)
    result = pl.pallas_call(
        kernel,
        out_shape=[
            jax.ShapeDtypeStruct(s, k) for s, k in zip(outs, kinds or [jnp.float32] * len(outs))
        ],
        in_specs=specs,
        out_specs=[pl.BlockSpec(memory_space=pltpu.VMEM)] * len(outs),
        scratch_shapes=list(scratch),
        compiler_params=pltpu.CompilerParams(vmem_limit_bytes=limit),
    )(*ins)
    return result


def exchange(first, second, axis):
    count = lax.axis_size(axis)
    got = []
    for cells, start in ((first, 0), (second, 1)):
        links = []
        for i in range(start, count - 1, 2):
            links += [(i, i + 1), (i + 1, i)]
        got.append(lax.ppermute(cells, axis, links))
    return got


def total_of(x, axis):
    count = lax.axis_size(axis)
    if count & (count - 1):
        return lax.psum(x, axis)
    step = 1
    while step < count:
        x = x + lax.ppermute(x, axis, [(i, i ^ step) for i in range(count)])
        step *= 2
    return x


def totals(parts):
    count = parts.shape[0]
    if count > 1:
        return lax.all_to_all(parts, ("gx", "gy"), 0, 0)
    return total_of(total_of(parts, "gy"), "gx")


def body(initial_guess, source, leaf_density, absorption):
    nx, ny, lanes = initial_guess.shape
    cells = jnp.transpose(jnp.stack([leaf_density, absorption]), (0, 2, 3, 1))
    depth = cells.shape[2]
    px = lax.rem(lax.axis_index("gx"), 2).astype(jnp.int32).reshape(1)
    py = lax.rem(lax.axis_index("gy"), 2).astype(jnp.int32).reshape(1)
    wide = nx + 2 * DEEP
    tall = ny + 2 * DEEP
    block = (nx, ny, lanes)
    across = ny * depth
    x_rows = DEEP * ny + ny + 2 * DEEP + 8 + 2 * DEEP * (across // lanes)
    side_rows = (nx - 2) * DEEP + 3 * nx
    y_rows = 2 * (DEEP + 1) * DEEP + 6 * DEEP + 8
    sides = ((2, nx, lanes), (2, ny, lanes))
    root, absb, b0, rim, edge, face, xa, xb, sa, sb = call(
        begin_kernel,
        (px, py, initial_guess, source, cells),
        ((nx, across), (nx, across), block, sides[1], *sides)
        + ((x_rows, lanes),) * 2
        + ((side_rows, lanes),) * 2,
        scratch=[
            pltpu.VMEM(block, jnp.float32),
            pltpu.VMEM(block, jnp.float32),
            pltpu.VMEM(cells.shape, jnp.float32),
            pltpu.VMEM(block, jnp.float32),
            pltpu.VMEM(block, jnp.float32),
            pltpu.SemaphoreType.DMA((3,)),
        ],
        scalars=2,
        space=pltpu.HBM,
        limit=BEGIN_BYTES,
    )
    xa, xb = exchange(xa, xb, "gx")
    sa, sb = exchange(sa, sb, "gy")
    root_h, abs_h, band, edges, ya, yb = call(
        widen_kernel,
        (px, py, xa, xb, edge, face, root, absb, rim),
        ((2, DEEP, across),) * 2
        + ((2, DEEP + 1, ny, lanes), (2, wide + 8, lanes))
        + ((y_rows, lanes),) * 2,
        scratch=[pltpu.VMEM((2, ny, lanes), jnp.float32)],
        scalars=2,
    )
    ya, yb = exchange(ya, yb, "gy")
    inner = (nx, tall, lanes)
    root_i, diag_i, frames, far = call(
        inner_kernel,
        (py, sa, sb, root, absb, b0, edge),
        (inner, inner, (S + 1, *inner), sides[0]),
        scalars=1,
    )
    frame = pltpu.VMEM((wide, tall, lanes), jnp.float32)
    halo = pltpu.VMEM((2 * DEEP, tall, lanes), jnp.float32)
    count = lax.axis_size("gx") * lax.axis_size("gy")
    count = count if count <= 64 else 1
    cells = nx * ny
    rough, fine, moments = call(
        basis_kernel,
        (py, ya, yb, root_h, abs_h, band, edges, root_i, diag_i, frames, far),
        ((cells, (S + 1) * lanes), (cells, (S + 1) * lanes), (count, NRHS, lanes)),
        scratch=[halo, halo, pltpu.VMEM((2, wide + 8, lanes), jnp.float32), frame, frame, frame],
        scalars=1,
        kinds=(jnp.bfloat16, jnp.bfloat16, jnp.float32),
    )
    return call(
        combine_kernel,
        (initial_guess, rough, fine, totals(moments)),
        (block, block),
        scratch=[pltpu.VMEM(((S + 1) * lanes, 2 * lanes), jnp.bfloat16)] * 2,
    )


def solution(mesh):
    spec = P("gx", "gy", None)
    return jax.shard_map(
        lambda *arrays: tuple(body(*arrays)),
        mesh=mesh,
        in_specs=(spec,) * 4,
        out_specs=(spec, spec),
        check_vma=False,
    )
```

```python
import functools

import jax
import jax.numpy as jnp
from jax import lax
from jax.experimental import pallas as pl
from jax.experimental.pallas import tpu as pltpu
from jax.sharding import PartitionSpec as P

NRHS = 8
S = 8
DEEP = S
LANES = 128

PEAK_COND = 0.6
CENTRE = 10.3
HALF_WIDTH = 9.8
RIDGE = 0.05
PANEL = 16
ROOT_SCALE = (2.0 / HALF_WIDTH) ** 0.5
VMEM_BYTES = 24 * 1024 * 1024
BEGIN_BYTES = 54300 * 1024


def lanes_of(shape):
    return lax.broadcasted_iota(jnp.int32, shape, len(shape) - 1)


def rows_at(shape):
    return lax.broadcasted_iota(jnp.int32, shape, len(shape) - 2)


def z_sum(f):
    lane = lanes_of(f.shape)
    ax = f.ndim - 1
    up = jnp.where(lane >= NRHS, pltpu.roll(f, NRHS, ax), 0.0)
    down = jnp.where(lane < LANES - NRHS, pltpu.roll(f, LANES - NRHS, ax), 0.0)
    return up + down


def row_sum(f):
    n = f.shape[-2]
    ax = f.ndim - 2
    return pltpu.roll(f, 1, ax) + pltpu.roll(f, n - 1, ax)


def row_sum_zero(f):
    n = f.shape[-2]
    ax = f.ndim - 2
    row = rows_at(f.shape)
    up = jnp.where(row >= 1, pltpu.roll(f, 1, ax), 0.0)
    down = jnp.where(row < n - 1, pltpu.roll(f, n - 1, ax), 0.0)
    return up + down


def slab_sum(before, here, after, rows):
    ux = before[0] + after[0]
    px = before[1] + after[1]
    s = here[1] + ux
    q = here[0] + 0.5 * s + (1.0 / 3.0) * px
    return s + 0.5 * px + rows(q)


def cross_sum(f, rows):
    p = z_sum(f)
    return f + 0.5 * p + rows(0.5 * f + (1.0 / 3.0) * p)


def spread(rows):
    n = rows.shape[0]
    depth = LANES // NRHS
    at = rows_at((NRHS, LANES)) * depth + lanes_of((NRHS, LANES)) // NRHS
    out = []
    for x in range(n):
        line = jnp.broadcast_to(rows[x : x + 1], (NRHS, LANES))
        out.append(jnp.take_along_axis(line, at, axis=1))
    return jnp.stack(out)


def begin_kernel(px, py, *refs):
    far, refs = refs[:3], refs[3:]
    (root_o, abs_o, b0_o, rim_o, edge_o, face_o), refs = refs[:6], refs[6:]
    (send_a, send_b, side_a, side_b), refs = refs[:4], refs[4:]
    guess, source, pair_in, root, absb, sems = refs
    copies = [
        pltpu.make_async_copy(there, here, sems.at[i])
        for i, (there, here) in enumerate(zip(far, (guess, source, pair_in)))
    ]
    for i in (2, 0, 1):
        copies[i].start()
    nx, ny, _ = guess.shape
    depth = pair_in.shape[2]
    copies[2].wait()
    turned = jnp.transpose(pair_in[0].reshape(ny * depth, nx))
    root_o[...] = jnp.sqrt(PEAK_COND / (1.0 + turned))
    abs_o[...] = jnp.transpose(pair_in[1].reshape(ny * depth, nx))
    for part, wide in ((root_o, root), (abs_o, absb)):
        for y in range(0, ny, NRHS):
            wide[:, y : y + NRHS, :] = spread(part[:, y * depth : (y + NRHS) * depth])
    copies[0].wait()
    copies[1].wait()
    for at, col, face in ((0, 0, 0), (1, ny - 1, nx - 1)):
        edge_o[at] = guess[:, col, :]
        face_o[at] = guess[face]
    zero = jnp.zeros((ny, LANES), jnp.float32)

    def pair(x, field):
        if x < 0 or x >= nx:
            return (zero, zero)
        u = root[x] if field is None else root[x] * field[x]
        return (u, z_sum(u))

    moving = [pair(-1, guess), pair(0, guess)]
    still = [pair(-1, None), pair(0, None)]
    for x in range(nx):
        moving.append(pair(x + 1, guess))
        still.append(pair(x + 1, None))
        wu = slab_sum(*moving, row_sum_zero)
        wr = slab_sum(*still, row_sum_zero)
        moving, still = moving[1:], still[1:]
        v = guess[x]
        b0_o[x] = source[x] - absb[x] * v + root[x] * (wu - v * wr)

    rim_o[0] = b0_o[0]
    rim_o[1] = b0_o[nx - 1]

    def write(out, x0, face, beyond):
        n = DEEP * ny
        out[0:n] = b0_o[x0 : x0 + DEEP].reshape(n, LANES)
        out[n : n + ny] = guess[face]
        n += ny
        for col in (0, ny - 1):
            out[n : n + DEEP] = guess[x0 : x0 + DEEP, col, :]
            n += DEEP
        out[n : n + 8] = jnp.zeros((8, LANES), jnp.float32)
        for at, col in ((0, 0), (1, ny - 1)):
            out[n + at : n + at + 1] = guess[beyond, col : col + 1, :]
            out[n + 2 + at : n + 3 + at] = root[beyond, col : col + 1, :]
        n += 8
        for part in (root_o, abs_o):
            for first in range(0, ny * depth, LANES):
                out[n : n + DEEP] = part[x0 : x0 + DEEP, first : first + LANES]
                n += DEEP

    @pl.when(px[0] == 0)
    def _():
        write(send_a, nx - DEEP, nx - 1, nx - DEEP - 1)
        write(send_b, 0, 0, DEEP)

    @pl.when(px[0] == 1)
    def _():
        write(send_b, nx - DEEP, nx - 1, nx - DEEP - 1)
        write(send_a, 0, 0, DEEP)

    def write_side(out, y0, at):
        n = (nx - 2) * DEEP
        out[0:n] = b0_o[1 : nx - 1, y0 : y0 + DEEP, :].reshape(n, LANES)
        out[n : n + nx] = edge_o[at]
        n += nx
        for part in (root_o, abs_o):
            out[n : n + nx] = part[:, y0 * depth : (y0 + DEEP) * depth]
            n += nx

    @pl.when(py[0] == 0)
    def _():
        write_side(side_a, ny - DEEP, 1)
        write_side(side_b, 0, 0)

    @pl.when(py[0] == 1)
    def _():
        write_side(side_b, ny - DEEP, 1)
        write_side(side_a, 0, 0)


def widen_kernel(
    px, py, recv_a, recv_b, edge_own, face_own, root, absb, rim,
    root_h, abs_h, band, edge, send_a, send_b, face
):
    nx, ny = edge_own.shape[1], face_own.shape[1]
    wide = nx + 2 * DEEP
    for at in (0, 1):
        edge[at, DEEP : DEEP + nx] = edge_own[at]
        edge[at, wide : wide + 8] = jnp.zeros((8, LANES), jnp.float32)

    def read(msg, x0, side):
        n = DEEP * ny
        band[side, side : side + DEEP] = msg[0:n].reshape(DEEP, ny, LANES)
        face[side] = msg[n : n + ny]
        n += ny
        for at in (0, 1):
            edge[at, x0 : x0 + DEEP] = msg[n : n + DEEP]
            n += DEEP
        for at in (0, 1):
            edge[at, wide + side : wide + side + 1] = msg[n + at : n + at + 1]
            edge[at, wide + 2 + side : wide + 3 + side] = msg[n + 2 + at : n + 3 + at]
        n += 8
        for out in (root_h, abs_h):
            for first in range(0, out.shape[2], LANES):
                out[side, :, first : first + LANES] = msg[n : n + DEEP]
                n += DEEP

    @pl.when(px[0] == 0)
    def _():
        read(recv_b, 0, 0)
        read(recv_a, DEEP + nx, 1)

    @pl.when(px[0] == 1)
    def _():
        read(recv_a, 0, 0)
        read(recv_b, DEEP + nx, 1)

    def line(rows):
        parts = [spread(rows[:, at : at + LANES]) for at in range(0, rows.shape[1], LANES)]
        return jnp.concatenate(parts, axis=1)[0]

    for side, out_x, in_x, far_x, near_x in (
        (0, DEEP - 1, DEEP, DEEP - 1, 0),
        (1, 1, 0, 0, nx - 1),
    ):
        va, ra = face[side], line(root_h[side, far_x : far_x + 1])
        vb, rb = face_own[side], line(root[near_x : near_x + 1])
        fix_a = ra * (cross_sum(rb * vb, row_sum_zero) - va * cross_sum(rb, row_sum_zero))
        fix_b = rb * (cross_sum(ra * va, row_sum_zero) - vb * cross_sum(ra, row_sum_zero))
        band[side, out_x] = band[side, out_x] + fix_a
        band[side, in_x] = rim[side] + fix_b

    def write(out, y0, at):
        n = 0
        for side in (0, 1):
            m = (DEEP + 1) * DEEP
            out[n : n + m] = band[side, :, y0 : y0 + DEEP, :].reshape(m, LANES)
            n += m
        first = y0 * (LANES // NRHS)
        for side, x0 in ((0, 0), (1, DEEP + nx)):
            out[n : n + DEEP] = edge[at, x0 : x0 + DEEP]
            n += DEEP
            for part in (root_h, abs_h):
                out[n : n + DEEP] = part[side, :, first : first + LANES]
                n += DEEP
        out[n : n + 8] = edge[at, wide : wide + 8]

    @pl.when(py[0] == 0)
    def _():
        write(send_a, ny - DEEP, 1)
        write(send_b, 0, 0)

    @pl.when(py[0] == 1)
    def _():
        write(send_b, ny - DEEP, 1)
        write(send_a, 0, 0)


def halves(a):
    high = a.astype(jnp.bfloat16)
    return high, (a - high.astype(jnp.float32)).astype(jnp.bfloat16)


def sweep(root, field, lo, hi, put):
    def pair(x):
        u = root(x) if field is None else root(x) * field(x)
        return (u, z_sum(u))

    first, second = pair(lo - 1), pair(lo)
    for x in range(lo, hi):
        third = pair(x + 1)
        put(x, slab_sum(first, second, third, row_sum))
        first, second = second, third


def final_diag(raw, root, total):
    return (raw - CENTRE) * (2.0 / HALF_WIDTH) + root * total


def next_basis(j, diag, root, here, total, before):
    new = diag * here - root * total
    return 0.5 * new if j == 1 else new - before


def inner_kernel(py, side_a, side_b, root_own, abs_own, b0, edge, root, diag, frames, far):
    nx, ny, _ = b0.shape
    for part, out, factor in ((root_own, root, ROOT_SCALE), (abs_own, diag, 1.0)):
        for y in range(0, ny, DEEP):
            first = y * (LANES // NRHS)
            some = factor * part[:, first : first + LANES]
            out[:, DEEP + y : 2 * DEEP + y, :] = spread(some)
    inner = slice(1, nx - 1)
    frames[0, inner, DEEP : DEEP + ny, :] = b0[inner]

    def read(msg, y0, side):
        n = (nx - 2) * DEEP
        frames[0, inner, y0 : y0 + DEEP, :] = msg[0:n].reshape(nx - 2, DEEP, LANES)
        far[side] = msg[n : n + nx]
        n += nx
        for out, factor in ((root, ROOT_SCALE), (diag, 1.0)):
            out[:, y0 : y0 + DEEP, :] = spread(factor * msg[n : n + nx])
            n += nx

    @pl.when(py[0] == 0)
    def _():
        read(side_b, 0, 0)
        read(side_a, DEEP + ny, 1)

    @pl.when(py[0] == 1)
    def _():
        read(side_a, 0, 0)
        read(side_b, DEEP + ny, 1)

    def column(v, y):
        r = root[:, y, :]
        return v, r, cross_sum(r * v, row_sum), cross_sum(r, row_sum)

    for side, out_y, in_y in ((0, DEEP - 1, DEEP), (1, DEEP + ny, DEEP + ny - 1)):
        va, ra, ua, wa = column(far[side], out_y)
        vb, rb, ub, wb = column(edge[side], in_y)
        for y, fix in ((out_y, ra * (ub - va * wb)), (in_y, rb * (ua - vb * wa))):
            fix = fix * (HALF_WIDTH / 2)
            frames[0, inner, y, :] = frames[0, inner, y, :] + fix[inner]

    def put_diag(x, total):
        diag[x] = final_diag(diag[x], root[x], total)

    sweep(lambda x: root[x], None, 1, nx - 1, put_diag)
    for j in range(1, S + 1):

        def put(x, total):
            before = frames[j - 2, x] if j > 1 else None
            new = next_basis(j, diag[x], root[x], frames[j - 1, x], total, before)
            if j < S:
                frames[j, x] = new
            else:
                frames[j, x, DEEP : DEEP + ny] = new[DEEP : DEEP + ny]

        sweep(lambda x: root[x], lambda x: frames[j - 1, x], 1 + j, nx - 1 - j, put)


def basis_kernel(
    py, recv_a, recv_b, root_h, abs_h, band, edge, root_i, diag_i, frames, far_own,
    rough, fine, moments, root_o, diag_o, far, f0, f1, f2
):
    _, nx, tall, _ = frames.shape
    ny = tall - 2 * DEEP
    wide = nx + 2 * DEEP
    low, high_x = DEEP + 1, DEEP + nx - 1
    for side in (0, 1):
        rows = slice(side * DEEP, (side + 1) * DEEP)
        for y in range(0, ny, DEEP):
            first = y * (LANES // NRHS)
            for part, out, factor in ((root_h, root_o, ROOT_SCALE), (abs_h, diag_o, 1.0)):
                some = factor * part[side, :, first : first + LANES]
                out[rows, DEEP + y : 2 * DEEP + y, :] = spread(some)
        far[side, DEEP : DEEP + nx] = far_own[side]
    f0[0:low, DEEP : DEEP + ny, :] = band[0]
    f0[high_x:wide, DEEP : DEEP + ny, :] = band[1]

    def read(msg, y0, side):
        n = 0
        for x0 in (0, high_x):
            m = (DEEP + 1) * DEEP
            f0[x0 : x0 + DEEP + 1, y0 : y0 + DEEP, :] = msg[n : n + m].reshape(
                DEEP + 1, DEEP, LANES
            )
            n += m
        for at, x0 in ((0, 0), (DEEP, DEEP + nx)):
            far[side, x0 : x0 + DEEP] = msg[n : n + DEEP]
            n += DEEP
            for out, factor in ((root_o, ROOT_SCALE), (diag_o, 1.0)):
                out[at : at + DEEP, y0 : y0 + DEEP, :] = spread(factor * msg[n : n + DEEP])
                n += DEEP
        far[side, wide : wide + 8] = msg[n : n + 8]

    @pl.when(py[0] == 0)
    def _():
        read(recv_b, 0, 0)
        read(recv_a, DEEP + ny, 1)

    @pl.when(py[0] == 1)
    def _():
        read(recv_a, 0, 0)
        read(recv_b, DEEP + ny, 1)

    row = lax.broadcasted_iota(jnp.int32, (wide, LANES), 0)

    def across(f, before, after):
        p = z_sum(f)
        ends = jnp.concatenate([before, after], axis=0)
        ends = 0.5 * ends + (1.0 / 3.0) * z_sum(ends)
        g = 0.5 * f + (1.0 / 3.0) * p
        up = jnp.where(row == 0, ends[0:1], pltpu.roll(g, 1, 0))
        down = jnp.where(row == wide - 1, ends[1:2], pltpu.roll(g, wide - 1, 0))
        return f + 0.5 * p + up + down

    def column(ref, at, y):
        v = ref[at, 0:wide]
        ends = ref[at, wide : wide + 8]
        r = jnp.concatenate([root_o[0:DEEP, y, :], root_i[:, y, :], root_o[DEEP:, y, :]], axis=0)
        r0, r1 = ROOT_SCALE * ends[2:3], ROOT_SCALE * ends[3:4]
        return v, r, across(r * v, r0 * ends[0:1], r1 * ends[1:2]), across(r, r0, r1)

    for side, out_y, in_y in ((0, DEEP - 1, DEEP), (1, DEEP + ny, DEEP + ny - 1)):
        va, ra, ua, wa = column(far, side, out_y)
        vb, rb, ub, wb = column(edge, side, in_y)
        for y, fix in ((out_y, ra * (ub - va * wb)), (in_y, rb * (ua - vb * wa))):
            fix = fix * (HALF_WIDTH / 2)
            f0[0:low, y, :] = f0[0:low, y, :] + fix[0:low]
            f0[high_x:wide, y, :] = f0[high_x:wide, y, :] + fix[high_x:wide]

    outer = [f0, f1, f2]

    def root(x):
        if DEEP <= x < DEEP + nx:
            return root_i[x - DEEP]
        return root_o[x if x < DEEP else x - nx]

    def field(j):
        def at(x):
            if low + j <= x < high_x - j:
                return frames[j, x - DEEP]
            return outer[j % 3][x]

        return at

    edges = {}

    def diag(x):
        if low <= x < high_x:
            return diag_i[x - DEEP]
        if x in (DEEP, DEEP + nx - 1):
            return diag_e[0 if x == DEEP else 1]
        return diag_o[x if x < DEEP else x - nx]

    def put_diag(x, total):
        if DEEP <= x < DEEP + nx:
            edges[x] = final_diag(diag_i[x - DEEP], root(x), total)
        else:
            at = x if x < DEEP else x - nx
            diag_o[at] = final_diag(diag_o[at], root(x), total)

    for lo, hi in ((1, low), (high_x, wide - 1)):
        sweep(root, None, lo, hi, put_diag)
    diag_e = (edges[DEEP], edges[DEEP + nx - 1])

    level = lanes_of((NRHS, LANES)) // NRHS
    depth = LANES // NRHS
    folded = [None] * (2 * S + 1)

    def note(n, block):
        if n in (0, 1, 2 * S):
            block = 0.5 * (block + block.T)
        f = block[0:NRHS]
        for z in range(1, depth):
            f = jnp.where(level == z, block[z * NRHS : (z + 1) * NRHS], f)
        folded[n] = f

    old = None
    for j in range(S + 1):
        now = outer[j % 3]
        if j > 0:
            here, before = field(j - 1), field(j - 2)

            def put(x, total):
                past = before(x) if j > 1 else None
                new = next_basis(j, diag(x), root(x), here(x), total, past)
                if j < S:
                    now[x] = new
                elif DEEP <= x < DEEP + nx:
                    now[x, DEEP : DEEP + ny] = new[DEEP : DEEP + ny]

            for lo, hi in ((j, low + j), (high_x - j, wide - j)):
                sweep(root, here, lo, hi, put)
        columns = slice(DEEP, DEEP + ny)
        own = jnp.concatenate(
            [
                now[DEEP : low + j, columns, :],
                frames[j, 1 + j : nx - 1 - j, columns, :],
                now[high_x - j : DEEP + nx, columns, :],
            ],
            axis=0,
        )
        high, rest = halves(own.reshape(nx * ny, LANES))
        rough[:, j * LANES : (j + 1) * LANES] = high
        fine[:, j * LANES : (j + 1) * LANES] = rest
        turned = high.T
        both = jnp.concatenate([high, rest], axis=1)
        left = turned if j == 0 else jnp.concatenate([turned, old[0]], axis=0)
        got = jnp.dot(left, both, preferred_element_type=jnp.float32)
        note(2 * j, got[:LANES, :LANES] + 2.0 * got[:LANES, LANES:])
        if j > 0:
            more = jnp.dot(turned, old[1], preferred_element_type=jnp.float32)
            note(2 * j - 1, got[LANES:, :LANES] + got[LANES:, LANES:] + more)
        old = (turned, rest)
    every = jnp.concatenate(folded, axis=0)
    shift = LANES // 2
    while shift >= NRHS:
        every = every + pltpu.roll(every, shift, 1)
        shift //= 2
    blocks = [every[n * NRHS : (n + 1) * NRHS] for n in range(2 * S + 1)]
    tile = jnp.zeros((NRHS, LANES), jnp.float32)
    row, col = rows_at((NRHS, LANES)), lanes_of((NRHS, LANES)) % NRHS
    last = blocks[2 * S]
    below = jnp.where(row == col + 1, pltpu.roll(last, 1, 0), 0.0)
    below = jnp.where((row == NRHS - 1) & (col == 0), pltpu.roll(last, 1, 1), below)
    blocks[0] = jnp.where(row <= col, blocks[0], last)
    blocks[1] = jnp.where(row <= col, blocks[1], below)
    for n in range(2 * S):
        tile = jnp.where(level == n, blocks[n], tile)
    moments[...] = jnp.broadcast_to(tile[None], moments.shape)


def moment_blocks(tile):
    depth = LANES // NRHS
    row, lane = rows_at((NRHS, LANES)), lanes_of((NRHS, LANES))
    raw = [tile] + [pltpu.roll(tile, LANES - NRHS * n, 1) for n in range(1, depth)]
    square = jnp.concatenate([tile, jnp.zeros((LANES - NRHS, LANES), jnp.float32)], axis=0).T
    turned = [square[n * NRHS : (n + 1) * NRHS] for n in range(depth)]
    first, second = raw[0], raw[1]
    last = jnp.where(row > lane, first, turned[0])
    last = jnp.where(row == lane, pltpu.roll(second, NRHS - 1, 0), last)
    last = jnp.where((row == NRHS - 1) & (lane == NRHS - 1), pltpu.roll(second, NRHS - 1, 1), last)
    even = [0.5 * (r + t) for r, t in zip(raw, turned)] + [last]
    even[0] = jnp.where(row <= lane, first, turned[0])
    even[1] = jnp.where(row <= lane, second, turned[1])
    even = [jnp.where(lane < NRHS, e, 0.0) for e in even]
    return even[:2] + [2.0 * even[n] - even[n % 2] for n in range(2, 2 * S + 1)]


def solve_small(m):
    lane = lanes_of((NRHS, LANES))
    half = HALF_WIDTH / 2
    size = S * NRHS

    def a_on(seq, n):
        return CENTRE * seq[n] + half * (seq[n + 1] + seq[abs(n - 1)])

    nu = [a_on(m, n) for n in range(2 * S)]
    mu = [a_on(nu, n) for n in range(2 * S - 1)]
    up = functools.reduce(jnp.add, [mu[n] if n == 0 else pltpu.roll(mu[n], NRHS * n, 1) for n in range(2 * S - 1)])
    around = functools.reduce(
        jnp.add,
        [mu[abs(n - (S - 1))] if n == 0 else pltpu.roll(mu[abs(n - (S - 1))], NRHS * n, 1) for n in range(2 * S - 1)],
    )

    def left(f, places):
        return f if places == 0 else pltpu.roll(f, LANES - places, 1)

    rows = []
    for c in range(S):
        both = 0.5 * (left(up, NRHS * c) + left(around, NRHS * (S - 1 - c)))
        rows.append(jnp.where(lane < size, both, pltpu.roll(nu[c], size, 1)))
    m = jnp.concatenate(rows, axis=0)
    row, col = rows_at((size, LANES)), lanes_of((size, LANES))
    on = row == col
    kept = jnp.where(on, m, 0.0)
    scale = 1.0 / jnp.sqrt(jnp.sum(kept, axis=1, keepdims=True))
    across = jnp.sum(kept, axis=0, keepdims=True)
    across = jnp.where(lanes_of((1, LANES)) < size, 1.0 / jnp.sqrt(across), 1.0)
    m = scale * m * across + jnp.where(on, RIDGE, 0.0)
    for first in range(0, size, PANEL):
        columns = [
            jnp.broadcast_to(m[:, i : i + 1], m.shape) for i in range(first, first + PANEL)
        ]
        for p in range(0, PANEL, 2):
            i = first + p
            c0, c1 = columns[p], columns[p + 1]
            a, b, d = c0[i : i + 1], c1[i : i + 1], c1[i + 1 : i + 2]
            inverse = 1.0 / (a * d - b * b)
            a, b, d = inverse * a, inverse * b, inverse * d
            d0 = jnp.where(row == i, c0 - 1.0, c0)
            d1 = jnp.where(row == i + 1, c1 - 1.0, c1)
            for later in range(p + 2, PANEL):
                r0 = c0[first + later : first + later + 1]
                r1 = c1[first + later : first + later + 1]
                columns[later] = columns[later] - d0 * (d * r0 - b * r1) - d1 * (a * r1 - b * r0)
            r0, r1 = m[i : i + 1], m[i + 1 : i + 2]
            m = m - d0 * (d * r0 - b * r1) - d1 * (a * r1 - b * r0)
    x = jnp.where((col >= size) & (col < size + NRHS), scale * m, 0.0)
    shift = NRHS
    while shift < LANES:
        x = x + pltpu.roll(x, shift, 1)
        shift *= 2
    c = [x[j * NRHS : (j + 1) * NRHS] for j in range(S)]
    unit = jnp.where(rows_at((NRHS, LANES)) == lane % NRHS, 1.0, 0.0)
    remain = []
    for j in range(S + 1):
        total = CENTRE * c[j] if j < S else 0.0
        if j > 0:
            total = total + (HALF_WIDTH if j == 1 else half) * c[j - 1]
        if j + 1 < S:
            total = total + half * c[j + 1]
        remain.append((unit if j == 0 else 0.0) - total)
    return c, remain


def combine_kernel(guess, rough, fine, parts, update, rest, wh, wl):
    nx, ny, _ = guess.shape
    level = lanes_of((NRHS, LANES)) // NRHS
    coeffs, remain = solve_small(moment_blocks(jnp.sum(parts[...], axis=0)))
    coeffs = coeffs + [jnp.zeros((NRHS, LANES), jnp.float32)]
    for part, tiles in ((0, coeffs), (1, remain)):
        for j in range(S + 1):
            full = jnp.concatenate(
                [jnp.where(level == z, tiles[j], 0.0) for z in range(LANES // NRHS)], axis=0
            )
            high, low = halves(full)
            wh[j * LANES : (j + 1) * LANES, part * LANES : (part + 1) * LANES] = high
            wl[j * LANES : (j + 1) * LANES, part * LANES : (part + 1) * LANES] = low
    chunk = nx // 4
    for i in range(4):
        at = slice(i * chunk, (i + 1) * chunk)
        cells = slice(i * chunk * ny, (i + 1) * chunk * ny)
        dot = functools.partial(jnp.dot, preferred_element_type=jnp.float32)
        out = dot(rough[cells], wh[...]) + dot(rough[cells], wl[...]) + dot(fine[cells], wh[...])
        out = out.reshape(chunk, ny, 2 * LANES)
        update[at] = guess[at] + out[:, :, :LANES]
        rest[at] = out[:, :, LANES:]


def call(kernel, ins, outs, scratch=(), scalars=0, kinds=None, space=pltpu.VMEM, limit=VMEM_BYTES):
    specs = [pl.BlockSpec(memory_space=pltpu.SMEM)] * scalars
    specs += [pl.BlockSpec(memory_space=space)] * (len(ins) - scalars)
    result = pl.pallas_call(
        kernel,
        out_shape=[
            jax.ShapeDtypeStruct(s, k) for s, k in zip(outs, kinds or [jnp.float32] * len(outs))
        ],
        in_specs=specs,
        out_specs=[pl.BlockSpec(memory_space=pltpu.VMEM)] * len(outs),
        scratch_shapes=list(scratch),
        compiler_params=pltpu.CompilerParams(vmem_limit_bytes=limit),
    )(*ins)
    return result


def exchange(first, second, axis):
    count = lax.axis_size(axis)
    got = []
    for cells, start in ((first, 0), (second, 1)):
        links = []
        for i in range(start, count - 1, 2):
            links += [(i, i + 1), (i + 1, i)]
        got.append(lax.ppermute(cells, axis, links))
    return got


def total_of(x, axis):
    count = lax.axis_size(axis)
    if count & (count - 1):
        return lax.psum(x, axis)
    step = 1
    while step < count:
        x = x + lax.ppermute(x, axis, [(i, i ^ step) for i in range(count)])
        step *= 2
    return x


def totals(parts):
    count = parts.shape[0]
    if count > 1:
        return lax.all_to_all(parts, ("gx", "gy"), 0, 0)
    return total_of(total_of(parts, "gy"), "gx")


def body(initial_guess, source, leaf_density, absorption):
    nx, ny, lanes = initial_guess.shape
    cells = jnp.transpose(jnp.stack([leaf_density, absorption]), (0, 2, 3, 1))
    depth = cells.shape[2]
    px = lax.rem(lax.axis_index("gx"), 2).astype(jnp.int32).reshape(1)
    py = lax.rem(lax.axis_index("gy"), 2).astype(jnp.int32).reshape(1)
    wide = nx + 2 * DEEP
    tall = ny + 2 * DEEP
    block = (nx, ny, lanes)
    across = ny * depth
    x_rows = DEEP * ny + ny + 2 * DEEP + 8 + 2 * DEEP * (across // lanes)
    side_rows = (nx - 2) * DEEP + 3 * nx
    y_rows = 2 * (DEEP + 1) * DEEP + 6 * DEEP + 8
    sides = ((2, nx, lanes), (2, ny, lanes))
    root, absb, b0, rim, edge, face, xa, xb, sa, sb = call(
        begin_kernel,
        (px, py, initial_guess, source, cells),
        ((nx, across), (nx, across), block, sides[1], *sides)
        + ((x_rows, lanes),) * 2
        + ((side_rows, lanes),) * 2,
        scratch=[
            pltpu.VMEM(block, jnp.float32),
            pltpu.VMEM(block, jnp.float32),
            pltpu.VMEM(cells.shape, jnp.float32),
            pltpu.VMEM(block, jnp.float32),
            pltpu.VMEM(block, jnp.float32),
            pltpu.SemaphoreType.DMA((3,)),
        ],
        scalars=2,
        space=pltpu.HBM,
        limit=BEGIN_BYTES,
    )
    xa, xb = exchange(xa, xb, "gx")
    sa, sb = exchange(sa, sb, "gy")
    root_h, abs_h, band, edges, ya, yb = call(
        widen_kernel,
        (px, py, xa, xb, edge, face, root, absb, rim),
        ((2, DEEP, across),) * 2
        + ((2, DEEP + 1, ny, lanes), (2, wide + 8, lanes))
        + ((y_rows, lanes),) * 2,
        scratch=[pltpu.VMEM((2, ny, lanes), jnp.float32)],
        scalars=2,
    )
    ya, yb = exchange(ya, yb, "gy")
    inner = (nx, tall, lanes)
    root_i, diag_i, frames, far = call(
        inner_kernel,
        (py, sa, sb, root, absb, b0, edge),
        (inner, inner, (S + 1, *inner), sides[0]),
        scalars=1,
    )
    frame = pltpu.VMEM((wide, tall, lanes), jnp.float32)
    halo = pltpu.VMEM((2 * DEEP, tall, lanes), jnp.float32)
    count = lax.axis_size("gx") * lax.axis_size("gy")
    count = count if count <= 64 else 1
    cells = nx * ny
    rough, fine, moments = call(
        basis_kernel,
        (py, ya, yb, root_h, abs_h, band, edges, root_i, diag_i, frames, far),
        ((cells, (S + 1) * lanes), (cells, (S + 1) * lanes), (count, NRHS, lanes)),
        scratch=[halo, halo, pltpu.VMEM((2, wide + 8, lanes), jnp.float32), frame, frame, frame],
        scalars=1,
        kinds=(jnp.bfloat16, jnp.bfloat16, jnp.float32),
    )
    return call(
        combine_kernel,
        (initial_guess, rough, fine, totals(moments)),
        (block, block),
        scratch=[pltpu.VMEM(((S + 1) * lanes, 2 * lanes), jnp.bfloat16)] * 2,
    )


def solution(mesh):
    spec = P("gx", "gy", None)
    return jax.shard_map(
        lambda *arrays: tuple(body(*arrays)),
        mesh=mesh,
        in_specs=(spec,) * 4,
        out_specs=(spec, spec),
        check_vma=False,
    )
```

```python
import functools

import jax
import jax.numpy as jnp
from jax import lax
from jax.experimental import pallas as pl
from jax.experimental.pallas import tpu as pltpu
from jax.sharding import PartitionSpec as P

NRHS = 8
S = 8
DEEP = S
LANES = 128

PEAK_COND = 0.6
CENTRE = 10.3
HALF_WIDTH = 9.8
RIDGE = 0.05
PANEL = 16
ROOT_SCALE = (2.0 / HALF_WIDTH) ** 0.5
VMEM_BYTES = 24 * 1024 * 1024
BEGIN_BYTES = 54300 * 1024


def lanes_of(shape):
    return lax.broadcasted_iota(jnp.int32, shape, len(shape) - 1)


def rows_at(shape):
    return lax.broadcasted_iota(jnp.int32, shape, len(shape) - 2)


def z_sum(f):
    lane = lanes_of(f.shape)
    ax = f.ndim - 1
    up = jnp.where(lane >= NRHS, pltpu.roll(f, NRHS, ax), 0.0)
    down = jnp.where(lane < LANES - NRHS, pltpu.roll(f, LANES - NRHS, ax), 0.0)
    return up + down


def row_sum(f):
    n = f.shape[-2]
    ax = f.ndim - 2
    return pltpu.roll(f, 1, ax) + pltpu.roll(f, n - 1, ax)


def row_sum_zero(f):
    n = f.shape[-2]
    ax = f.ndim - 2
    row = rows_at(f.shape)
    up = jnp.where(row >= 1, pltpu.roll(f, 1, ax), 0.0)
    down = jnp.where(row < n - 1, pltpu.roll(f, n - 1, ax), 0.0)
    return up + down


def slab_sum(before, here, after, rows):
    ux = before[0] + after[0]
    px = before[1] + after[1]
    s = here[1] + ux
    q = here[0] + 0.5 * s + (1.0 / 3.0) * px
    return s + 0.5 * px + rows(q)


def cross_sum(f, rows):
    p = z_sum(f)
    return f + 0.5 * p + rows(0.5 * f + (1.0 / 3.0) * p)


def spread(rows):
    n = rows.shape[0]
    depth = LANES // NRHS
    at = rows_at((NRHS, LANES)) * depth + lanes_of((NRHS, LANES)) // NRHS
    out = []
    for x in range(n):
        line = jnp.broadcast_to(rows[x : x + 1], (NRHS, LANES))
        out.append(jnp.take_along_axis(line, at, axis=1))
    return jnp.stack(out)


def begin_kernel(px, py, *refs):
    far, refs = refs[:3], refs[3:]
    (root_o, abs_o, b0_o, rim_o, edge_o, face_o), refs = refs[:6], refs[6:]
    (send_a, send_b, side_a, side_b), refs = refs[:4], refs[4:]
    guess, source, pair_in, root, absb, sems = refs
    copies = [
        pltpu.make_async_copy(there, here, sems.at[i])
        for i, (there, here) in enumerate(zip(far, (guess, source, pair_in)))
    ]
    for i in (2, 0, 1):
        copies[i].start()
    nx, ny, _ = guess.shape
    depth = pair_in.shape[2]
    copies[2].wait()
    turned = jnp.transpose(pair_in[0].reshape(ny * depth, nx))
    root_o[...] = jnp.sqrt(PEAK_COND / (1.0 + turned))
    abs_o[...] = jnp.transpose(pair_in[1].reshape(ny * depth, nx))
    for part, wide in ((root_o, root), (abs_o, absb)):
        for y in range(0, ny, NRHS):
            wide[:, y : y + NRHS, :] = spread(part[:, y * depth : (y + NRHS) * depth])
    copies[0].wait()
    copies[1].wait()
    for at, col, face in ((0, 0, 0), (1, ny - 1, nx - 1)):
        edge_o[at] = guess[:, col, :]
        face_o[at] = guess[face]
    zero = jnp.zeros((ny, LANES), jnp.float32)

    def pair(x, field):
        if x < 0 or x >= nx:
            return (zero, zero)
        u = root[x] if field is None else root[x] * field[x]
        return (u, z_sum(u))

    moving = [pair(-1, guess), pair(0, guess)]
    still = [pair(-1, None), pair(0, None)]
    for x in range(nx):
        moving.append(pair(x + 1, guess))
        still.append(pair(x + 1, None))
        wu = slab_sum(*moving, row_sum_zero)
        wr = slab_sum(*still, row_sum_zero)
        moving, still = moving[1:], still[1:]
        v = guess[x]
        b0_o[x] = source[x] - absb[x] * v + root[x] * (wu - v * wr)

    rim_o[0] = b0_o[0]
    rim_o[1] = b0_o[nx - 1]

    def write(out, x0, face, beyond):
        n = DEEP * ny
        out[0:n] = b0_o[x0 : x0 + DEEP].reshape(n, LANES)
        out[n : n + ny] = guess[face]
        n += ny
        for col in (0, ny - 1):
            out[n : n + DEEP] = guess[x0 : x0 + DEEP, col, :]
            n += DEEP
        out[n : n + 8] = jnp.zeros((8, LANES), jnp.float32)
        for at, col in ((0, 0), (1, ny - 1)):
            out[n + at : n + at + 1] = guess[beyond, col : col + 1, :]
            out[n + 2 + at : n + 3 + at] = root[beyond, col : col + 1, :]
        n += 8
        for part in (root_o, abs_o):
            for first in range(0, ny * depth, LANES):
                out[n : n + DEEP] = part[x0 : x0 + DEEP, first : first + LANES]
                n += DEEP

    @pl.when(px[0] == 0)
    def _():
        write(send_a, nx - DEEP, nx - 1, nx - DEEP - 1)
        write(send_b, 0, 0, DEEP)

    @pl.when(px[0] == 1)
    def _():
        write(send_b, nx - DEEP, nx - 1, nx - DEEP - 1)
        write(send_a, 0, 0, DEEP)

    def write_side(out, y0, at):
        n = (nx - 2) * DEEP
        out[0:n] = b0_o[1 : nx - 1, y0 : y0 + DEEP, :].reshape(n, LANES)
        out[n : n + nx] = edge_o[at]
        n += nx
        for part in (root_o, abs_o):
            out[n : n + nx] = part[:, y0 * depth : (y0 + DEEP) * depth]
            n += nx

    @pl.when(py[0] == 0)
    def _():
        write_side(side_a, ny - DEEP, 1)
        write_side(side_b, 0, 0)

    @pl.when(py[0] == 1)
    def _():
        write_side(side_b, ny - DEEP, 1)
        write_side(side_a, 0, 0)


def widen_kernel(
    px, py, recv_a, recv_b, edge_own, face_own, root, absb, rim,
    root_h, abs_h, band, edge, send_a, send_b, face
):
    nx, ny = edge_own.shape[1], face_own.shape[1]
    wide = nx + 2 * DEEP
    for at in (0, 1):
        edge[at, DEEP : DEEP + nx] = edge_own[at]
        edge[at, wide : wide + 8] = jnp.zeros((8, LANES), jnp.float32)

    def read(msg, x0, side):
        n = DEEP * ny
        band[side, side : side + DEEP] = msg[0:n].reshape(DEEP, ny, LANES)
        face[side] = msg[n : n + ny]
        n += ny
        for at in (0, 1):
            edge[at, x0 : x0 + DEEP] = msg[n : n + DEEP]
            n += DEEP
        for at in (0, 1):
            edge[at, wide + side : wide + side + 1] = msg[n + at : n + at + 1]
            edge[at, wide + 2 + side : wide + 3 + side] = msg[n + 2 + at : n + 3 + at]
        n += 8
        for out in (root_h, abs_h):
            for first in range(0, out.shape[2], LANES):
                out[side, :, first : first + LANES] = msg[n : n + DEEP]
                n += DEEP

    @pl.when(px[0] == 0)
    def _():
        read(recv_b, 0, 0)
        read(recv_a, DEEP + nx, 1)

    @pl.when(px[0] == 1)
    def _():
        read(recv_a, 0, 0)
        read(recv_b, DEEP + nx, 1)

    def line(rows):
        parts = [spread(rows[:, at : at + LANES]) for at in range(0, rows.shape[1], LANES)]
        return jnp.concatenate(parts, axis=1)[0]

    for side, out_x, in_x, far_x, near_x in (
        (0, DEEP - 1, DEEP, DEEP - 1, 0),
        (1, 1, 0, 0, nx - 1),
    ):
        va, ra = face[side], line(root_h[side, far_x : far_x + 1])
        vb, rb = face_own[side], line(root[near_x : near_x + 1])
        fix_a = ra * (cross_sum(rb * vb, row_sum_zero) - va * cross_sum(rb, row_sum_zero))
        fix_b = rb * (cross_sum(ra * va, row_sum_zero) - vb * cross_sum(ra, row_sum_zero))
        band[side, out_x] = band[side, out_x] + fix_a
        band[side, in_x] = rim[side] + fix_b

    def write(out, y0, at):
        n = 0
        for side in (0, 1):
            m = (DEEP + 1) * DEEP
            out[n : n + m] = band[side, :, y0 : y0 + DEEP, :].reshape(m, LANES)
            n += m
        first = y0 * (LANES // NRHS)
        for side, x0 in ((0, 0), (1, DEEP + nx)):
            out[n : n + DEEP] = edge[at, x0 : x0 + DEEP]
            n += DEEP
            for part in (root_h, abs_h):
                out[n : n + DEEP] = part[side, :, first : first + LANES]
                n += DEEP
        out[n : n + 8] = edge[at, wide : wide + 8]

    @pl.when(py[0] == 0)
    def _():
        write(send_a, ny - DEEP, 1)
        write(send_b, 0, 0)

    @pl.when(py[0] == 1)
    def _():
        write(send_b, ny - DEEP, 1)
        write(send_a, 0, 0)


def halves(a):
    high = a.astype(jnp.bfloat16)
    return high, (a - high.astype(jnp.float32)).astype(jnp.bfloat16)


def sweep(root, field, lo, hi, put):
    def pair(x):
        u = root(x) if field is None else root(x) * field(x)
        return (u, z_sum(u))

    first, second = pair(lo - 1), pair(lo)
    for x in range(lo, hi):
        third = pair(x + 1)
        put(x, slab_sum(first, second, third, row_sum))
        first, second = second, third


def final_diag(raw, root, total):
    return (raw - CENTRE) * (2.0 / HALF_WIDTH) + root * total


def next_basis(j, diag, root, here, total, before):
    new = diag * here - root * total
    return 0.5 * new if j == 1 else new - before


def inner_kernel(py, side_a, side_b, root_own, abs_own, b0, edge, root, diag, frames, far):
    nx, ny, _ = b0.shape
    for part, out, factor in ((root_own, root, ROOT_SCALE), (abs_own, diag, 1.0)):
        for y in range(0, ny, DEEP):
            first = y * (LANES // NRHS)
            some = factor * part[:, first : first + LANES]
            out[:, DEEP + y : 2 * DEEP + y, :] = spread(some)
    inner = slice(1, nx - 1)
    frames[0, inner, DEEP : DEEP + ny, :] = b0[inner]

    def read(msg, y0, side):
        n = (nx - 2) * DEEP
        frames[0, inner, y0 : y0 + DEEP, :] = msg[0:n].reshape(nx - 2, DEEP, LANES)
        far[side] = msg[n : n + nx]
        n += nx
        for out, factor in ((root, ROOT_SCALE), (diag, 1.0)):
            out[:, y0 : y0 + DEEP, :] = spread(factor * msg[n : n + nx])
            n += nx

    @pl.when(py[0] == 0)
    def _():
        read(side_b, 0, 0)
        read(side_a, DEEP + ny, 1)

    @pl.when(py[0] == 1)
    def _():
        read(side_a, 0, 0)
        read(side_b, DEEP + ny, 1)

    def column(v, y):
        r = root[:, y, :]
        return v, r, cross_sum(r * v, row_sum), cross_sum(r, row_sum)

    for side, out_y, in_y in ((0, DEEP - 1, DEEP), (1, DEEP + ny, DEEP + ny - 1)):
        va, ra, ua, wa = column(far[side], out_y)
        vb, rb, ub, wb = column(edge[side], in_y)
        for y, fix in ((out_y, ra * (ub - va * wb)), (in_y, rb * (ua - vb * wa))):
            fix = fix * (HALF_WIDTH / 2)
            frames[0, inner, y, :] = frames[0, inner, y, :] + fix[inner]

    def put_diag(x, total):
        diag[x] = final_diag(diag[x], root[x], total)

    sweep(lambda x: root[x], None, 1, nx - 1, put_diag)
    for j in range(1, S + 1):

        def put(x, total):
            before = frames[j - 2, x] if j > 1 else None
            new = next_basis(j, diag[x], root[x], frames[j - 1, x], total, before)
            if j < S:
                frames[j, x] = new
            else:
                frames[j, x, DEEP : DEEP + ny] = new[DEEP : DEEP + ny]

        sweep(lambda x: root[x], lambda x: frames[j - 1, x], 1 + j, nx - 1 - j, put)


def basis_kernel(
    py, recv_a, recv_b, root_h, abs_h, band, edge, root_i, diag_i, frames, far_own,
    rough, fine, moments, root_o, diag_o, far, f0, f1, f2
):
    _, nx, tall, _ = frames.shape
    ny = tall - 2 * DEEP
    wide = nx + 2 * DEEP
    low, high_x = DEEP + 1, DEEP + nx - 1
    for side in (0, 1):
        rows = slice(side * DEEP, (side + 1) * DEEP)
        for y in range(0, ny, DEEP):
            first = y * (LANES // NRHS)
            for part, out, factor in ((root_h, root_o, ROOT_SCALE), (abs_h, diag_o, 1.0)):
                some = factor * part[side, :, first : first + LANES]
                out[rows, DEEP + y : 2 * DEEP + y, :] = spread(some)
        far[side, DEEP : DEEP + nx] = far_own[side]
    f0[0:low, DEEP : DEEP + ny, :] = band[0]
    f0[high_x:wide, DEEP : DEEP + ny, :] = band[1]

    def read(msg, y0, side):
        n = 0
        for x0 in (0, high_x):
            m = (DEEP + 1) * DEEP
            f0[x0 : x0 + DEEP + 1, y0 : y0 + DEEP, :] = msg[n : n + m].reshape(
                DEEP + 1, DEEP, LANES
            )
            n += m
        for at, x0 in ((0, 0), (DEEP, DEEP + nx)):
            far[side, x0 : x0 + DEEP] = msg[n : n + DEEP]
            n += DEEP
            for out, factor in ((root_o, ROOT_SCALE), (diag_o, 1.0)):
                out[at : at + DEEP, y0 : y0 + DEEP, :] = spread(factor * msg[n : n + DEEP])
                n += DEEP
        far[side, wide : wide + 8] = msg[n : n + 8]

    @pl.when(py[0] == 0)
    def _():
        read(recv_b, 0, 0)
        read(recv_a, DEEP + ny, 1)

    @pl.when(py[0] == 1)
    def _():
        read(recv_a, 0, 0)
        read(recv_b, DEEP + ny, 1)

    row = lax.broadcasted_iota(jnp.int32, (wide, LANES), 0)

    def across(f, before, after):
        p = z_sum(f)
        ends = jnp.concatenate([before, after], axis=0)
        ends = 0.5 * ends + (1.0 / 3.0) * z_sum(ends)
        g = 0.5 * f + (1.0 / 3.0) * p
        up = jnp.where(row == 0, ends[0:1], pltpu.roll(g, 1, 0))
        down = jnp.where(row == wide - 1, ends[1:2], pltpu.roll(g, wide - 1, 0))
        return f + 0.5 * p + up + down

    def column(ref, at, y):
        v = ref[at, 0:wide]
        ends = ref[at, wide : wide + 8]
        r = jnp.concatenate([root_o[0:DEEP, y, :], root_i[:, y, :], root_o[DEEP:, y, :]], axis=0)
        r0, r1 = ROOT_SCALE * ends[2:3], ROOT_SCALE * ends[3:4]
        return v, r, across(r * v, r0 * ends[0:1], r1 * ends[1:2]), across(r, r0, r1)

    for side, out_y, in_y in ((0, DEEP - 1, DEEP), (1, DEEP + ny, DEEP + ny - 1)):
        va, ra, ua, wa = column(far, side, out_y)
        vb, rb, ub, wb = column(edge, side, in_y)
        for y, fix in ((out_y, ra * (ub - va * wb)), (in_y, rb * (ua - vb * wa))):
            fix = fix * (HALF_WIDTH / 2)
            f0[0:low, y, :] = f0[0:low, y, :] + fix[0:low]
            f0[high_x:wide, y, :] = f0[high_x:wide, y, :] + fix[high_x:wide]

    outer = [f0, f1, f2]

    def root(x):
        if DEEP <= x < DEEP + nx:
            return root_i[x - DEEP]
        return root_o[x if x < DEEP else x - nx]

    def field(j):
        def at(x):
            if low + j <= x < high_x - j:
                return frames[j, x - DEEP]
            return outer[j % 3][x]

        return at

    edges = {}

    def diag(x):
        if low <= x < high_x:
            return diag_i[x - DEEP]
        if x in (DEEP, DEEP + nx - 1):
            return diag_e[0 if x == DEEP else 1]
        return diag_o[x if x < DEEP else x - nx]

    def put_diag(x, total):
        if DEEP <= x < DEEP + nx:
            edges[x] = final_diag(diag_i[x - DEEP], root(x), total)
        else:
            at = x if x < DEEP else x - nx
            diag_o[at] = final_diag(diag_o[at], root(x), total)

    for lo, hi in ((1, low), (high_x, wide - 1)):
        sweep(root, None, lo, hi, put_diag)
    diag_e = (edges[DEEP], edges[DEEP + nx - 1])

    level = lanes_of((NRHS, LANES)) // NRHS
    depth = LANES // NRHS
    folded = [None] * (2 * S + 1)

    def note(n, block):
        if n in (0, 1, 2 * S):
            block = 0.5 * (block + block.T)
        f = block[0:NRHS]
        for z in range(1, depth):
            f = jnp.where(level == z, block[z * NRHS : (z + 1) * NRHS], f)
        folded[n] = f

    old = None
    for j in range(S + 1):
        now = outer[j % 3]
        if j > 0:
            here, before = field(j - 1), field(j - 2)

            def put(x, total):
                past = before(x) if j > 1 else None
                new = next_basis(j, diag(x), root(x), here(x), total, past)
                if j < S:
                    now[x] = new
                elif DEEP <= x < DEEP + nx:
                    now[x, DEEP : DEEP + ny] = new[DEEP : DEEP + ny]

            for lo, hi in ((j, low + j), (high_x - j, wide - j)):
                sweep(root, here, lo, hi, put)
        columns = slice(DEEP, DEEP + ny)
        own = jnp.concatenate(
            [
                now[DEEP : low + j, columns, :],
                frames[j, 1 + j : nx - 1 - j, columns, :],
                now[high_x - j : DEEP + nx, columns, :],
            ],
            axis=0,
        )
        high, rest = halves(own.reshape(nx * ny, LANES))
        rough[:, j * LANES : (j + 1) * LANES] = high
        fine[:, j * LANES : (j + 1) * LANES] = rest
        turned = high.T
        both = jnp.concatenate([high, rest], axis=1)
        left = turned if j == 0 else jnp.concatenate([turned, old[0]], axis=0)
        got = jnp.dot(left, both, preferred_element_type=jnp.float32)
        note(2 * j, got[:LANES, :LANES] + 2.0 * got[:LANES, LANES:])
        if j > 0:
            more = jnp.dot(turned, old[1], preferred_element_type=jnp.float32)
            note(2 * j - 1, got[LANES:, :LANES] + got[LANES:, LANES:] + more)
        old = (turned, rest)
    every = jnp.concatenate(folded, axis=0)
    shift = LANES // 2
    while shift >= NRHS:
        every = every + pltpu.roll(every, shift, 1)
        shift //= 2
    blocks = [every[n * NRHS : (n + 1) * NRHS] for n in range(2 * S + 1)]
    tile = jnp.zeros((NRHS, LANES), jnp.float32)
    row, col = rows_at((NRHS, LANES)), lanes_of((NRHS, LANES)) % NRHS
    last = blocks[2 * S]
    below = jnp.where(row == col + 1, pltpu.roll(last, 1, 0), 0.0)
    below = jnp.where((row == NRHS - 1) & (col == 0), pltpu.roll(last, 1, 1), below)
    blocks[0] = jnp.where(row <= col, blocks[0], last)
    blocks[1] = jnp.where(row <= col, blocks[1], below)
    for n in range(2 * S):
        tile = jnp.where(level == n, blocks[n], tile)
    moments[...] = jnp.broadcast_to(tile[None], moments.shape)


def moment_blocks(tile):
    depth = LANES // NRHS
    row, lane = rows_at((NRHS, LANES)), lanes_of((NRHS, LANES))
    raw = [tile] + [pltpu.roll(tile, LANES - NRHS * n, 1) for n in range(1, depth)]
    square = jnp.concatenate([tile, jnp.zeros((LANES - NRHS, LANES), jnp.float32)], axis=0).T
    turned = [square[n * NRHS : (n + 1) * NRHS] for n in range(depth)]
    first, second = raw[0], raw[1]
    last = jnp.where(row > lane, first, turned[0])
    last = jnp.where(row == lane, pltpu.roll(second, NRHS - 1, 0), last)
    last = jnp.where((row == NRHS - 1) & (lane == NRHS - 1), pltpu.roll(second, NRHS - 1, 1), last)
    even = [0.5 * (r + t) for r, t in zip(raw, turned)] + [last]
    even[0] = jnp.where(row <= lane, first, turned[0])
    even[1] = jnp.where(row <= lane, second, turned[1])
    even = [jnp.where(lane < NRHS, e, 0.0) for e in even]
    return even[:2] + [2.0 * even[n] - even[n % 2] for n in range(2, 2 * S + 1)]


def solve_small(m):
    lane = lanes_of((NRHS, LANES))
    half = HALF_WIDTH / 2
    size = S * NRHS

    def a_on(seq, n):
        return CENTRE * seq[n] + half * (seq[n + 1] + seq[abs(n - 1)])

    nu = [a_on(m, n) for n in range(2 * S)]
    mu = [a_on(nu, n) for n in range(2 * S - 1)]
    up = functools.reduce(jnp.add, [mu[n] if n == 0 else pltpu.roll(mu[n], NRHS * n, 1) for n in range(2 * S - 1)])
    around = functools.reduce(
        jnp.add,
        [mu[abs(n - (S - 1))] if n == 0 else pltpu.roll(mu[abs(n - (S - 1))], NRHS * n, 1) for n in range(2 * S - 1)],
    )

    def left(f, places):
        return f if places == 0 else pltpu.roll(f, LANES - places, 1)

    rows = []
    for c in range(S):
        both = 0.5 * (left(up, NRHS * c) + left(around, NRHS * (S - 1 - c)))
        rows.append(jnp.where(lane < size, both, pltpu.roll(nu[c], size, 1)))
    m = jnp.concatenate(rows, axis=0)
    row, col = rows_at((size, LANES)), lanes_of((size, LANES))
    on = row == col
    kept = jnp.where(on, m, 0.0)
    scale = 1.0 / jnp.sqrt(jnp.sum(kept, axis=1, keepdims=True))
    across = jnp.sum(kept, axis=0, keepdims=True)
    across = jnp.where(lanes_of((1, LANES)) < size, 1.0 / jnp.sqrt(across), 1.0)
    m = scale * m * across + jnp.where(on, RIDGE, 0.0)
    for first in range(0, size, PANEL):
        columns = [
            jnp.broadcast_to(m[:, i : i + 1], m.shape) for i in range(first, first + PANEL)
        ]
        for p in range(0, PANEL, 2):
            i = first + p
            c0, c1 = columns[p], columns[p + 1]
            a, b, d = c0[i : i + 1], c1[i : i + 1], c1[i + 1 : i + 2]
            inverse = 1.0 / (a * d - b * b)
            a, b, d = inverse * a, inverse * b, inverse * d
            d0 = jnp.where(row == i, c0 - 1.0, c0)
            d1 = jnp.where(row == i + 1, c1 - 1.0, c1)
            for later in range(p + 2, PANEL):
                r0 = c0[first + later : first + later + 1]
                r1 = c1[first + later : first + later + 1]
                columns[later] = columns[later] - d0 * (d * r0 - b * r1) - d1 * (a * r1 - b * r0)
            r0, r1 = m[i : i + 1], m[i + 1 : i + 2]
            m = m - d0 * (d * r0 - b * r1) - d1 * (a * r1 - b * r0)
    x = jnp.where((col >= size) & (col < size + NRHS), scale * m, 0.0)
    shift = NRHS
    while shift < LANES:
        x = x + pltpu.roll(x, shift, 1)
        shift *= 2
    c = [x[j * NRHS : (j + 1) * NRHS] for j in range(S)]
    unit = jnp.where(rows_at((NRHS, LANES)) == lane % NRHS, 1.0, 0.0)
    remain = []
    for j in range(S + 1):
        total = CENTRE * c[j] if j < S else 0.0
        if j > 0:
            total = total + (HALF_WIDTH if j == 1 else half) * c[j - 1]
        if j + 1 < S:
            total = total + half * c[j + 1]
        remain.append((unit if j == 0 else 0.0) - total)
    return c, remain


def combine_kernel(guess, rough, fine, parts, update, rest, wh, wl):
    nx, ny, _ = guess.shape
    level = lanes_of((NRHS, LANES)) // NRHS
    coeffs, remain = solve_small(moment_blocks(jnp.sum(parts[...], axis=0)))
    coeffs = coeffs + [jnp.zeros((NRHS, LANES), jnp.float32)]
    for part, tiles in ((0, coeffs), (1, remain)):
        for j in range(S + 1):
            full = jnp.concatenate(
                [jnp.where(level == z, tiles[j], 0.0) for z in range(LANES // NRHS)], axis=0
            )
            high, low = halves(full)
            wh[j * LANES : (j + 1) * LANES, part * LANES : (part + 1) * LANES] = high
            wl[j * LANES : (j + 1) * LANES, part * LANES : (part + 1) * LANES] = low
    chunk = nx // 4
    for i in range(4):
        at = slice(i * chunk, (i + 1) * chunk)
        cells = slice(i * chunk * ny, (i + 1) * chunk * ny)
        dot = functools.partial(jnp.dot, preferred_element_type=jnp.float32)
        out = dot(rough[cells], wh[...]) + dot(rough[cells], wl[...]) + dot(fine[cells], wh[...])
        out = out.reshape(chunk, ny, 2 * LANES)
        update[at] = guess[at] + out[:, :, :LANES]
        rest[at] = out[:, :, LANES:]


def call(kernel, ins, outs, scratch=(), scalars=0, kinds=None, space=pltpu.VMEM, limit=VMEM_BYTES):
    specs = [pl.BlockSpec(memory_space=pltpu.SMEM)] * scalars
    specs += [pl.BlockSpec(memory_space=space)] * (len(ins) - scalars)
    result = pl.pallas_call(
        kernel,
        out_shape=[
            jax.ShapeDtypeStruct(s, k) for s, k in zip(outs, kinds or [jnp.float32] * len(outs))
        ],
        in_specs=specs,
        out_specs=[pl.BlockSpec(memory_space=pltpu.VMEM)] * len(outs),
        scratch_shapes=list(scratch),
        compiler_params=pltpu.CompilerParams(vmem_limit_bytes=limit),
    )(*ins)
    return result


def exchange(first, second, axis):
    count = lax.axis_size(axis)
    got = []
    order = ((first, 0), (second, 1))
    for cells, start in order[::-1] if axis == "gx" else order:
        links = []
        for i in range(start, count - 1, 2):
            links += [(i, i + 1), (i + 1, i)]
        got.append(lax.ppermute(cells, axis, links))
    return got[::-1] if axis == "gx" else got


def total_of(x, axis):
    count = lax.axis_size(axis)
    if count & (count - 1):
        return lax.psum(x, axis)
    step = 1
    while step < count:
        x = x + lax.ppermute(x, axis, [(i, i ^ step) for i in range(count)])
        step *= 2
    return x


def totals(parts):
    count = parts.shape[0]
    if count > 1:
        return lax.all_to_all(parts, ("gx", "gy"), 0, 0)
    return total_of(total_of(parts, "gy"), "gx")


def body(initial_guess, source, leaf_density, absorption):
    nx, ny, lanes = initial_guess.shape
    cells = jnp.transpose(jnp.stack([leaf_density, absorption]), (0, 2, 3, 1))
    depth = cells.shape[2]
    px = lax.rem(lax.axis_index("gx"), 2).astype(jnp.int32).reshape(1)
    py = lax.rem(lax.axis_index("gy"), 2).astype(jnp.int32).reshape(1)
    wide = nx + 2 * DEEP
    tall = ny + 2 * DEEP
    block = (nx, ny, lanes)
    across = ny * depth
    x_rows = DEEP * ny + ny + 2 * DEEP + 8 + 2 * DEEP * (across // lanes)
    side_rows = (nx - 2) * DEEP + 3 * nx
    y_rows = 2 * (DEEP + 1) * DEEP + 6 * DEEP + 8
    sides = ((2, nx, lanes), (2, ny, lanes))
    root, absb, b0, rim, edge, face, xa, xb, sa, sb = call(
        begin_kernel,
        (px, py, initial_guess, source, cells),
        ((nx, across), (nx, across), block, sides[1], *sides)
        + ((x_rows, lanes),) * 2
        + ((side_rows, lanes),) * 2,
        scratch=[
            pltpu.VMEM(block, jnp.float32),
            pltpu.VMEM(block, jnp.float32),
            pltpu.VMEM(cells.shape, jnp.float32),
            pltpu.VMEM(block, jnp.float32),
            pltpu.VMEM(block, jnp.float32),
            pltpu.SemaphoreType.DMA((3,)),
        ],
        scalars=2,
        space=pltpu.HBM,
        limit=BEGIN_BYTES,
    )
    xa, xb = exchange(xa, xb, "gx")
    sa, sb = exchange(sa, sb, "gy")
    root_h, abs_h, band, edges, ya, yb = call(
        widen_kernel,
        (px, py, xa, xb, edge, face, root, absb, rim),
        ((2, DEEP, across),) * 2
        + ((2, DEEP + 1, ny, lanes), (2, wide + 8, lanes))
        + ((y_rows, lanes),) * 2,
        scratch=[pltpu.VMEM((2, ny, lanes), jnp.float32)],
        scalars=2,
    )
    ya, yb = exchange(ya, yb, "gy")
    inner = (nx, tall, lanes)
    root_i, diag_i, frames, far = call(
        inner_kernel,
        (py, sa, sb, root, absb, b0, edge),
        (inner, inner, (S + 1, *inner), sides[0]),
        scalars=1,
    )
    frame = pltpu.VMEM((wide, tall, lanes), jnp.float32)
    halo = pltpu.VMEM((2 * DEEP, tall, lanes), jnp.float32)
    count = lax.axis_size("gx") * lax.axis_size("gy")
    count = count if count <= 64 else 1
    cells = nx * ny
    rough, fine, moments = call(
        basis_kernel,
        (py, ya, yb, root_h, abs_h, band, edges, root_i, diag_i, frames, far),
        ((cells, (S + 1) * lanes), (cells, (S + 1) * lanes), (count, NRHS, lanes)),
        scratch=[halo, halo, pltpu.VMEM((2, wide + 8, lanes), jnp.float32), frame, frame, frame],
        scalars=1,
        kinds=(jnp.bfloat16, jnp.bfloat16, jnp.float32),
    )
    return call(
        combine_kernel,
        (initial_guess, rough, fine, totals(moments)),
        (block, block),
        scratch=[pltpu.VMEM(((S + 1) * lanes, 2 * lanes), jnp.bfloat16)] * 2,
    )


def solution(mesh):
    spec = P("gx", "gy", None)
    return jax.shard_map(
        lambda *arrays: tuple(body(*arrays)),
        mesh=mesh,
        in_specs=(spec,) * 4,
        out_specs=(spec, spec),
        check_vma=False,
    )
```
